32 devices in a mesh: seq: 16 (over z, y, x), fsdp: 2 (over core).
Axes of the slice: x: 2, y: 2, z: 4, core: 2. Of those that a mesh axis runs over, the one named last changes fastest.
Arguments:
- hidden_in: bfloat16 [2, 8192, 1536], P('fsdp', 'seq'), may hold values from -6 to 6
- norm_gain: float32 [1536], replicated, may hold values from 0.5 to 1.5
- in_weight: bfloat16 [1536, 6448], P('fsdp'), may hold values from -0.15625 to 0.15625
- conv_weight: float32 [4, 3328], replicated, may hold values from -3 to 3
- conv_bias: float32 [3328], replicated, may hold values from -3 to 3
- step_bias: float32 [48], replicated, may hold values from -2 to 0
- decay_log: float32 [48], replicated, as said below
- skip_gain: float32 [48], replicated, may hold values from 0.5 to 2
- gate_gain: float32 [3072], replicated, may hold values from 0.5 to 1.5
- out_weight: bfloat16 [3072, 1536], P('fsdp'), may hold values from -0.109375 to 0.109375
- cotangent: bfloat16 [2, 8192, 1536], P('fsdp', 'seq'), may hold values from -6 to 6
Outputs:
- block_out: bfloat16 [2, 8192, 1536], P('fsdp', 'seq')
- input_grad: bfloat16 [2, 8192, 1536], P('fsdp', 'seq')
- norm_gain_grad: float32 [1536], replicated
- in_weight_grad: float32 [1536, 6448], P('fsdp')
- conv_weight_grad: float32 [4, 3328], replicated
- conv_bias_grad: float32 [3328], replicated
- step_bias_grad: float32 [48], replicated
- decay_log_grad: float32 [48], replicated
- skip_gain_grad: float32 [48], replicated
- gate_gain_grad: float32 [3072], replicated
- out_weight_grad: float32 [3072, 1536], P('fsdp')
The draws below stay inside these ranges and needn't reach their ends.
Inputs may be any that keep to these rules, and one draw needn't show every extreme that they name: `decay_log`: natural logarithm of each head's decay rate per unit of step size.
All inputs are finite; a program needn't handle non-finite values.
Results may differ from the reference program's by a relative error of at most 0.012.
The reference program's roundings to bfloat16 on the way count: a program that leaves them out, or rounds other values in their place, can miss the bound.
Values may be sent and summed in bfloat16 or wider, within the bound.
No kernel may reach another device: no remote copies, remote signals or barrier semaphores. Data moves between devices by JAX's collectives and lax.ppermute only.
A program may use at most 512 MiB of HBM per device.

```python
import jax
import jax.numpy as jnp
from jax import lax

D = 1536
HEADS = 48
HEAD_DIM = 64
STATE = 128
CONV = 4
SPAN = 256
TOK_DEV = 512
INNER = 3072
CONV_CH = 3328
PROJ = 6448
SEQ_LEN = 4096
TOKENS = 8192
GROUPS = 2
N_SEQ = 16


def draw_decay_log(key, part):
    key = jax.random.fold_in(key, 11)
    order_key, fast_key, slow_key = jax.random.split(key, 3)
    fast_count = max(1, HEADS // 3)
    ranks = jax.random.permutation(order_key, HEADS)
    fast_values = jax.random.uniform(fast_key, (HEADS,), jnp.float32, -3.4, -2.4)
    slow_values = jax.random.uniform(slow_key, (HEADS,), jnp.float32, -1.5, 1.2) - jnp.log(jnp.float32(SEQ_LEN))
    return jnp.where(ranks < fast_count, fast_values, slow_values)


def level_of(stream_key, shape, shards, smallest, largest):
    level = 1.0
    for dim, shards_of in shards:
        draws = jax.random.uniform(jax.random.fold_in(jax.random.fold_in(stream_key, 6), dim), (shards_of,), jnp.float32, smallest / len(shards), largest / len(shards))
        level = level * jnp.repeat(jnp.exp(draws), shape[dim] // shards_of).reshape((-1,) + (1,) * (len(shape) - 1 - dim))
    return level


def centred(key, shape, width, reach, shards=(), kind=jnp.bfloat16):
    values = width * jax.random.normal(key, shape, jnp.float32)
    if shards:
        values = values * level_of(key, shape, shards, -0.22, 0.18)
    return jnp.clip(values, -reach, reach).astype(kind)


def setup_inputs(seed: int = 0) -> dict:
    seeds = jax.random.split(jax.random.key(seed), 12)
    return {
        "hidden_in": centred(seeds[0], (GROUPS, TOKENS, D), 1.0, 6.0, ((0, 2), (1, 16))),
        "norm_gain": jnp.clip(1.0 + 0.1 * jax.random.normal(seeds[1], (D,), jnp.float32), 0.5, 1.5),
        "in_weight": centred(seeds[2], (D, PROJ), D ** -0.5, 0.15625, ((0, 2),)),
        "conv_weight": centred(seeds[3], (CONV, CONV_CH), 0.5, 3.0, (), jnp.float32),
        "conv_bias": centred(seeds[4], (CONV_CH,), 0.5, 3.0, (), jnp.float32),
        "step_bias": jnp.clip(jax.random.uniform(seeds[5], (HEADS,), jnp.float32, -2.0, 0.0), -2.0, 0.0),
        "decay_log": draw_decay_log(jax.random.fold_in(seeds[11], 71), 0),
        "skip_gain": jnp.clip(jax.random.uniform(seeds[7], (HEADS,), jnp.float32, 0.5, 2.0), 0.5, 2.0),
        "gate_gain": jnp.clip(1.0 + 0.1 * jax.random.normal(seeds[8], (INNER,), jnp.float32), 0.5, 1.5),
        "out_weight": centred(seeds[9], (INNER, D), INNER ** -0.5, 0.109375, ((0, 2),)),
        "cotangent": centred(seeds[10], (GROUPS, TOKENS, D), 1.0, 6.0, ((0, 2), (1, 16))),
    }


EPSILON = 1e-05
HIGHEST = lax.Precision.HIGHEST

@jax.custom_vjp
def low(v):
    return lax.optimization_barrier(v.astype(jnp.bfloat16)).astype(jnp.float32)

@jax.custom_vjp
def low_back(v):
    return v

def low_keep(v):
    return (low(v), None)

def low_pass(kept, grad):
    return (grad,)

def back_keep(v):
    return (v, None)

def back_low(kept, grad):
    return (low(grad),)
low.defvjp(low_keep, low_pass)
low_back.defvjp(back_keep, back_low)

def span_step(carry_state, pieces):
    values, writes, readout, log_decay, step_size = pieces
    extent = values.shape[0]
    running = jnp.cumsum(log_decay, axis=0)
    scaled = values * step_size[:, :, None]
    scores = jnp.dot(readout, writes.T, precision=HIGHEST)
    causal = (jnp.arange(extent)[:, None] >= jnp.arange(extent)[None, :])[:, :, None]
    spread = running[:, None, :] - running[None, :, :]
    weights = jnp.where(causal, jnp.exp(jnp.where(causal, spread, 0.0)), 0.0) * scores[:, :, None]
    inside = jnp.einsum('tsh,shp->thp', weights, scaled, precision=HIGHEST)
    carried = jnp.exp(running)[:, :, None] * jnp.einsum('tn,hpn->thp', readout, carry_state, precision=HIGHEST)
    remain = jnp.exp(running[-1][None, :] - running)
    added_state = jnp.einsum('sh,shp,sn->hpn', remain, scaled, writes, precision=HIGHEST)
    return (jnp.exp(running[-1])[:, None, None] * carry_state + added_state, inside + carried)

def layer_forward(rows_in, norm_gain, in_weight, conv_weight, conv_bias, step_bias, decay_log, skip_gain, gate_gain, out_weight):
    length = rows_in.shape[0]
    rescale = lax.rsqrt(lax.optimization_barrier(jnp.mean(rows_in * rows_in, axis=1, keepdims=True)) + EPSILON)
    normed = low(rows_in * rescale * norm_gain)
    projected = low_back(jnp.dot(normed, in_weight, precision=HIGHEST))
    gate_part = projected[:, :INNER]
    conv_input = projected[:, INNER:INNER + CONV_CH]
    step_raw = projected[:, INNER + CONV_CH:]
    padded = jnp.concatenate([jnp.zeros((CONV - 1, CONV_CH), jnp.float32), conv_input], axis=0)
    mixture = conv_bias + conv_weight[0] * padded[0:length]
    for offset in range(1, CONV):
        mixture = mixture + conv_weight[offset] * padded[offset:offset + length]
    active = jax.nn.silu(mixture)
    values = active[:, :INNER].reshape(length, HEADS, HEAD_DIM)
    writes = active[:, INNER:INNER + STATE]
    readout = active[:, INNER + STATE:]
    step_size = jax.nn.softplus(step_raw + step_bias)
    log_decay = -jnp.exp(decay_log) * step_size
    blocks = length // SPAN

    def block_view(array):
        return array.reshape((blocks, SPAN) + array.shape[1:])
    initial = jnp.zeros((HEADS, HEAD_DIM, STATE), jnp.float32)
    span_out = lax.scan(jax.checkpoint(span_step), initial, (block_view(values), block_view(writes), block_view(readout), block_view(log_decay), block_view(step_size)))[1]
    scanned = span_out.reshape(length, HEADS, HEAD_DIM) + skip_gain[:, None] * values
    gated_out = scanned.reshape(length, INNER) * jax.nn.silu(gate_part)
    inverse = lax.rsqrt(lax.optimization_barrier(jnp.mean(gated_out * gated_out, axis=1, keepdims=True)) + EPSILON)
    normed_out = low(gated_out * inverse * gate_gain)
    return rows_in + jnp.dot(normed_out, out_weight, precision=HIGHEST)

def to_sequences(array):
    blocked = array.astype(jnp.float32).reshape(GROUPS, N_SEQ, 2, TOK_DEV // 2, D)
    return blocked.transpose(0, 2, 1, 3, 4).reshape(GROUPS * 2, SEQ_LEN, D)

def from_sequences(array):
    blocked = array.reshape(GROUPS, 2, N_SEQ, TOK_DEV // 2, D)
    return blocked.transpose(0, 2, 1, 3, 4).reshape(GROUPS, TOKENS, D)

def reference(hidden_in, norm_gain, in_weight, conv_weight, conv_bias, step_bias, decay_log, skip_gain, gate_gain, out_weight, cotangent):
    sequences = to_sequences(hidden_in)
    upstream = to_sequences(cotangent)
    weights_all = (norm_gain, in_weight.astype(jnp.float32), conv_weight, conv_bias, step_bias, decay_log, skip_gain, gate_gain, out_weight.astype(jnp.float32))
    zero_grads = jax.tree.map(jnp.zeros_like, weights_all)

    def one_sequence(totals, sample):
        rows_in, upstream_rows = sample
        result, pullback = jax.vjp(layer_forward, rows_in, *weights_all)
        gradients = pullback(upstream_rows)
        return (jax.tree.map(jnp.add, totals, tuple(gradients[1:])), (result, gradients[0]))
    totals, (results, in_grads) = lax.scan(one_sequence, zero_grads, (sequences, upstream))
    block_out = from_sequences(results).astype(jnp.bfloat16)
    input_grad = from_sequences(in_grads).astype(jnp.bfloat16)
    return (block_out, input_grad, totals[0], totals[1], totals[2], totals[3], totals[4], totals[5], totals[6], totals[7], totals[8])
```

```python
import functools

import jax
import jax.numpy as jnp
from jax import lax
from jax.experimental import pallas as pl
from jax.experimental.pallas import tpu as pltpu
from jax.sharding import PartitionSpec as P

HEADS = 48
HEAD_DIM = 64
STATE = 128
CONV = 4
INNER = 3072
CONV_CH = 3328
EPSILON = 1e-05

QUARTERS = 4
Q_HEADS = HEADS // QUARTERS
Q_LANES = INNER // QUARTERS
TILE = 128
Q_TILES = Q_LANES // TILE
EDGE = 16
PAYLOAD = STATE + EDGE
ROWS = 64
SUB = 128
FAR = -1e30
VMEM = 60 * 1024 * 1024
HIGHEST = lax.Precision.HIGHEST
F32 = jnp.float32
BF16 = jnp.bfloat16


def params():
    return pltpu.CompilerParams(vmem_limit_bytes=VMEM)


def low_lanes():
    return lax.broadcasted_iota(jnp.int32, (1, TILE), 1) < HEAD_DIM


def pick(per_head, tile):
    return jnp.where(
        low_lanes(),
        per_head[:, 2 * tile : 2 * tile + 1],
        per_head[:, 2 * tile + 1 : 2 * tile + 2],
    )


def head_columns(channels, columns, offset):
    row = lax.broadcasted_iota(jnp.int32, (channels, columns), 0)
    col = lax.broadcasted_iota(jnp.int32, (channels, columns), 1) - offset
    return ((row >= HEAD_DIM * col) & (row < HEAD_DIM * col + HEAD_DIM)).astype(BF16)


def head_sums(wide, selector):
    high = wide.astype(BF16)
    rest = (wide - high.astype(F32)).astype(BF16)
    return jnp.dot(high, selector, preferred_element_type=F32) + jnp.dot(
        rest, selector, preferred_element_type=F32
    )


def dot(left, right):
    return jnp.dot(left, right, preferred_element_type=F32)


def dot_last(left, right, precision=None):
    return lax.dot_general(
        left,
        right,
        (((1,), (1,)), ((), ())),
        preferred_element_type=F32,
        precision=precision,
    )


def dot_first(left, right, precision=None):
    return lax.dot_general(
        left,
        right,
        (((0,), (0,)), ((), ())),
        preferred_element_type=F32,
        precision=precision,
    )


def mixture_of(conv_input, seq, lanes, weight, bias):
    total = bias
    for tap in range(CONV):
        start = EDGE - CONV + 1 + tap
        total = total + weight[tap : tap + 1] * conv_input[seq, start : start + 256, lanes]
    return total


def silu_slope(value):
    gate = jax.nn.sigmoid(value)
    return gate * (1.0 + value * (1.0 - gate))


def step_kernel(
    conv_input,
    weight,
    bias,
    small,
    bc_ref,
    bt_ref,
    scores_ref,
    scores_t_ref,
    step_ref,
    sum_ref,
    step_q_ref,
    sum_q_ref,
    sum_t_ref,
):
    row = lax.broadcasted_iota(jnp.int32, (256, 256), 0)
    col = lax.broadcasted_iota(jnp.int32, (256, 256), 1)
    lower = (row >= col).astype(F32)
    head = lax.broadcasted_iota(jnp.int32, (1, TILE), 1) < HEADS
    for seq in range(2):
        mixture = mixture_of(conv_input, seq, slice(0, 256), weight[...], bias[...])
        active = mixture * jax.nn.sigmoid(mixture)
        bc_ref[seq] = active
        writes, readout = active[:, :STATE], active[:, STATE:]
        bt_ref[seq] = writes.T.astype(BF16)
        scores = dot_last(readout, writes, HIGHEST)
        scores_ref[seq] = scores
        scores_t_ref[seq] = scores.T
        raw = jnp.where(head, conv_input[seq, EDGE : EDGE + 256, 256:384] + small[0:1], 0.0)
        step = jnp.maximum(raw, 0.0) + jnp.log1p(jnp.exp(-jnp.abs(raw)))
        log_decay = -jnp.exp(small[1:2]) * step
        running = jnp.dot(lower, log_decay, preferred_element_type=F32, precision=HIGHEST)
        step_ref[seq] = step
        sum_ref[seq] = running
        for quarter in range(QUARTERS):
            shift = (TILE - Q_HEADS * quarter) % TILE
            step_q = pltpu.roll(step, shift, 1) if shift else step
            sum_q = pltpu.roll(running, shift, 1) if shift else running
            step_q_ref[quarter, seq] = step_q[:, :Q_HEADS]
            sum_q_ref[quarter, seq] = sum_q[:, :Q_HEADS]
            sum_t_ref[quarter, seq] = sum_q.T[:EDGE]


def state_kernel(conv_input, weight, bias, step_q, sum_q, bt_ref, x_ref, payload_ref):
    index = lax.broadcasted_iota(jnp.int32, (EDGE, TILE), 0)
    for seq in range(2):
        running = sum_q[0, seq]
        last = running[255:256]
        scale = step_q[0, seq] * jnp.exp(last - running)
        whole = jnp.exp(last)
        for tile in range(Q_TILES):
            lanes = slice(TILE * tile, TILE * tile + TILE)
            mixture = mixture_of(conv_input, seq, lanes, weight[:, lanes], bias[:, lanes])
            x = mixture * jax.nn.sigmoid(mixture)
            x_ref[seq, :, lanes] = x
            added = dot(bt_ref[seq], (x * pick(scale, tile)).astype(BF16))
            payload_ref[0, seq, :STATE, lanes] = added.astype(BF16)
            decay = pick(whole, tile)
            high = decay.astype(BF16).astype(F32)
            middle = (decay - high).astype(BF16).astype(F32)
            rest = decay - high - middle
            edge = jnp.where(
                index == 0, high, jnp.where(index == 1, middle, jnp.where(index == 2, rest, 0.0))
            )
            payload_ref[0, seq, STATE:, lanes] = edge.astype(BF16)


def intra_kernel(x_ref, step_q, sum_q, sum_t, scores, y_ref):
    row = lax.broadcasted_iota(jnp.int32, (SUB, SUB), 0)
    col = lax.broadcasted_iota(jnp.int32, (SUB, SUB), 1)
    causal = row >= col
    low = low_lanes()
    for seq in range(2):
        step, running = step_q[0, seq], sum_q[0, seq]
        middle = running[SUB - 1 : SUB]
        ahead = jnp.exp(middle - running[:SUB])
        after = jnp.exp(running[SUB:] - middle)
        across = scores[seq, SUB:, :SUB].astype(BF16)
        for tile in range(Q_TILES):
            lanes = slice(TILE * tile, TILE * tile + TILE)
            scaled = x_ref[seq, :, lanes] * pick(step, tile)
            low_part = jnp.where(low, scaled, 0.0).astype(BF16)
            high_part = jnp.where(low, 0.0, scaled).astype(BF16)
            for part in range(2):
                rows = slice(SUB * part, SUB * part + SUB)
                weights = []
                for h in (2 * tile, 2 * tile + 1):
                    spread = running[rows, h : h + 1] - sum_t[0, seq, h : h + 1, rows]
                    decayed = jnp.exp(jnp.where(causal, spread, FAR))
                    weights.append((decayed * scores[seq, rows, rows]).astype(BF16))
                inside = dot(
                    jnp.concatenate(weights, 1),
                    jnp.concatenate([low_part[rows], high_part[rows]], 0),
                )
                if part:
                    earlier = (scaled[:SUB] * pick(ahead, tile)).astype(BF16)
                    inside = inside + pick(after, tile) * dot(across, earlier)
                y_ref[seq, rows, lanes] = inside


def gate_kernel(
    y_ref,
    x_ref,
    z_ref,
    grad_ref,
    bc_ref,
    sum_ref,
    entering,
    skip,
    gain,
    out_ref,
    grad_z_ref,
    grad_scan_ref,
    grad_state_ref,
    grad_read_ref,
    products_ref,
    gain_grad_ref,
    whole_y,
    whole_gated,
    spread,
    product,
):
    step = pl.program_id(0)
    steps = pl.num_programs(0)
    start = jnp.exp(sum_ref[0])
    readout = bc_ref[0, :, STATE:].astype(BF16)
    squares = jnp.zeros((ROWS, TILE), F32)
    overlap = jnp.zeros((ROWS, TILE), F32)
    for tile in range(INNER // TILE):
        lanes = slice(TILE * tile, TILE * tile + TILE)
        carried = dot(readout, entering[0, :, lanes])
        y = y_ref[0, :, lanes] + pick(start, tile) * carried
        whole_y[:, lanes] = y
        z = z_ref[0, :, lanes]
        gated = (y + skip[:, lanes] * x_ref[0, :, lanes]) * (z * jax.nn.sigmoid(z))
        whole_gated[:, lanes] = gated
        squares = squares + gated * gated
        overlap = overlap + gated * (grad_ref[0, :, lanes] * gain[:, lanes])
    mean = jnp.sum(squares, axis=1, keepdims=True) / INNER
    inverse = lax.rsqrt(mean + EPSILON)
    back = jnp.sum(overlap, axis=1, keepdims=True) / INNER * inverse * inverse * inverse

    @pl.when(step == 0)
    def _():
        gain_grad_ref[...] = jnp.zeros_like(gain_grad_ref)

    for tile in range(INNER // TILE):
        lanes = slice(TILE * tile, TILE * tile + TILE)
        gated = whole_gated[:, lanes]
        grad = grad_ref[0, :, lanes]
        scaled = gated * inverse
        out_ref[0, :, lanes] = (scaled * gain[:, lanes]).astype(BF16)
        gain_grad_ref[:, lanes] += jnp.sum(grad * scaled, axis=0, keepdims=True)
        grad_gated = inverse * (grad * gain[:, lanes]) - gated * back
        z = z_ref[0, :, lanes]
        gate = jax.nn.sigmoid(z)
        y = whole_y[:, lanes]
        scanned = y + skip[:, lanes] * x_ref[0, :, lanes]
        grad_scan = grad_gated * (z * gate)
        grad_z_ref[0, :, lanes] = (
            grad_gated * scanned * (gate * (1.0 + z * (1.0 - gate)))
        ).astype(BF16)
        grad_scan_ref[0, :, lanes] = grad_scan
        rounded = grad_scan.astype(BF16).astype(F32)
        product[:, lanes] = rounded * y
        spread[:, lanes] = (rounded * pick(start, tile)).astype(BF16)
    products_ref[0] = head_sums(product[...], head_columns(INNER, TILE, 0))
    grad_read_ref[0] = dot_last(spread[...], entering[0])

    @pl.when(step % (steps // 2) == 0)
    def _():
        grad_state_ref[...] = jnp.zeros_like(grad_state_ref)

    grad_state_ref[0] += dot_first(readout, spread[...])


def intra_back_kernel(x_ref, grad_ref, step_q, sum_q, sum_t, scores_t, grad_x_ref, grad_scores_ref):
    row = lax.broadcasted_iota(jnp.int32, (SUB, SUB), 0)
    col = lax.broadcasted_iota(jnp.int32, (SUB, SUB), 1)
    causal = row <= col
    low = low_lanes()

    @pl.when(pl.program_id(0) == 0)
    def _():
        grad_scores_ref[...] = jnp.zeros_like(grad_scores_ref)

    for seq in range(2):
        step, running = step_q[0, seq], sum_q[0, seq]
        middle = running[SUB - 1 : SUB]
        ahead = jnp.exp(middle - running[:SUB])
        after = jnp.exp(running[SUB:] - middle)
        across = scores_t[seq, :SUB, SUB:].astype(BF16)
        inner = [jnp.zeros((SUB, SUB), F32) for _ in range(2)]
        outer = jnp.zeros((SUB, SUB), F32)
        for tile in range(Q_TILES):
            lanes = slice(TILE * tile, TILE * tile + TILE)
            scaled = x_ref[seq, :, lanes] * pick(step, tile)
            grad = grad_ref[seq, :, lanes]
            low_grad = jnp.where(low, grad, 0.0).astype(BF16)
            high_grad = jnp.where(low, 0.0, grad).astype(BF16)
            rounded = grad.astype(BF16)
            sides = (
                jnp.where(low, scaled, 0.0).astype(BF16),
                jnp.where(low, 0.0, scaled).astype(BF16),
            )
            for part in range(2):
                rows = slice(SUB * part, SUB * part + SUB)
                weights = []
                for side in range(2):
                    h = 2 * tile + side
                    spread = sum_t[0, seq, h : h + 1, rows] - running[rows, h : h + 1]
                    decayed = jnp.exp(jnp.where(causal, spread, FAR))
                    weights.append((decayed * scores_t[seq, rows, rows]).astype(BF16))
                    inner[part] = inner[part] + decayed * dot_last(
                        sides[side][rows], rounded[rows]
                    )
                inside = dot(
                    jnp.concatenate(weights, 1),
                    jnp.concatenate([low_grad[rows], high_grad[rows]], 0),
                )
                if not part:
                    later = (rounded[SUB:].astype(F32) * pick(after, tile)).astype(BF16)
                    factor = pick(ahead, tile)
                    inside = inside + factor * dot(across, later)
                    outer = outer + dot_last((scaled[:SUB] * factor).astype(BF16), later)
                grad_x_ref[seq, rows, lanes] = inside
        grad_scores_ref[seq, :SUB, :SUB] += inner[0]
        grad_scores_ref[seq, SUB:, SUB:] += inner[1]
        grad_scores_ref[seq, :SUB, SUB:] += outer


def channel_kernel(
    conv_input,
    weight,
    bias,
    x_ref,
    grad_ref,
    grad_x_ref,
    step_q,
    sum_q,
    bc_ref,
    leaving,
    entering,
    skip,
    grad_conv_ref,
    tail_ref,
    halo_ref,
    sums_ref,
    heads_ref,
    grad_writes_ref,
    padded,
    product,
    spread,
):
    quarter = pl.program_id(0)
    zeros = jnp.zeros((EDGE, TILE), F32)
    padded[:EDGE] = zeros
    padded[EDGE + 256 :] = zeros
    sums_ref[...] = jnp.zeros_like(sums_ref)

    @pl.when(quarter == 0)
    def _():
        grad_writes_ref[...] = jnp.zeros_like(grad_writes_ref)

    for seq in range(2):
        step, running = step_q[0, seq], sum_q[0, seq]
        remain = jnp.exp(running[255:256] - running)
        writes = bc_ref[seq, :, :STATE].astype(BF16)
        for tile in range(Q_TILES):
            lanes = slice(TILE * tile, TILE * tile + TILE)
            taps = weight[:, lanes]
            x = x_ref[seq, :, lanes]
            grad = grad_ref[seq, :, lanes]
            size = pick(step, tile)
            scaled = x * size
            left = pick(remain, tile)
            from_state = left * dot(writes, leaving[seq, :, lanes])
            inside = grad_x_ref[seq, :, lanes]
            whole = inside + from_state
            at_state = scaled * from_state
            product[0, :, lanes] = scaled.astype(BF16).astype(F32) * inside + at_state
            product[1, :, lanes] = x * whole
            product[2, :, lanes] = at_state
            spread[:, lanes] = (scaled * left).astype(BF16)
            mixture = mixture_of(conv_input, seq, lanes, taps, bias[:, lanes])
            grad_mix = (size * whole + skip[:, lanes] * grad) * silu_slope(mixture)
            padded[EDGE : EDGE + 256] = grad_mix
            grad_conv = taps[0:1] * padded[3 : 3 + EDGE + 256]
            for tap in range(1, CONV):
                grad_conv = (
                    grad_conv + taps[tap : tap + 1] * padded[3 - tap : 3 - tap + EDGE + 256]
                )
            halo_ref[seq, :, lanes] = grad_conv[:EDGE].astype(BF16)
            grad_conv_ref[seq, :, lanes] = grad_conv[EDGE:].astype(BF16)
            tail_ref[seq, :, lanes] = grad_conv[256:]
            for tap in range(CONV):
                begin = EDGE - CONV + 1 + tap
                sums_ref[tap : tap + 1, lanes] += jnp.sum(
                    grad_mix * conv_input[seq, begin : begin + 256, lanes], axis=0, keepdims=True
                )
            sums_ref[4:5, lanes] += jnp.sum(grad_mix, axis=0, keepdims=True)
            sums_ref[5:6, lanes] += jnp.sum(grad * x, axis=0, keepdims=True)
            meeting = entering[seq, :, lanes].astype(F32) * leaving[seq, :, lanes].astype(F32)
            sums_ref[6 + seq : 7 + seq, lanes] = jnp.sum(meeting, axis=0, keepdims=True)
        total = jnp.zeros((256, TILE), F32)
        for kind in range(3):
            total = total + head_sums(product[kind], head_columns(Q_LANES, TILE, Q_HEADS * kind))
        heads_ref[0, seq] = total
        grad_writes_ref[seq] += dot_last(spread[...], leaving[seq])


def last_kernel(
    conv_input,
    weight,
    bias,
    small,
    bc_ref,
    grad_scores,
    grad_writes,
    grad_read,
    products,
    heads,
    sums,
    step_ref,
    sum_ref,
    grad_conv_ref,
    tail_ref,
    halo_ref,
    sums_ref,
    small_ref,
    padded,
):
    row = lax.broadcasted_iota(jnp.int32, (256, 256), 0)
    col = lax.broadcasted_iota(jnp.int32, (256, 256), 1)
    upper = (row <= col).astype(F32)
    lane = lax.broadcasted_iota(jnp.int32, (1, TILE), 1)
    line = lax.broadcasted_iota(jnp.int32, (256, 1), 0)
    padded[:EDGE] = jnp.zeros((EDGE, 256), F32)
    padded[EDGE + 256 :] = jnp.zeros((EDGE, 256), F32)
    sums_ref[...] = jnp.zeros_like(sums_ref)
    small_ref[...] = jnp.zeros_like(small_ref)
    rate = jnp.exp(small[1:2])
    per_head = head_sums(sums[...], head_columns(INNER, TILE, 0))
    small_ref[2:3] = per_head[5:6]
    taps = weight[...]
    for seq in range(2):
        kinds = []
        for kind in range(3):
            total = jnp.zeros((256, TILE), F32)
            for quarter in range(QUARTERS):
                value = heads[quarter, seq]
                shift = (Q_HEADS * (quarter - kind)) % TILE
                if shift:
                    value = pltpu.roll(value, shift, 1)
                first = Q_HEADS * quarter
                total = total + jnp.where((lane >= first) & (lane < first + Q_HEADS), value, 0.0)
            kinds.append(total)
        met, by_value, at_state = kinds
        running = sum_ref[seq]
        end = jnp.exp(running[255:256]) * per_head[6 + seq : 7 + seq] + jnp.sum(
            at_state, axis=0, keepdims=True
        )
        grad_sum = products[seq] - met + jnp.where(line == 255, end, 0.0)
        grad_log = jnp.dot(upper, grad_sum, preferred_element_type=F32, precision=HIGHEST)
        step = step_ref[seq]
        small_ref[1:2] += jnp.sum(-rate * step * grad_log, axis=0, keepdims=True)
        raw = jnp.where(
            lane < HEADS, conv_input[seq, EDGE : EDGE + 256, 256:384] + small[0:1], 0.0
        )
        grad_raw = (by_value - rate * grad_log) * jax.nn.sigmoid(raw)
        small_ref[0:1] += jnp.sum(grad_raw, axis=0, keepdims=True)
        grad_conv_ref[seq, :, 256:] = grad_raw[:, :HEADS].astype(BF16)
        writes, readout = bc_ref[seq, :, :STATE], bc_ref[seq, :, STATE:]
        into_writes = dot(grad_scores[seq].astype(BF16), readout.astype(BF16)) + grad_writes[seq]
        into_read = dot_first(grad_scores[seq].astype(BF16), writes.astype(BF16)) + grad_read[seq]
        mixture = mixture_of(conv_input, seq, slice(0, 256), taps, bias[...])
        grad_mix = jnp.concatenate([into_writes, into_read], 1) * silu_slope(mixture)
        padded[EDGE : EDGE + 256] = grad_mix
        grad_conv = taps[0:1] * padded[3 : 3 + EDGE + 256]
        for tap in range(1, CONV):
            grad_conv = grad_conv + taps[tap : tap + 1] * padded[3 - tap : 3 - tap + EDGE + 256]
        halo_ref[seq] = grad_conv[:EDGE].astype(BF16)
        grad_conv_ref[seq, :, :256] = grad_conv[EDGE:].astype(BF16)
        tail_ref[seq] = grad_conv[256:]
        for tap in range(CONV):
            begin = EDGE - CONV + 1 + tap
            sums_ref[tap : tap + 1] += jnp.sum(
                grad_mix * conv_input[seq, begin : begin + 256, :256], axis=0, keepdims=True
            )
        sums_ref[4:5] += jnp.sum(grad_mix, axis=0, keepdims=True)


def shape(dims, dtype=F32):
    return jax.ShapeDtypeStruct(dims, dtype)


def whole_block(dims):
    return pl.BlockSpec(dims, lambda g: (0,) * len(dims))


def lane_block(dims, width=Q_LANES):
    return pl.BlockSpec(dims + (width,), lambda g: (0,) * len(dims) + (g,))


def quarter_block(dims):
    return pl.BlockSpec((1,) + dims, lambda g: (g,) + (0,) * len(dims))


def fixed_block(dims, index):
    return pl.BlockSpec(dims, lambda g: index)


def row_block(width, length=256):
    steps = length // ROWS
    return pl.BlockSpec((1, ROWS, width), lambda g: (g // steps, g % steps, 0))


def decay_row(edge):
    rows = edge.astype(F32)
    return (rows[..., 0:1, :] + rows[..., 1:2, :]) + rows[..., 2:3, :]


def join(state, decay):
    high = decay.astype(BF16).astype(F32)
    middle = (decay - high).astype(BF16).astype(F32)
    rest = decay - high - middle
    blank = jnp.zeros(decay.shape[:-2] + (EDGE - 3,) + decay.shape[-1:], BF16)
    parts = [state, high, middle, rest]
    return jnp.concatenate([p.astype(BF16) for p in parts] + [blank], axis=-2)


def split(payload):
    return payload[..., :STATE, :].astype(F32), decay_row(payload[..., STATE:, :])


def exchange(payload, axis, reverse):
    count = lax.axis_size(axis)
    place = lax.axis_index(axis)
    member = place % QUARTERS

    def swap(value, by):
        return lax.ppermute(value, axis, [(i, i ^ by) for i in range(count)])

    def quarter_of(array, by):
        return lax.dynamic_index_in_dim(array, member ^ by, 0, False)

    relative = [quarter_of(payload, 0)] + [
        swap(quarter_of(payload, by), by) for by in range(1, QUARTERS)
    ]

    def select(items, which):
        result = items[QUARTERS - 1]
        for by in range(QUARTERS - 1):
            result = jnp.where((member ^ by) == which, items[by], result)
        return result

    order = range(QUARTERS)[::-1] if reverse else range(QUARTERS)
    state = jnp.zeros((2, STATE, Q_LANES), F32)
    decay = jnp.ones((2, 1, Q_LANES), F32)
    before = {}
    for which in order:
        before[which] = (state, decay)
        here, factor = split(select(relative, which))
        state, decay = here + factor * state, factor * decay
    total = join(state, decay)
    span = 1
    inclusive = total
    entering = None
    while span < count // QUARTERS:
        shift = -QUARTERS * span if reverse else QUARTERS * span
        pairs = [(i, i + shift) for i in range(count) if 0 <= i + shift < count]
        received = lax.ppermute(inclusive, axis, pairs)
        got, factor = split(received)
        if entering is None:
            entering = (got, factor)
        else:
            entering = (entering[0] + entering[1] * got, entering[1] * factor)
        inclusive = join(state + decay * entering[0], decay * entering[1])
        span *= 2
    carried = entering[0]
    sends = [
        (before[which][0] + before[which][1] * carried).astype(BF16) for which in range(QUARTERS)
    ]

    def sent_to(by):
        result = sends[QUARTERS - 1]
        for which in range(QUARTERS - 1):
            result = jnp.where((member ^ by) == which, sends[which], result)
        return result

    back = [sent_to(0)] + [swap(sent_to(by), by) for by in range(1, QUARTERS)]
    return jnp.concatenate([select(back, which) for which in range(QUARTERS)], axis=-1)


def local(
    hidden_in,
    norm_gain,
    in_weight,
    conv_weight,
    conv_bias,
    step_bias,
    decay_log,
    skip_gain,
    gate_gain,
    out_weight,
    cotangent,
):
    hidden = hidden_in[0]
    upstream = cotangent[0]
    tokens, width = hidden.shape
    half = tokens // 2
    share = in_weight.shape[0]
    count = lax.axis_size("seq")
    core = lax.axis_index("fsdp")
    other = [(0, 1), (1, 0)]

    conv_rows = in_weight[:, INNER:]
    gate_rows = in_weight[:, :INNER]
    conv_rows_other = lax.ppermute(conv_rows, "fsdp", other)
    gate_rows_other = lax.ppermute(gate_rows, "fsdp", other)
    out_rows_other = lax.ppermute(out_weight, "fsdp", other)

    paired = hidden.reshape(2, half, width)
    halo = lax.ppermute(paired[:, half - EDGE :], "seq", [(i, i + 1) for i in range(count - 1)])
    extended = jnp.concatenate([halo, paired], axis=1).reshape(2 * (half + EDGE), width)
    rows = extended.astype(F32)
    rescale = lax.rsqrt(jnp.mean(rows * rows, axis=-1, keepdims=True) + EPSILON)
    normed_ext = (rows * rescale * norm_gain).astype(BF16)

    def mine(array, axis):
        first = lax.slice_in_dim(array, 0, share, axis=axis)
        second = lax.slice_in_dim(array, share, 2 * share, axis=axis)
        return (
            jnp.where(core == 0, first, second),
            jnp.where(core == 0, second, first),
        )

    def ordered(own, foreign, axis):
        return jnp.where(
            core == 0,
            jnp.concatenate([own, foreign], axis),
            jnp.concatenate([foreign, own], axis),
        )

    own_ext, other_ext = mine(normed_ext, 1)
    conv_input = (dot(own_ext, conv_rows) + dot(other_ext, conv_rows_other)).reshape(
        2, half + EDGE, CONV_CH + HEADS
    )
    normed = normed_ext.reshape(2, half + EDGE, width)[:, EDGE:].reshape(tokens, width)
    own_normed, other_normed = mine(normed, 1)

    small = jnp.pad(jnp.stack([step_bias, decay_log, skip_gain]), ((0, 5), (0, TILE - HEADS)))
    bias_row = conv_bias[None]
    gain_row = gate_gain[None]
    skip_row = jnp.repeat(skip_gain, HEAD_DIM)[None]

    last_columns = fixed_block((2, half + EDGE, 384), (0, 0, INNER // 384))
    last_taps = fixed_block((CONV, 256), (0, INNER // 256))
    last_bias = fixed_block((1, 256), (0, INNER // 256))
    per_quarter = (QUARTERS, 2, half, Q_HEADS)
    bc, bt, scores, scores_t, step, running, step_q, sum_q, sum_t = pl.pallas_call(
        step_kernel,
        grid=(1,),
        in_specs=[last_columns, last_taps, last_bias, whole_block((8, TILE))],
        out_specs=[
            whole_block((2, half, 256)),
            whole_block((2, STATE, half)),
            whole_block((2, half, half)),
            whole_block((2, half, half)),
            whole_block((2, half, TILE)),
            whole_block((2, half, TILE)),
            whole_block(per_quarter),
            whole_block(per_quarter),
            whole_block((QUARTERS, 2, EDGE, half)),
        ],
        out_shape=[
            shape((2, half, 256)),
            shape((2, STATE, half), BF16),
            shape((2, half, half)),
            shape((2, half, half)),
            shape((2, half, TILE)),
            shape((2, half, TILE)),
            shape(per_quarter),
            shape(per_quarter),
            shape((QUARTERS, 2, EDGE, half)),
        ],
        compiler_params=params(),
        name="steps",
    )(conv_input, conv_weight, bias_row, small)

    columns = lane_block((2, half + EDGE))
    taps_block = lane_block((CONV,))
    row_of = lane_block((1,))
    heads_block = quarter_block((2, half, Q_HEADS))
    line_block = quarter_block((2, EDGE, half))
    tokens_block = lane_block((2, half))
    x, payload = pl.pallas_call(
        state_kernel,
        grid=(QUARTERS,),
        in_specs=[
            columns,
            taps_block,
            row_of,
            heads_block,
            heads_block,
            whole_block((2, STATE, half)),
        ],
        out_specs=[tokens_block, quarter_block((2, PAYLOAD, Q_LANES))],
        out_shape=[shape((2, half, INNER)), shape((QUARTERS, 2, PAYLOAD, Q_LANES), BF16)],
        compiler_params=params(),
        name="states",
    )(conv_input, conv_weight, bias_row, step_q, sum_q, bt)

    entering = exchange(payload, "seq", False)

    y_inside = pl.pallas_call(
        intra_kernel,
        grid=(QUARTERS,),
        in_specs=[
            tokens_block,
            heads_block,
            heads_block,
            line_block,
            whole_block((2, half, half)),
        ],
        out_specs=tokens_block,
        out_shape=shape((2, half, INNER)),
        compiler_params=params(),
        name="inside",
    )(x, step_q, sum_q, sum_t, scores)
    z = (dot(own_normed, gate_rows) + dot(other_normed, gate_rows_other)).reshape(2, half, INNER)
    grad_normed_out = ordered(
        dot_last(upstream, out_weight), dot_last(upstream, out_rows_other), 1
    ).reshape(2, half, INNER)

    token_rows = row_block(INNER)
    steps = half // ROWS
    state_rows = pl.BlockSpec((1, STATE, INNER), lambda g: (g // steps, 0, 0))
    normed_out, grad_z, grad_scan, grad_state, grad_read, products, gate_gain_grad = pl.pallas_call(
        gate_kernel,
        grid=(2 * steps,),
        in_specs=[
            token_rows,
            token_rows,
            token_rows,
            token_rows,
            row_block(256),
            row_block(TILE),
            state_rows,
            whole_block((1, INNER)),
            whole_block((1, INNER)),
        ],
        out_specs=[
            token_rows,
            token_rows,
            token_rows,
            state_rows,
            row_block(STATE),
            row_block(TILE),
            whole_block((1, INNER)),
        ],
        out_shape=[
            shape((2, half, INNER), BF16),
            shape((2, half, INNER), BF16),
            shape((2, half, INNER)),
            shape((2, STATE, INNER)),
            shape((2, half, STATE)),
            shape((2, half, TILE)),
            shape((1, INNER)),
        ],
        scratch_shapes=[
            pltpu.VMEM((ROWS, INNER), F32),
            pltpu.VMEM((ROWS, INNER), F32),
            pltpu.VMEM((ROWS, INNER), BF16),
            pltpu.VMEM((ROWS, INNER), F32),
        ],
        compiler_params=params(),
        name="gates",
    )(y_inside, x, z, grad_normed_out, bc, running, entering, skip_row, gain_row)

    normed_out = normed_out.reshape(tokens, INNER)
    grad_z = grad_z.reshape(tokens, INNER)

    own_out, other_out = None, None
    first_out, second_out = normed_out[:, : INNER // 2], normed_out[:, INNER // 2 :]
    own_out = jnp.where(core == 0, first_out, second_out)
    other_out = jnp.where(core == 0, second_out, first_out)

    def weight_part(own, foreign, right):
        sent = lax.ppermute(dot_first(foreign, right).astype(BF16), "fsdp", other)
        return dot_first(own, right) + sent.astype(F32)

    out_grad = lax.psum(weight_part(own_out, other_out, upstream).astype(BF16), "seq")
    gate_grad = lax.psum(weight_part(own_normed, other_normed, grad_z).astype(BF16), "seq")

    edge = payload[:, :, STATE:].transpose(1, 2, 0, 3)
    back_payload = jnp.concatenate(
        [
            grad_state.astype(BF16).reshape(2, STATE, QUARTERS, Q_LANES),
            edge,
        ],
        axis=1,
    ).transpose(2, 0, 1, 3)
    leaving = exchange(back_payload, "seq", True)

    branch = dot(own_out, out_weight) + dot(other_out, out_rows_other)
    block_out = (hidden.astype(F32) + branch).astype(BF16)

    grad_x, grad_scores = pl.pallas_call(
        intra_back_kernel,
        grid=(QUARTERS,),
        in_specs=[
            tokens_block,
            tokens_block,
            heads_block,
            heads_block,
            line_block,
            whole_block((2, half, half)),
        ],
        out_specs=[tokens_block, whole_block((2, half, half))],
        out_shape=[shape((2, half, INNER)), shape((2, half, half))],
        compiler_params=params(),
        name="inside_back",
    )(x, grad_scan, step_q, sum_q, sum_t, scores_t)

    state_columns = lane_block((2, STATE))
    edge_columns = lane_block((2, EDGE))
    grad_conv, tail, halo_grad, sums, heads, grad_writes = pl.pallas_call(
        channel_kernel,
        grid=(QUARTERS,),
        in_specs=[
            columns,
            taps_block,
            row_of,
            tokens_block,
            tokens_block,
            tokens_block,
            heads_block,
            heads_block,
            whole_block((2, half, 256)),
            state_columns,
            state_columns,
            row_of,
        ],
        out_specs=[
            tokens_block,
            edge_columns,
            edge_columns,
            lane_block((8,)),
            quarter_block((2, half, TILE)),
            whole_block((2, half, STATE)),
        ],
        out_shape=[
            shape((2, half, INNER), BF16),
            shape((2, EDGE, INNER)),
            shape((2, EDGE, INNER), BF16),
            shape((8, INNER)),
            shape((QUARTERS, 2, half, TILE)),
            shape((2, half, STATE)),
        ],
        scratch_shapes=[
            pltpu.VMEM((half + 2 * EDGE, TILE), F32),
            pltpu.VMEM((3, half, Q_LANES), F32),
            pltpu.VMEM((half, Q_LANES), BF16),
        ],
        compiler_params=params(),
        name="channels",
    )(
        conv_input,
        conv_weight,
        bias_row,
        x,
        grad_scan,
        grad_x,
        step_q,
        sum_q,
        bc,
        leaving,
        entering,
        skip_row,
    )

    grad_conv_last, tail_last, halo_last, sums_last, small_grads = pl.pallas_call(
        last_kernel,
        grid=(1,),
        in_specs=[
            last_columns,
            last_taps,
            last_bias,
            whole_block((8, TILE)),
            whole_block((2, half, 256)),
            whole_block((2, half, half)),
            whole_block((2, half, STATE)),
            whole_block((2, half, STATE)),
            whole_block((2, half, TILE)),
            whole_block((QUARTERS, 2, half, TILE)),
            whole_block((8, INNER)),
            whole_block((2, half, TILE)),
            whole_block((2, half, TILE)),
        ],
        out_specs=[
            whole_block((2, half, 256 + HEADS)),
            whole_block((2, EDGE, 256)),
            whole_block((2, EDGE, 256)),
            whole_block((8, 256)),
            whole_block((8, TILE)),
        ],
        out_shape=[
            shape((2, half, 256 + HEADS), BF16),
            shape((2, EDGE, 256)),
            shape((2, EDGE, 256), BF16),
            shape((8, 256)),
            shape((8, TILE)),
        ],
        scratch_shapes=[pltpu.VMEM((half + 2 * EDGE, 256), F32)],
        compiler_params=params(),
        name="last",
    )(
        conv_input,
        conv_weight,
        bias_row,
        small,
        bc,
        grad_scores,
        grad_writes,
        grad_read,
        products,
        heads,
        sums,
        step,
        running,
    )

    returned = lax.ppermute(
        jnp.concatenate([halo_grad, halo_last], axis=-1),
        "seq",
        [(i, i - 1) for i in range(1, count)],
    )
    fixed_tail = jnp.concatenate([tail, tail_last], axis=-1) + returned.astype(F32)
    grad_proj = jnp.concatenate([grad_conv, grad_conv_last], axis=-1)
    fixed_tail = jnp.concatenate(
        [fixed_tail.astype(BF16), grad_conv_last[:, half - EDGE :, 256:]], axis=-1
    )
    grad_proj = jnp.concatenate([grad_proj[:, : half - EDGE], fixed_tail], axis=1).reshape(
        tokens, CONV_CH + HEADS
    )

    conv_grad = lax.psum(weight_part(own_normed, other_normed, grad_proj).astype(BF16), "seq")

    grad_normed = ordered(
        dot_last(grad_z, gate_rows) + dot_last(grad_proj, conv_rows),
        dot_last(grad_z, gate_rows_other) + dot_last(grad_proj, conv_rows_other),
        1,
    )
    u = hidden.astype(F32)
    r = lax.rsqrt(jnp.mean(u * u, axis=-1, keepdims=True) + EPSILON)
    norm_gain_grad = jnp.sum(grad_normed * u * r, axis=0)
    through = grad_normed * norm_gain
    input_grad = (
        upstream.astype(F32)
        + r * through
        - u * (r * r * r) * jnp.mean(through * u, axis=-1, keepdims=True)
    ).astype(BF16)

    vector = jnp.concatenate(
        [
            norm_gain_grad,
            sums[:5].reshape(-1),
            sums_last[:5].reshape(-1),
            small_grads[:3].reshape(-1),
            gate_gain_grad[0],
        ]
    )
    vector = lax.psum(vector, ("seq", "fsdp"))
    parts = []
    begin = 0
    for size in (width, 5 * INNER, 5 * 256, 3 * TILE, INNER):
        parts.append(vector[begin : begin + size])
        begin += size
    wide, narrow = parts[1].reshape(5, INNER), parts[2].reshape(5, 256)
    conv_sums = jnp.concatenate([wide, narrow], axis=1)
    smalls = parts[3].reshape(3, TILE)[:, :HEADS]
    in_weight_grad = jnp.concatenate([gate_grad, conv_grad], axis=1).astype(F32)
    return (
        block_out[None],
        input_grad[None],
        parts[0],
        in_weight_grad,
        conv_sums[:4],
        conv_sums[4],
        smalls[0],
        smalls[1],
        smalls[2],
        parts[4],
        out_grad.astype(F32),
    )


def solution(mesh):
    return jax.shard_map(
        local,
        mesh=mesh,
        in_specs=(
            P("fsdp", "seq", None),
            P(),
            P("fsdp", None),
            P(),
            P(),
            P(),
            P(),
            P(),
            P(),
            P("fsdp", None),
            P("fsdp", "seq", None),
        ),
        out_specs=(
            P("fsdp", "seq", None),
            P("fsdp", "seq", None),
            P(),
            P("fsdp", None),
            P(),
            P(),
            P(),
            P(),
            P(),
            P(),
            P("fsdp", None),
        ),
        check_vma=False,
    )
```

```python
import functools

import jax
import jax.numpy as jnp
from jax import lax
from jax.experimental import pallas as pl
from jax.experimental.pallas import tpu as pltpu
from jax.sharding import PartitionSpec as P

HEADS = 48
HEAD_DIM = 64
STATE = 128
CONV = 4
INNER = 3072
CONV_CH = 3328
EPSILON = 1e-05

QUARTERS = 4
Q_HEADS = HEADS // QUARTERS
Q_LANES = INNER // QUARTERS
TILE = 128
Q_TILES = Q_LANES // TILE
EDGE = 16
PAYLOAD = STATE + EDGE
ROWS = 128
SIDE = 16
SUB = 128
FAR = -1e30
VMEM = 60 * 1024 * 1024
HIGHEST = lax.Precision.HIGHEST
F32 = jnp.float32
BF16 = jnp.bfloat16


def params():
    return pltpu.CompilerParams(vmem_limit_bytes=VMEM)


def cost(microseconds):
    return pl.CostEstimate(
        flops=0, transcendentals=0, bytes_accessed=int(microseconds * 3_400_000)
    )


def low_lanes():
    return lax.broadcasted_iota(jnp.int32, (1, TILE), 1) < HEAD_DIM


def pick(per_head, tile):
    return jnp.where(
        low_lanes(),
        per_head[:, 2 * tile : 2 * tile + 1],
        per_head[:, 2 * tile + 1 : 2 * tile + 2],
    )


def head_columns(channels, columns, offset):
    row = lax.broadcasted_iota(jnp.int32, (channels, columns), 0)
    col = lax.broadcasted_iota(jnp.int32, (channels, columns), 1) - offset
    return ((row >= HEAD_DIM * col) & (row < HEAD_DIM * col + HEAD_DIM)).astype(BF16)


def head_sums(wide, selector):
    high = wide.astype(BF16)
    rest = (wide - high.astype(F32)).astype(BF16)
    return jnp.dot(high, selector, preferred_element_type=F32) + jnp.dot(
        rest, selector, preferred_element_type=F32
    )


def dot(left, right):
    return jnp.dot(left, right, preferred_element_type=F32)


def dot_last(left, right, precision=None):
    return lax.dot_general(
        left,
        right,
        (((1,), (1,)), ((), ())),
        preferred_element_type=F32,
        precision=precision,
    )


def dot_first(left, right, precision=None):
    return lax.dot_general(
        left,
        right,
        (((0,), (0,)), ((), ())),
        preferred_element_type=F32,
        precision=precision,
    )


def mixture_of(conv_input, seq, lanes, weight, bias):
    total = bias
    for tap in range(CONV):
        start = EDGE - CONV + 1 + tap
        total = total + weight[tap : tap + 1] * conv_input[seq, start : start + 256, lanes]
    return total


def silu_slope(value):
    gate = jax.nn.sigmoid(value)
    return gate * (1.0 + value * (1.0 - gate))


def three_parts(value):
    high = value.astype(BF16).astype(F32)
    middle = (value - high).astype(BF16).astype(F32)
    return high, middle, value - high - middle


def edge_rows(decay, along):
    index = lax.broadcasted_iota(jnp.int32, (EDGE, TILE), 0)
    rows = jnp.zeros((EDGE, TILE), F32)
    for row, part in enumerate(three_parts(decay) + three_parts(along)):
        rows = jnp.where(index == row, part, rows)
    return rows.astype(BF16)


def read_payload(ref, seq, lanes):
    state = ref[seq, :STATE, lanes].astype(F32)
    rows = ref[seq, STATE:, lanes].astype(F32)
    decay = rows[0:1] + rows[1:2] + rows[2:3]
    along = rows[3:4] + rows[4:5] + rows[5:6]
    return state, decay, along


def write_payload(ref, seq, lanes, state, decay, along):
    ref[seq, :STATE, lanes] = state.astype(BF16)
    ref[seq, STATE:, lanes] = edge_rows(decay, along)


def after(first, second):
    return (
        second[0] + second[1] * first[0],
        second[1] * first[1],
        second[2] + second[1] * first[2],
    )


def empty():
    return (
        jnp.zeros((STATE, TILE), F32),
        jnp.ones((1, TILE), F32),
        jnp.zeros((1, TILE), F32),
    )


def parts_of_quarter():
    for seq in range(2):
        for tile in range(Q_TILES):
            yield seq, slice(TILE * tile, TILE * tile + TILE)


def joined(refs, seq, lanes):
    result = read_payload(refs[0], seq, lanes)
    for ref in refs[1:]:
        result = after(read_payload(ref, seq, lanes), result)
    return result


def plane_kernel(reverse, member, *refs):
    members, total = refs[:QUARTERS], refs[QUARTERS]
    order = range(QUARTERS)[::-1] if reverse else range(QUARTERS)
    for place in range(QUARTERS):

        @pl.when(member[0] == place)
        def _(place=place):
            for seq, lanes in parts_of_quarter():
                whole = None
                for which in order:
                    here = read_payload(members[place ^ which], seq, lanes)
                    whole = here if whole is None else after(whole, here)
                write_payload(total, seq, lanes, *whole)


def link_kernel(*refs):
    total, received, result = refs[0], refs[1:-1], refs[-1]
    for seq, lanes in parts_of_quarter():
        whole = after(joined(received, seq, lanes), read_payload(total, seq, lanes))
        write_payload(result, seq, lanes, *whole)


def spread_kernel(reverse, member, *refs):
    members, received, results = refs[:QUARTERS], refs[QUARTERS:-QUARTERS], refs[-QUARTERS:]
    order = list(range(QUARTERS)[::-1] if reverse else range(QUARTERS))
    for place in range(QUARTERS):

        @pl.when(member[0] == place)
        def _(place=place):
            for seq, lanes in parts_of_quarter():
                whole = joined(received, seq, lanes)
                for which in order:
                    write_payload(results[place ^ which], seq, lanes, *whole)
                    if which != order[-1]:
                        whole = after(whole, read_payload(members[place ^ which], seq, lanes))


def arrange_kernel(member, *refs):
    pieces, state_ref, along_ref = refs[:QUARTERS], refs[QUARTERS], refs[QUARTERS + 1]
    for by in range(QUARTERS):

        @pl.when(pl.program_id(0) == by)
        def _(by=by):
            for seq, lanes in parts_of_quarter():
                state_ref[seq, :, lanes] = pieces[by][seq, :STATE, lanes]
                rows = pieces[by][seq, STATE:, lanes].astype(F32)
                along = rows[3:4] + rows[4:5] + rows[5:6]
                along_ref[seq, :, lanes] = jnp.broadcast_to(along, (8, TILE))


def step_kernel(
    conv_input,
    weight,
    bias,
    small,
    direction,
    bc_ref,
    bt_ref,
    scores_ref,
    scores_t_ref,
    step_ref,
    sum_ref,
    step_q_ref,
    sum_q_ref,
    sum_t_ref,
):
    row = lax.broadcasted_iota(jnp.int32, (256, 256), 0)
    col = lax.broadcasted_iota(jnp.int32, (256, 256), 1)
    lower = (row >= col).astype(F32)
    lane = lax.broadcasted_iota(jnp.int32, (1, TILE), 1)
    for seq in range(2):
        mixture = mixture_of(conv_input, seq, slice(0, 256), weight[...], bias[...])
        active = mixture * jax.nn.sigmoid(mixture)
        bc_ref[seq] = active
        writes, readout = active[:, :STATE], active[:, STATE:]
        bt_ref[seq] = writes.T.astype(BF16)
        scores = dot_last(readout, writes, HIGHEST)
        scores_ref[seq] = scores
        scores_t_ref[seq] = scores.T
        along = jnp.sum(readout * direction[...], axis=1, keepdims=True)
        raw = conv_input[seq, EDGE : EDGE + 256, 256:384] + small[0:1]
        raw = jnp.where(lane < HEADS, raw, 0.0)
        step = jnp.maximum(raw, 0.0) + jnp.log1p(jnp.exp(-jnp.abs(raw)))
        log_decay = -jnp.exp(small[1:2]) * step
        running = jnp.dot(lower, log_decay, preferred_element_type=F32, precision=HIGHEST)
        step_ref[seq] = step
        sum_ref[seq] = jnp.where(lane == HEADS, along, running)
        for quarter in range(QUARTERS):
            shift = (TILE - Q_HEADS * quarter) % TILE
            step_q = pltpu.roll(step, shift, 1) if shift else step
            sum_q = pltpu.roll(running, shift, 1) if shift else running
            step_q_ref[quarter, seq] = step_q[:, :SIDE]
            sum_q_ref[quarter, seq] = jnp.where(lane == Q_HEADS, along, sum_q)[:, :SIDE]
            sum_t_ref[quarter, seq] = sum_q.T[:EDGE]


def state_kernel(
    member, conv_input, weight, bias, step_q, sum_q, bt_ref, column, x_ref, payload_ref
):
    for seq in range(2):
        running = sum_q[0, seq]
        last = running[255:256]
        scale = step_q[0, seq] * jnp.exp(last - running)
        whole = jnp.exp(last)
        for tile in range(Q_TILES):
            lanes = slice(TILE * tile, TILE * tile + TILE)
            mixture = mixture_of(conv_input, seq, lanes, weight[:, lanes], bias[:, lanes])
            x = mixture * jax.nn.sigmoid(mixture)
            x_ref[seq, :, lanes] = x
            added = dot(bt_ref[seq], (x * pick(scale, tile)).astype(BF16))
            along = jnp.sum(added * column[...], axis=0, keepdims=True)
            payload_ref[0, seq, :STATE, lanes] = (added - column[...] * along).astype(BF16)
            payload_ref[0, seq, STATE:, lanes] = edge_rows(pick(whole, tile), along)


def intra_kernel(x_ref, step_q, sum_q, sum_t, scores, skip, *refs):
    y_ref = refs[-1]
    row = lax.broadcasted_iota(jnp.int32, (SUB, SUB), 0)
    col = lax.broadcasted_iota(jnp.int32, (SUB, SUB), 1)
    causal = row >= col
    low = low_lanes()
    for seq in range(2):
        step, running = step_q[0, seq], sum_q[0, seq]
        middle = running[SUB - 1 : SUB]
        ahead = jnp.exp(middle - running[:SUB])
        later = jnp.exp(running[SUB:] - middle)
        across = scores[seq, SUB:, :SUB].astype(BF16)
        for tile in range(Q_TILES):
            lanes = slice(TILE * tile, TILE * tile + TILE)
            x = x_ref[seq, :, lanes]
            scaled = x * pick(step, tile)
            low_part = jnp.where(low, scaled, 0.0).astype(BF16)
            high_part = jnp.where(low, 0.0, scaled).astype(BF16)
            for part in range(2):
                rows = slice(SUB * part, SUB * part + SUB)
                weights = []
                for h in (2 * tile, 2 * tile + 1):
                    spread = running[rows, h : h + 1] - sum_t[0, seq, h : h + 1, rows]
                    decayed = jnp.exp(jnp.where(causal, spread, FAR))
                    weights.append((decayed * scores[seq, rows, rows]).astype(BF16))
                inside = dot(
                    jnp.concatenate(weights, 1),
                    jnp.concatenate([low_part[rows], high_part[rows]], 0),
                )
                if part:
                    earlier = (scaled[:SUB] * pick(ahead, tile)).astype(BF16)
                    inside = inside + pick(later, tile) * dot(across, earlier)
                y_ref[seq, rows, lanes] = inside + skip[:, lanes] * x[rows]


def gate_kernel(
    member,
    y_ref,
    z_ref,
    grad_ref,
    bc_ref,
    sum_ref,
    entering,
    along,
    gain,
    out_ref,
    grad_z_ref,
    grad_scan_ref,
    payload_ref,
    gain_grad_ref,
    scanned_ref,
    gated_ref,
    gate_ref,
    spread,
    state_ref,
):
    step = pl.program_id(0)
    per_seq = pl.num_programs(0) // 2
    running = sum_ref[0]
    start = jnp.exp(running)
    read_along = running[:, HEADS : HEADS + 1]
    readout = bc_ref[0, :, STATE:].astype(BF16)
    scanned_ref[...] = dot(readout, entering[0])
    squares = jnp.zeros((ROWS, TILE), F32)
    overlap = jnp.zeros((ROWS, TILE), F32)
    for tile in range(INNER // TILE):
        lanes = slice(TILE * tile, TILE * tile + TILE)
        carried = scanned_ref[:, lanes] + read_along * along[0, 0:1, lanes]
        scanned = y_ref[0, :, lanes] + pick(start, tile) * carried
        scanned_ref[:, lanes] = scanned
        z = z_ref[0, :, lanes]
        gate = jax.nn.sigmoid(z)
        gate_ref[:, lanes] = gate
        gated = scanned * (z * gate)
        gated_ref[:, lanes] = gated
        squares = squares + gated * gated
        overlap = overlap + gated * (grad_ref[0, :, lanes] * gain[:, lanes])
    mean = jnp.sum(squares, axis=1, keepdims=True) / INNER
    inverse = lax.rsqrt(mean + EPSILON)
    back = jnp.sum(overlap, axis=1, keepdims=True) / INNER * inverse * inverse * inverse

    @pl.when(step == 0)
    def _():
        gain_grad_ref[...] = jnp.zeros_like(gain_grad_ref)

    for tile in range(INNER // TILE):
        lanes = slice(TILE * tile, TILE * tile + TILE)
        gated = gated_ref[:, lanes]
        grad = grad_ref[0, :, lanes]
        scaled = gated * inverse
        out_ref[0, :, lanes] = (scaled * gain[:, lanes]).astype(BF16)
        gain_grad_ref[:, lanes] += jnp.sum(grad * scaled, axis=0, keepdims=True)
        grad_gated = inverse * (grad * gain[:, lanes]) - gated * back
        z = z_ref[0, :, lanes]
        gate = gate_ref[:, lanes]
        grad_scan = grad_gated * (z * gate)
        grad_z_ref[0, :, lanes] = (
            grad_gated * scanned_ref[:, lanes] * (gate * (1.0 + z * (1.0 - gate)))
        ).astype(BF16)
        grad_scan_ref[0, :, lanes] = grad_scan
        rounded = grad_scan.astype(BF16).astype(F32)
        spread[:, lanes] = (rounded * pick(start, tile)).astype(BF16)
    added = dot_first(readout, spread[...])

    @pl.when(step % per_seq == 0)
    def _():
        state_ref[...] = added

    @pl.when(step % per_seq != 0)
    def _():
        state_ref[...] += added

    @pl.when(step % per_seq == per_seq - 1)
    def _():
        seq = step // per_seq
        whole = start[ROWS - 1 : ROWS]
        zero = jnp.zeros((1, TILE), F32)
        for tile in range(INNER // TILE):
            lanes = slice(TILE * tile, TILE * tile + TILE)
            place = slice(TILE * (tile % Q_TILES), TILE * (tile % Q_TILES) + TILE)
            slot = member[0] ^ (tile // Q_TILES)
            payload_ref[slot, seq, :STATE, place] = state_ref[:, lanes].astype(BF16)
            payload_ref[slot, seq, STATE:, place] = edge_rows(pick(whole, tile), zero)


def intra_back_kernel(
    x_ref,
    grad_ref,
    y_ref,
    conv_input,
    weight,
    bias,
    step_q,
    sum_q,
    sum_t,
    scores_t,
    bc_ref,
    entering,
    along,
    skip,
    direction,
    *refs,
):
    known_ref, slope_ref, grad_scores_ref, heads_ref, grad_read_ref, product, spread = refs[-7:]
    row = lax.broadcasted_iota(jnp.int32, (SUB, SUB), 0)
    col = lax.broadcasted_iota(jnp.int32, (SUB, SUB), 1)
    causal = row <= col
    low = low_lanes()

    @pl.when(pl.program_id(0) == 0)
    def _():
        grad_scores_ref[...] = jnp.zeros_like(grad_scores_ref)
        grad_read_ref[...] = jnp.zeros_like(grad_read_ref)

    for seq in range(2):
        step, running = step_q[0, seq], sum_q[0, seq]
        middle = running[SUB - 1 : SUB]
        start = jnp.exp(running)
        read_along = running[:, Q_HEADS : Q_HEADS + 1]
        ahead = jnp.exp(middle - running[:SUB])
        later = jnp.exp(running[SUB:] - middle)
        across = scores_t[seq, :SUB, SUB:].astype(BF16)
        readout = bc_ref[seq, :, STATE:].astype(BF16)
        inner = [jnp.zeros((SUB, SUB), F32) for _ in range(2)]
        outer = jnp.zeros((SUB, SUB), F32)
        meeting = jnp.zeros((256, TILE), F32)
        for tile in range(Q_TILES):
            lanes = slice(TILE * tile, TILE * tile + TILE)
            x = x_ref[seq, :, lanes]
            size = pick(step, tile)
            scaled = x * size
            grad = grad_ref[seq, :, lanes]
            begin = pick(start, tile)
            low_grad = jnp.where(low, grad, 0.0).astype(BF16)
            high_grad = jnp.where(low, 0.0, grad).astype(BF16)
            rounded = grad.astype(BF16)
            line = along[seq, 0:1, lanes]
            carried = dot(readout, entering[seq, :, lanes]) + read_along * line
            through = skip[:, lanes] * x
            product[2, :, lanes] = rounded.astype(F32) * (
                y_ref[seq, :, lanes] + begin * carried - through
            )
            widened = grad * begin
            meeting = meeting + widened * line
            spread[:, lanes] = widened.astype(BF16)
            mixture = mixture_of(conv_input, seq, lanes, weight[:, lanes], bias[:, lanes])
            slope = silu_slope(mixture)
            slope_ref[seq, :, lanes] = slope.astype(BF16)
            sides = (
                jnp.where(low, scaled, 0.0).astype(BF16),
                jnp.where(low, 0.0, scaled).astype(BF16),
            )
            for part in range(2):
                rows = slice(SUB * part, SUB * part + SUB)
                weights = []
                for side in range(2):
                    h = 2 * tile + side
                    apart = sum_t[0, seq, h : h + 1, rows] - running[rows, h : h + 1]
                    decayed = jnp.exp(jnp.where(causal, apart, FAR))
                    weights.append((decayed * scores_t[seq, rows, rows]).astype(BF16))
                    inner[part] = inner[part] + decayed * dot_last(
                        sides[side][rows], rounded[rows]
                    )
                inside = dot(
                    jnp.concatenate(weights, 1),
                    jnp.concatenate([low_grad[rows], high_grad[rows]], 0),
                )
                if not part:
                    beyond = (rounded[SUB:].astype(F32) * pick(later, tile)).astype(BF16)
                    factor = pick(ahead, tile)
                    inside = inside + factor * dot(across, beyond)
                    outer = outer + dot_last((scaled[:SUB] * factor).astype(BF16), beyond)
                product[0, rows, lanes] = scaled[rows].astype(BF16).astype(F32) * inside
                product[1, rows, lanes] = x[rows] * inside
                known_ref[seq, rows, lanes] = (
                    size[rows] * inside + skip[:, lanes] * grad[rows]
                ) * slope[rows]
        grad_scores_ref[seq, :SUB, :SUB] += inner[0]
        grad_scores_ref[seq, SUB:, SUB:] += inner[1]
        grad_scores_ref[seq, :SUB, SUB:] += outer
        total = jnp.zeros((256, TILE), F32)
        for kind in range(3):
            total = total + head_sums(product[kind], head_columns(Q_LANES, TILE, Q_HEADS * kind))
        heads_ref[0, seq] = total
        grad_read_ref[seq] += (
            dot_last(spread[...], entering[seq])
            + jnp.sum(meeting, axis=1, keepdims=True) * direction[...]
        )


def channel_kernel(
    known_ref,
    slope_ref,
    x_ref,
    weight,
    step_q,
    sum_q,
    bc_ref,
    leaving,
    entering,
    along,
    column,
    grad_conv_ref,
    tail_ref,
    halo_ref,
    grad_mix_ref,
    heads_ref,
    grad_writes_ref,
    meeting_ref,
    padded,
    product,
    spread,
):
    zeros = jnp.zeros((EDGE, TILE), F32)
    padded[:EDGE] = zeros
    padded[EDGE + 256 :] = zeros
    meeting_ref[...] = jnp.zeros_like(meeting_ref)

    @pl.when(pl.program_id(0) == 0)
    def _():
        grad_writes_ref[...] = jnp.zeros_like(grad_writes_ref)

    for seq in range(2):
        running = sum_q[0, seq]
        remain = jnp.exp(running[255:256] - running)
        scale = step_q[0, seq] * remain
        writes = bc_ref[seq, :, :STATE].astype(BF16)
        for tile in range(Q_TILES):
            lanes = slice(TILE * tile, TILE * tile + TILE)
            taps = weight[:, lanes]
            x = x_ref[seq, :, lanes]
            back = leaving[seq, :, lanes]
            shared = dot(writes, back)
            left = pick(remain, tile)
            product[:, lanes] = x * (left * shared)
            factor = pick(scale, tile)
            spread[:, lanes] = (x * factor).astype(BF16)
            slope = slope_ref[seq, :, lanes].astype(F32)
            grad_mix = known_ref[seq, :, lanes] + factor * slope * shared
            grad_mix_ref[seq, :, lanes] = grad_mix.astype(BF16)
            padded[EDGE : EDGE + 256] = grad_mix
            grad_conv = taps[0:1] * padded[3 : 3 + EDGE + 256]
            for tap in range(1, CONV):
                grad_conv = (
                    grad_conv + taps[tap : tap + 1] * padded[3 - tap : 3 - tap + EDGE + 256]
                )
            halo_ref[seq, :, lanes] = grad_conv[:EDGE].astype(BF16)
            grad_conv_ref[seq, :, lanes] = grad_conv[EDGE:].astype(BF16)
            tail_ref[seq, :, lanes] = grad_conv[256:]
            state = entering[seq, :, lanes].astype(F32) + column[...] * along[seq, 0:1, lanes]
            meeting_ref[seq : seq + 1, lanes] = jnp.sum(
                state * back.astype(F32), axis=0, keepdims=True
            )
        heads_ref[0, seq] = head_sums(product[...], head_columns(Q_LANES, TILE, 0))
        grad_writes_ref[seq] += dot_last(spread[...], leaving[seq])


def sums_kernel(conv_input, grad_mix_ref, grad_ref, x_ref, sums_ref):
    sums_ref[...] = jnp.zeros_like(sums_ref)
    for seq in range(2):
        for tile in range(Q_TILES):
            lanes = slice(TILE * tile, TILE * tile + TILE)
            grad_mix = grad_mix_ref[seq, :, lanes].astype(F32)
            for tap in range(CONV):
                begin = EDGE - CONV + 1 + tap
                sums_ref[tap : tap + 1, lanes] += jnp.sum(
                    grad_mix * conv_input[seq, begin : begin + 256, lanes], axis=0, keepdims=True
                )
            sums_ref[4:5, lanes] += jnp.sum(grad_mix, axis=0, keepdims=True)
            sums_ref[5:6, lanes] += jnp.sum(
                grad_ref[seq, :, lanes] * x_ref[seq, :, lanes], axis=0, keepdims=True
            )


def last_kernel(
    conv_input,
    weight,
    bias,
    small,
    bc_ref,
    grad_scores_0,
    grad_scores_1,
    grad_writes,
    grad_read_0,
    grad_read_1,
    known_heads,
    heads,
    meeting,
    step_ref,
    sum_ref,
    grad_conv_ref,
    tail_ref,
    halo_ref,
    sums_ref,
    small_ref,
    padded,
):
    row = lax.broadcasted_iota(jnp.int32, (256, 256), 0)
    col = lax.broadcasted_iota(jnp.int32, (256, 256), 1)
    upper = (row <= col).astype(F32)
    lane = lax.broadcasted_iota(jnp.int32, (1, TILE), 1)
    line = lax.broadcasted_iota(jnp.int32, (256, 1), 0)
    padded[:EDGE] = jnp.zeros((EDGE, 256), F32)
    padded[EDGE + 256 :] = jnp.zeros((EDGE, 256), F32)
    sums_ref[...] = jnp.zeros_like(sums_ref)
    small_ref[...] = jnp.zeros_like(small_ref)
    rate = jnp.exp(small[1:2])
    met_states = head_sums(meeting[...], head_columns(INNER, TILE, 0))
    taps = weight[...]

    def gather(source, seq, kind):
        total = jnp.zeros((256, TILE), F32)
        for quarter in range(QUARTERS):
            value = source[quarter, seq]
            shift = (Q_HEADS * (quarter - kind)) % TILE
            if shift:
                value = pltpu.roll(value, shift, 1)
            first = Q_HEADS * quarter
            total = total + jnp.where((lane >= first) & (lane < first + Q_HEADS), value, 0.0)
        return total

    for seq in range(2):
        step = step_ref[seq]
        by_state = gather(heads, seq, 0)
        at_state = step * by_state
        running = sum_ref[seq]
        last = jnp.where(lane < HEADS, running[255:256], 0.0)
        end = jnp.exp(last) * met_states[seq : seq + 1] + jnp.sum(
            at_state, axis=0, keepdims=True
        )
        grad_sum = (
            gather(known_heads, seq, 2)
            - gather(known_heads, seq, 0)
            - at_state
            + jnp.where(line == 255, end, 0.0)
        )
        grad_log = jnp.dot(upper, grad_sum, preferred_element_type=F32, precision=HIGHEST)
        small_ref[1:2] += jnp.sum(-rate * step * grad_log, axis=0, keepdims=True)
        raw = conv_input[seq, EDGE : EDGE + 256, 256:384] + small[0:1]
        raw = jnp.where(lane < HEADS, raw, 0.0)
        grad_step = gather(known_heads, seq, 1) + by_state - rate * grad_log
        grad_raw = grad_step * jax.nn.sigmoid(raw)
        small_ref[0:1] += jnp.sum(grad_raw, axis=0, keepdims=True)
        grad_conv_ref[seq, :, 256:] = grad_raw[:, :HEADS].astype(BF16)
        writes, readout = bc_ref[seq, :, :STATE], bc_ref[seq, :, STATE:]
        grad_scores = grad_scores_0[seq] + grad_scores_1[seq]
        into_writes = (
            jnp.dot(grad_scores, readout, preferred_element_type=F32, precision=HIGHEST)
            + grad_writes[seq]
        )
        into_read = dot_first(grad_scores, writes, HIGHEST) + grad_read_0[seq] + grad_read_1[seq]
        mixture = mixture_of(conv_input, seq, slice(0, 256), taps, bias[...])
        grad_mix = jnp.concatenate([into_writes, into_read], 1) * silu_slope(mixture)
        padded[EDGE : EDGE + 256] = grad_mix
        grad_conv = taps[0:1] * padded[3 : 3 + EDGE + 256]
        for tap in range(1, CONV):
            grad_conv = grad_conv + taps[tap : tap + 1] * padded[3 - tap : 3 - tap + EDGE + 256]
        halo_ref[seq] = grad_conv[:EDGE].astype(BF16)
        grad_conv_ref[seq, :, :256] = grad_conv[EDGE:].astype(BF16)
        tail_ref[seq] = grad_conv[256:]
        for tap in range(CONV):
            begin = EDGE - CONV + 1 + tap
            sums_ref[tap : tap + 1] += jnp.sum(
                grad_mix * conv_input[seq, begin : begin + 256, :256], axis=0, keepdims=True
            )
        sums_ref[4:5] += jnp.sum(grad_mix, axis=0, keepdims=True)


def shape(dims, dtype=F32):
    return jax.ShapeDtypeStruct(dims, dtype)


def whole_block(dims):
    return pl.BlockSpec(dims, lambda *g: (0,) * len(dims))


def lane_block(dims, width=Q_LANES):
    return pl.BlockSpec(dims + (width,), lambda g: (0,) * len(dims) + (g,))


def quarter_block(dims):
    return pl.BlockSpec((1,) + dims, lambda g, *_: (g,) + (0,) * len(dims))


def own_lanes(dims):
    return pl.BlockSpec(
        dims + (Q_LANES,), lambda g, member: (0,) * len(dims) + (g ^ member[0],)
    )


def own_quarter(dims):
    return pl.BlockSpec((1,) + dims, lambda g, member: (g ^ member[0],) + (0,) * len(dims))


def fixed_block(dims, index):
    return pl.BlockSpec(dims, lambda g: index)


def row_block(width, length=256):
    steps = length // ROWS
    return pl.BlockSpec((1, ROWS, width), lambda g: (g // steps, g % steps, 0))


SCALAR = pl.BlockSpec(memory_space=pltpu.SMEM)
MESSAGE = (2, PAYLOAD, Q_LANES)


def tie(value, *others):
    return lax.optimization_barrier((value,) + others)[0]


def exchange(payload, member, axis, reverse, stages):
    count = lax.axis_size(axis)
    stages = iter(stages)

    def swap(value, by):
        return lax.ppermute(value, axis, [(i, i ^ by) for i in range(count)])

    def meanwhile(sent, arrived):
        work = next(stages, None)
        return tie(arrived, *work(sent)) if work else arrived

    message = shape(MESSAGE, BF16)
    block = whole_block(MESSAGE)
    members = [payload[0]] + [swap(payload[by], by) for by in range(1, QUARTERS)]
    members[-1] = meanwhile(payload, members[-1])
    total = pl.pallas_call(
        functools.partial(plane_kernel, reverse),
        grid=(1,),
        in_specs=[SCALAR] + [block] * QUARTERS,
        out_specs=block,
        out_shape=message,
        compiler_params=params(),
        cost_estimate=cost(2),
        name="plane",
    )(member, *members)
    received = []
    inclusive = total
    span = 1
    while span < count // QUARTERS:
        shift = -QUARTERS * span if reverse else QUARTERS * span
        pairs = [(i, i + shift) for i in range(count) if 0 <= i + shift < count]
        arrived = lax.ppermute(inclusive, axis, pairs)
        received.append(meanwhile(inclusive, arrived) if span < 4 else arrived)
        span *= 2
        if span < count // QUARTERS:
            inclusive = pl.pallas_call(
                link_kernel,
                grid=(1,),
                in_specs=[block] * (1 + len(received)),
                out_specs=block,
                out_shape=message,
                compiler_params=params(),
                cost_estimate=cost(1.5),
                name="link",
            )(total, *received)
    results = pl.pallas_call(
        functools.partial(spread_kernel, reverse),
        grid=(1,),
        in_specs=[SCALAR] + [block] * (QUARTERS + len(received)),
        out_specs=[block] * QUARTERS,
        out_shape=[message] * QUARTERS,
        compiler_params=params(),
        cost_estimate=cost(3),
        name="spread",
    )(member, *members, *received)
    back = [results[0]] + [swap(results[by], by) for by in range(1, QUARTERS)]
    back[-1] = meanwhile(results[-1], back[-1])
    return pl.pallas_call(
        arrange_kernel,
        grid_spec=pltpu.PrefetchScalarGridSpec(
            num_scalar_prefetch=1,
            grid=(QUARTERS,),
            in_specs=[block] * QUARTERS,
            out_specs=[own_lanes((2, STATE)), own_lanes((2, 8))],
        ),
        out_shape=[shape((2, STATE, INNER), BF16), shape((2, 8, INNER))],
        compiler_params=params(),
        cost_estimate=cost(1.5),
        name="arrange",
    )(member, *back)


class Scatter:
    def __init__(self, arrays, axis):
        self.axis = axis
        self.count = lax.axis_size(axis)
        self.place = lax.axis_index(axis)
        self.bits = list(range(self.count.bit_length() - 1))[::-1]
        self.values = [
            a.reshape((2,) * len(self.bits) + (a.shape[0] // self.count, a.shape[1]))
            for a in arrays
        ]

    def wait_for(self, *others):
        self.values = list(lax.optimization_barrier(tuple(self.values) + others))[
            : len(self.values)
        ]

    def send(self, bit):
        position = self.bits.index(bit)
        mine = (self.place >> bit) & 1
        away = [lax.dynamic_index_in_dim(v, 1 - mine, position, False) for v in self.values]
        away = jnp.concatenate([v.astype(BF16) for v in away], axis=-2)
        self.values = [lax.dynamic_index_in_dim(v, mine, position, False) for v in self.values]
        self.bits.remove(bit)
        self.sent = lax.ppermute(
            away, self.axis, [(i, i ^ (1 << bit)) for i in range(self.count)]
        )

    def add(self):
        begin = 0
        for i, value in enumerate(self.values):
            end = begin + value.shape[-2]
            self.values[i] = value + self.sent[..., begin:end, :].astype(F32)
            begin = end


def add_up(value, axes):
    for axis in axes:
        count = lax.axis_size(axis)
        for bit in range(count.bit_length() - 1):
            value = value + lax.ppermute(value, axis, [(i, i ^ (1 << bit)) for i in range(count)])
    return value


def finish_kernel(gate_rows, last_rows, out_rows, in_grad, out_grad):
    step = pl.program_id(0)
    length, columns = gate_rows.shape[0] * gate_rows.shape[1], gate_rows.shape[2]

    @pl.when(step < 2 * INNER // length)
    def _():
        in_grad[...] = gate_rows[...].reshape(length, columns).astype(F32)

    @pl.when(step == 2 * INNER // length)
    def _():
        rows = last_rows.shape[0] * last_rows.shape[1]
        keep = min(rows, in_grad.shape[0])
        in_grad[:keep] = last_rows[...].reshape(rows, columns)[:keep].astype(F32)

    @pl.when(step < INNER // length)
    def _():
        group, per = out_rows.shape[0], out_rows.shape[1] // 2
        for side in range(2):
            out_grad[:, columns * side : columns * side + columns] = (
                out_rows[:, per * side : per * side + per].reshape(group * per, columns).astype(F32)
            )


def local(
    hidden_in,
    norm_gain,
    in_weight,
    conv_weight,
    conv_bias,
    step_bias,
    decay_log,
    skip_gain,
    gate_gain,
    out_weight,
    cotangent,
):
    hidden = hidden_in[0]
    upstream = cotangent[0]
    tokens, width = hidden.shape
    half = tokens // 2
    share = in_weight.shape[0]
    count = lax.axis_size("seq")
    core = lax.axis_index("fsdp")
    other = [(0, 1), (1, 0)]

    rows_of = in_weight.T
    conv_rows = rows_of[INNER:]
    conv_rows_other = lax.ppermute(conv_rows, "fsdp", other)

    paired = hidden.reshape(2, half, width)
    halo = lax.ppermute(paired[:, half - EDGE :], "seq", [(i, i + 1) for i in range(count - 1)])
    extended = jnp.concatenate([halo, paired], axis=1).reshape(2 * (half + EDGE), width)
    rows = extended.astype(F32)
    rescale = lax.rsqrt(jnp.mean(rows * rows, axis=-1, keepdims=True) + EPSILON)
    normed_ext = (rows * rescale * norm_gain).astype(BF16)

    rows_of_writes = rows_of[2 * INNER : 2 * INNER + STATE].astype(F32)
    power = 2.0 * jnp.sum(rows_of_writes * rows_of_writes, axis=1)
    deviation = jnp.sqrt(
        power * jnp.sum(jnp.square(conv_weight[:, INNER : INNER + STATE]), axis=0)
    )
    guess = jnp.zeros((STATE,), F32)
    for point, share_of in ((-1.7320508, 1 / 6), (0.0, 2 / 3), (1.7320508, 1 / 6)):
        guess = guess + share_of * jax.nn.silu(
            conv_bias[INNER : INNER + STATE] + point * deviation
        )
    direction = guess * lax.rsqrt(jnp.sum(guess * guess) + 1e-20)
    row_direction, column_direction = direction[None], direction[:, None]
    member = (lax.axis_index("seq") % QUARTERS).astype(jnp.int32).reshape(1)

    def mine(array, axis):
        first = lax.slice_in_dim(array, 0, share, axis=axis)
        second = lax.slice_in_dim(array, share, 2 * share, axis=axis)
        return (
            jnp.where(core == 0, first, second),
            jnp.where(core == 0, second, first),
        )

    def ordered(own, foreign, axis):
        return jnp.where(
            core == 0,
            jnp.concatenate([own, foreign], axis),
            jnp.concatenate([foreign, own], axis),
        )

    own_ext, other_ext = mine(normed_ext, 1)
    own_part = dot_last(own_ext, conv_rows)
    gate_rows = tie(rows_of[:INNER], own_part)
    gate_rows_other = lax.ppermute(gate_rows, "fsdp", other)
    conv_input = (own_part + dot_last(other_ext, conv_rows_other)).reshape(
        2, half + EDGE, CONV_CH + HEADS
    )
    out_rows = lax.all_gather(tie(out_weight, gate_rows_other), "fsdp", axis=0, tiled=True)
    normed = normed_ext.reshape(2, half + EDGE, width)[:, EDGE:].reshape(tokens, width)
    own_normed, other_normed = mine(normed, 1)

    small = jnp.pad(jnp.stack([step_bias, decay_log, skip_gain]), ((0, 5), (0, TILE - HEADS)))
    bias_row = conv_bias[None]
    gain_row = gate_gain[None]
    skip_row = jnp.repeat(skip_gain, HEAD_DIM)[None]

    last_columns = fixed_block((2, half + EDGE, 384), (0, 0, INNER // 384))
    last_taps = fixed_block((CONV, 256), (0, INNER // 256))
    last_bias = fixed_block((1, 256), (0, INNER // 256))
    per_quarter = (QUARTERS, 2, half, SIDE)
    bc, bt, scores, scores_t, step, running, step_q, sum_q, sum_t = pl.pallas_call(
        step_kernel,
        grid=(1,),
        in_specs=[
            last_columns,
            last_taps,
            last_bias,
            whole_block((8, TILE)),
            whole_block((1, STATE)),
        ],
        out_specs=[
            whole_block((2, half, 256)),
            whole_block((2, STATE, half)),
            whole_block((2, half, half)),
            whole_block((2, half, half)),
            whole_block((2, half, TILE)),
            whole_block((2, half, TILE)),
            whole_block(per_quarter),
            whole_block(per_quarter),
            whole_block((QUARTERS, 2, EDGE, half)),
        ],
        out_shape=[
            shape((2, half, 256)),
            shape((2, STATE, half), BF16),
            shape((2, half, half)),
            shape((2, half, half)),
            shape((2, half, TILE)),
            shape((2, half, TILE)),
            shape(per_quarter),
            shape(per_quarter),
            shape((QUARTERS, 2, EDGE, half)),
        ],
        compiler_params=params(),
        cost_estimate=cost(4),
        name="steps",
    )(conv_input, conv_weight, bias_row, small, row_direction)

    columns = lane_block((2, half + EDGE))
    taps_block = lane_block((CONV,))
    row_of = lane_block((1,))
    heads_block = quarter_block((2, half, SIDE))
    line_block = quarter_block((2, EDGE, half))
    tokens_block = lane_block((2, half))
    x, payload = pl.pallas_call(
        state_kernel,
        grid_spec=pltpu.PrefetchScalarGridSpec(
            num_scalar_prefetch=1,
            grid=(QUARTERS,),
            in_specs=[
                own_lanes((2, half + EDGE)),
                own_lanes((CONV,)),
                own_lanes((1,)),
                own_quarter((2, half, SIDE)),
                own_quarter((2, half, SIDE)),
                whole_block((2, STATE, half)),
                whole_block((STATE, 1)),
            ],
            out_specs=[own_lanes((2, half)), quarter_block(MESSAGE)],
        ),
        out_shape=[shape((2, half, INNER)), shape((QUARTERS,) + MESSAGE, BF16)],
        compiler_params=params(),
        cost_estimate=cost(8),
        name="states",
    )(member, conv_input, conv_weight, bias_row, step_q, sum_q, bt, column_direction)

    half_grid = QUARTERS // 2

    def later_half(spec, first):
        old = spec.index_map
        return pl.BlockSpec(spec.block_shape, lambda g: old(g + first))

    def shifted(specs, first):
        return [later_half(spec, first) for spec in specs]

    kept = {}

    def while_states_cross(sent):
        kept["grad"] = dot_last(tie(upstream, sent), out_rows).reshape(2, half, INNER)
        kept["gate"] = dot_last(tie(own_normed, sent), gate_rows)
        return kept["grad"], kept["gate"]

    def inside(first):
        def work(sent):
            specs = [
                tokens_block,
                heads_block,
                heads_block,
                line_block,
                whole_block((2, half, half)),
                row_of,
            ]
            inputs = [tie(x, sent), step_q, sum_q, sum_t, scores, skip_row]
            kept["inside"] = pl.pallas_call(
                intra_kernel,
                grid=(half_grid,),
                in_specs=shifted(specs, first)
                + [pl.BlockSpec(memory_space=pl.ANY)] * (first > 0),
                out_specs=later_half(tokens_block, first),
                out_shape=shape((2, half, INNER)),
                input_output_aliases={len(specs): 0} if first else {},
                compiler_params=params(),
                cost_estimate=cost(8),
                name="inside",
            )(*inputs, *([kept["inside"]] if first else []))
            return (kept["inside"],)

        return work

    def while_states_return(sent):
        kept["z"] = (
            kept["gate"] + dot_last(tie(other_normed, sent), gate_rows_other)
        ).reshape(2, half, INNER)
        return (kept["z"],)

    entering, along = exchange(
        payload,
        member,
        "seq",
        False,
        [while_states_cross, inside(0), inside(half_grid), while_states_return],
    )
    y_inside, z, grad_normed_out = kept["inside"], kept["z"], kept["grad"]

    token_rows = row_block(INNER)
    steps = half // ROWS
    normed_out, grad_z, grad_scan, back_payload, gate_gain_grad = pl.pallas_call(
        gate_kernel,
        grid=(2 * steps,),
        in_specs=[
            SCALAR,
            token_rows,
            token_rows,
            token_rows,
            row_block(256),
            row_block(TILE),
            pl.BlockSpec((1, STATE, INNER), lambda g: (g // steps, 0, 0)),
            pl.BlockSpec((1, 8, INNER), lambda g: (g // steps, 0, 0)),
            whole_block((1, INNER)),
        ],
        out_specs=[
            token_rows,
            token_rows,
            token_rows,
            whole_block((QUARTERS,) + MESSAGE),
            whole_block((1, INNER)),
        ],
        out_shape=[
            shape((2, half, INNER), BF16),
            shape((2, half, INNER), BF16),
            shape((2, half, INNER)),
            shape((QUARTERS,) + MESSAGE, BF16),
            shape((1, INNER)),
        ],
        scratch_shapes=[
            pltpu.VMEM((ROWS, INNER), F32),
            pltpu.VMEM((ROWS, INNER), F32),
            pltpu.VMEM((ROWS, INNER), F32),
            pltpu.VMEM((ROWS, INNER), BF16),
            pltpu.VMEM((STATE, INNER), F32),
        ],
        compiler_params=params(),
        cost_estimate=cost(14),
        name="gates",
    )(
        member,
        y_inside,
        z,
        grad_normed_out,
        bc,
        running,
        entering,
        along,
        gain_row,
    )

    normed_out = normed_out.reshape(tokens, INNER)
    grad_z = grad_z.reshape(tokens, INNER)
    first_out, second_out = normed_out[:, : INNER // 2], normed_out[:, INNER // 2 :]
    own_out = jnp.where(core == 0, first_out, second_out)
    other_out = jnp.where(core == 0, second_out, first_out)

    def weight_part(own, foreign):
        sent = lax.ppermute(dot_first(*foreign).astype(BF16), "fsdp", other)
        return dot_first(*own) + sent.astype(F32)

    def while_gradients_cross(sent):
        out_part = weight_part((own_out, upstream), (other_out, upstream))
        gate_part = weight_part((grad_z, own_normed), (grad_z, other_normed))
        kept["out"] = Scatter([out_part], "seq")
        kept["gates"] = Scatter([gate_part], "seq")
        return out_part, gate_part

    state_columns = lane_block((2, STATE))
    line_columns = lane_block((2, 8))
    edge_columns = lane_block((2, EDGE))
    back_parts = []

    def inside_back(first):
        def work(sent):
            if not first:
                for part, bit in ((kept["out"], 0), (kept["gates"], 1)):
                    part.wait_for(sent)
                    part.send(bit)
            specs = [
                tokens_block,
                tokens_block,
                tokens_block,
                columns,
                taps_block,
                row_of,
                heads_block,
                heads_block,
                line_block,
                whole_block((2, half, half)),
                whole_block((2, half, 256)),
                state_columns,
                line_columns,
                row_of,
                whole_block((1, STATE)),
            ]
            inputs = [
                x,
                tie(grad_scan, sent),
                y_inside,
                conv_input,
                conv_weight,
                bias_row,
                step_q,
                sum_q,
                sum_t,
                scores_t,
                bc,
                entering,
                along,
                skip_row,
                row_direction,
            ]
            earlier = [back_parts[0][i] for i in (0, 1, 3)] if first else []
            back_parts.append(
                pl.pallas_call(
                    intra_back_kernel,
                    grid=(half_grid,),
                    in_specs=shifted(specs, first)
                    + [pl.BlockSpec(memory_space=pl.ANY)] * len(earlier),
                    out_specs=shifted(
                        [
                            tokens_block,
                            tokens_block,
                            whole_block((2, half, half)),
                            quarter_block((2, half, TILE)),
                            whole_block((2, half, STATE)),
                        ],
                        first,
                    ),
                    out_shape=[
                        shape((2, half, INNER)),
                        shape((2, half, INNER), BF16),
                        shape((2, half, half)),
                        shape((QUARTERS, 2, half, TILE)),
                        shape((2, half, STATE)),
                    ],
                    scratch_shapes=[
                        pltpu.VMEM((3, half, Q_LANES), F32),
                        pltpu.VMEM((half, Q_LANES), BF16),
                    ],
                    input_output_aliases={
                        len(specs) + i: (0, 1, 3)[i] for i in range(len(earlier))
                    },
                    compiler_params=params(),
                    cost_estimate=cost(17),
                    name="inside_back",
                )(*inputs, *earlier)
            )
            return tuple(back_parts[-1])

        return work

    def while_gradients_return(sent):
        for part in (kept["out"], kept["gates"]):
            part.sent = tie(part.sent, sent)
            part.add()
        return kept["out"].values[0], kept["gates"].values[0]

    leaving, _ = exchange(
        back_payload,
        member,
        "seq",
        True,
        [while_gradients_cross, inside_back(0), inside_back(half_grid), while_gradients_return],
    )
    out_part, gate_part = kept["out"], kept["gates"]
    for part, bit in ((out_part, 1), (gate_part, 0)):
        part.wait_for(leaving)
        part.send(bit)
    known, slope, _, known_heads, _ = back_parts[1]
    grad_conv, tail, halo_grad, grad_mix, heads, grad_writes, meeting = pl.pallas_call(
        channel_kernel,
        grid=(QUARTERS,),
        in_specs=[
            tokens_block,
            tokens_block,
            tokens_block,
            taps_block,
            heads_block,
            heads_block,
            whole_block((2, half, 256)),
            state_columns,
            state_columns,
            line_columns,
            whole_block((STATE, 1)),
        ],
        out_specs=[
            tokens_block,
            edge_columns,
            edge_columns,
            tokens_block,
            quarter_block((2, half, TILE)),
            whole_block((2, half, STATE)),
            lane_block((8,)),
        ],
        out_shape=[
            shape((2, half, INNER), BF16),
            shape((2, EDGE, INNER)),
            shape((2, EDGE, INNER), BF16),
            shape((2, half, INNER), BF16),
            shape((QUARTERS, 2, half, TILE)),
            shape((2, half, STATE)),
            shape((8, INNER)),
        ],
        scratch_shapes=[
            pltpu.VMEM((half + 2 * EDGE, TILE), F32),
            pltpu.VMEM((half, Q_LANES), F32),
            pltpu.VMEM((half, Q_LANES), BF16),
        ],
        compiler_params=params(),
        cost_estimate=cost(12),
        name="channels",
    )(
        known,
        slope,
        x,
        conv_weight,
        step_q,
        sum_q,
        bc,
        leaving,
        entering,
        along,
        column_direction,
    )

    grad_conv_last, tail_last, halo_last, sums_last, small_grads = pl.pallas_call(
        last_kernel,
        grid=(1,),
        in_specs=[
            last_columns,
            last_taps,
            last_bias,
            whole_block((8, TILE)),
            whole_block((2, half, 256)),
            whole_block((2, half, half)),
            whole_block((2, half, half)),
            whole_block((2, half, STATE)),
            whole_block((2, half, STATE)),
            whole_block((2, half, STATE)),
            whole_block((QUARTERS, 2, half, TILE)),
            whole_block((QUARTERS, 2, half, TILE)),
            whole_block((8, INNER)),
            whole_block((2, half, TILE)),
            whole_block((2, half, TILE)),
        ],
        out_specs=[
            whole_block((2, half, 256 + HEADS)),
            whole_block((2, EDGE, 256)),
            whole_block((2, EDGE, 256)),
            whole_block((8, 256)),
            whole_block((8, TILE)),
        ],
        out_shape=[
            shape((2, half, 256 + HEADS), BF16),
            shape((2, EDGE, 256)),
            shape((2, EDGE, 256), BF16),
            shape((8, 256)),
            shape((8, TILE)),
        ],
        scratch_shapes=[pltpu.VMEM((half + 2 * EDGE, 256), F32)],
        compiler_params=params(),
        cost_estimate=cost(6),
        name="last",
    )(
        conv_input,
        conv_weight,
        bias_row,
        small,
        bc,
        back_parts[0][2],
        back_parts[1][2],
        grad_writes,
        back_parts[0][4],
        back_parts[1][4],
        known_heads,
        heads,
        meeting,
        step,
        running,
    )

    returned = lax.ppermute(
        jnp.concatenate([halo_grad, halo_last], axis=-1),
        "seq",
        [(i, i - 1) for i in range(1, count)],
    )
    fixed_tail = (jnp.concatenate([tail, tail_last], axis=-1) + returned.astype(F32)).astype(BF16)
    body = half - EDGE
    grad_wide = jnp.concatenate([grad_conv[:, :body], fixed_tail[:, :, :INNER]], axis=1)
    grad_wide = grad_wide.reshape(tokens, INNER)
    per = INNER // count
    per_last = -(-(CONV_CH + HEADS - INNER) // (16 * count)) * 16
    spare = per_last * count - (CONV_CH + HEADS - INNER)
    grad_narrow = jnp.concatenate(
        [
            grad_conv_last[:, :body],
            jnp.concatenate([fixed_tail[:, :, INNER:], grad_conv_last[:, body:, 256:]], axis=-1),
        ],
        axis=1,
    ).reshape(tokens, CONV_CH + HEADS - INNER)
    grad_padded = jnp.pad(grad_narrow, ((0, 0), (0, spare)))

    for part in (out_part, gate_part):
        part.sent = tie(part.sent, grad_wide)
        part.add()
    early = gate_part
    out_value = out_part.values[0]
    early.values.append(
        jnp.concatenate([out_value[..., :share], out_value[..., share:]], axis=-2)
    )
    bits = early.bits[::-1]
    early.send(bits[0])

    wide_part = weight_part((grad_wide, own_normed), (grad_wide, other_normed))
    last_part = weight_part((grad_padded, own_normed), (grad_padded, other_normed))
    cut = share // 2
    first_part = Scatter([wide_part[:, :cut], last_part[:, :cut]], "seq")
    second_part = Scatter([wide_part[:, cut:], last_part[:, cut:]], "seq")
    first_part.send(0)
    second_part.send(1)
    early.add()
    for bit in bits[1:]:
        early.send(bit)
        early.add()
    for part, bit in ((first_part, 1), (second_part, 0)):
        part.add()
        part.send(bit)
    for part in (first_part, second_part):
        part.add()
    late = second_part
    late.values = [
        jnp.concatenate(pair, axis=-1) for pair in zip(first_part.values, second_part.values)
    ]
    late.wait_for(*early.values)
    for bit in bits:
        late.send(bit)
        late.add()

    gate_value, out_value = early.values
    shard = jnp.concatenate([gate_value, out_value] + late.values, axis=-2).astype(BF16)
    gathered = lax.all_gather(shard, "seq", axis=0)

    grad_z, grad_wide, grad_narrow, normed_out, grad_mix = lax.optimization_barrier(
        (grad_z, grad_wide, grad_narrow, normed_out, grad_mix, shard)
    )[:5]

    def through_rows(first, second):
        return (
            dot(grad_z, first) + dot(grad_wide, second[:INNER]) + dot(grad_narrow, second[INNER:])
        )

    grad_normed = ordered(
        through_rows(gate_rows, conv_rows), through_rows(gate_rows_other, conv_rows_other), 1
    )
    u = hidden.astype(F32)
    r = lax.rsqrt(jnp.mean(u * u, axis=-1, keepdims=True) + EPSILON)
    norm_gain_grad = jnp.sum(grad_normed * u * r, axis=0)
    through = grad_normed * norm_gain
    input_grad = (
        upstream.astype(F32)
        + r * through
        - u * (r * r * r) * jnp.mean(through * u, axis=-1, keepdims=True)
    ).astype(BF16)
    block_out = (hidden.astype(F32) + dot(normed_out, out_rows)).astype(BF16)

    sums = pl.pallas_call(
        sums_kernel,
        grid=(QUARTERS,),
        in_specs=[columns, tokens_block, tokens_block, tokens_block],
        out_specs=lane_block((8,)),
        out_shape=shape((8, INNER)),
        compiler_params=params(),
        cost_estimate=cost(10),
        name="sums",
    )(conv_input, grad_mix, grad_scan, x)

    skip_grad = jnp.sum(sums[5].reshape(HEADS, HEAD_DIM), axis=1)
    vector = jnp.concatenate(
        [
            norm_gain_grad,
            sums[:5].reshape(-1),
            sums_last[:5].reshape(-1),
            small_grads[:2].reshape(-1),
            gate_gain_grad[0],
            jnp.pad(skip_grad, (0, TILE - HEADS)),
        ]
    )
    length = vector.shape[0]
    vector = add_up(vector.reshape(length // TILE, TILE), ("fsdp", "seq")).reshape(length)
    parts = []
    begin = 0
    for size in (width, 5 * INNER, 5 * 256, 2 * TILE, INNER, HEADS):
        parts.append(vector[begin : begin + size])
        begin += size
    conv_sums = jnp.concatenate(
        [parts[1].reshape(5, INNER), parts[2].reshape(5, 256)], axis=1
    )
    smalls = parts[3].reshape(2, TILE)[:, :HEADS]

    group = share // per
    parts_of = INNER // share
    gathered_block = (group, per, share)
    in_grad, out_grad = pl.pallas_call(
        finish_kernel,
        grid=(2 * parts_of + 1,),
        in_specs=[
            pl.BlockSpec(
                gathered_block,
                lambda g: (jnp.minimum(g, 2 * parts_of - 1) % parts_of, g // parts_of * 2 % 4, 0),
            ),
            pl.BlockSpec((count, per_last, share), lambda g: (0, 3 * per // per_last, 0)),
            pl.BlockSpec(gathered_block, lambda g: (jnp.minimum(g, parts_of - 1), 1, 0)),
        ],
        out_specs=[
            pl.BlockSpec((share, share), lambda g: (g, 0)),
            pl.BlockSpec((share // 2, width), lambda g: (jnp.minimum(g, parts_of - 1), 0)),
        ],
        out_shape=[shape((CONV_CH + HEADS + INNER, share)), shape((2 * share, width))],
        compiler_params=params(),
        cost_estimate=cost(14),
        name="finish",
    )(gathered, gathered, gathered)
    return (
        block_out[None],
        input_grad[None],
        parts[0],
        in_grad.T,
        conv_sums[:4],
        conv_sums[4],
        smalls[0],
        smalls[1],
        parts[5],
        parts[4],
        out_grad,
    )


def solution(mesh):
    return jax.shard_map(
        local,
        mesh=mesh,
        in_specs=(
            P("fsdp", "seq", None),
            P(),
            P("fsdp", None),
            P(),
            P(),
            P(),
            P(),
            P(),
            P(),
            P("fsdp", None),
            P("fsdp", "seq", None),
        ),
        out_specs=(
            P("fsdp", "seq", None),
            P("fsdp", "seq", None),
            P(),
            P("fsdp", None),
            P(),
            P(),
            P(),
            P(),
            P(),
            P(),
            P("fsdp", None),
        ),
        check_vma=False,
    )
```

```python
import functools

import jax
import jax.numpy as jnp
from jax import lax
from jax.experimental import pallas as pl
from jax.experimental.pallas import tpu as pltpu
from jax.sharding import PartitionSpec as P

HEADS = 48
HEAD_DIM = 64
STATE = 128
CONV = 4
INNER = 3072
CONV_CH = 3328
EPSILON = 1e-05

QUARTERS = 4
Q_HEADS = HEADS // QUARTERS
Q_LANES = INNER // QUARTERS
TILE = 128
Q_TILES = Q_LANES // TILE
EDGE = 16
PAYLOAD = STATE + EDGE
ROWS = 128
SIDE = 16
SUB = 128
FAR = -1e30
VMEM = 60 * 1024 * 1024
HIGHEST = lax.Precision.HIGHEST
F32 = jnp.float32
BF16 = jnp.bfloat16


def params():
    return pltpu.CompilerParams(vmem_limit_bytes=VMEM)


def cost(microseconds):
    return pl.CostEstimate(
        flops=0, transcendentals=0, bytes_accessed=int(microseconds * 3_400_000)
    )


def low_lanes():
    return lax.broadcasted_iota(jnp.int32, (1, TILE), 1) < HEAD_DIM


def pick(per_head, tile):
    return jnp.where(
        low_lanes(),
        per_head[:, 2 * tile : 2 * tile + 1],
        per_head[:, 2 * tile + 1 : 2 * tile + 2],
    )


def head_columns(channels, columns, offset):
    row = lax.broadcasted_iota(jnp.int32, (channels, columns), 0)
    col = lax.broadcasted_iota(jnp.int32, (channels, columns), 1) - offset
    return ((row >= HEAD_DIM * col) & (row < HEAD_DIM * col + HEAD_DIM)).astype(BF16)


def head_sums(wide, selector):
    high = wide.astype(BF16)
    rest = (wide - high.astype(F32)).astype(BF16)
    return jnp.dot(high, selector, preferred_element_type=F32) + jnp.dot(
        rest, selector, preferred_element_type=F32
    )


def dot(left, right):
    return jnp.dot(left, right, preferred_element_type=F32)


def dot_last(left, right, precision=None):
    return lax.dot_general(
        left,
        right,
        (((1,), (1,)), ((), ())),
        preferred_element_type=F32,
        precision=precision,
    )


def dot_first(left, right, precision=None):
    return lax.dot_general(
        left,
        right,
        (((0,), (0,)), ((), ())),
        preferred_element_type=F32,
        precision=precision,
    )


def mixture_of(conv_input, seq, lanes, weight, bias):
    total = bias
    for tap in range(CONV):
        start = EDGE - CONV + 1 + tap
        total = total + weight[tap : tap + 1] * conv_input[seq, start : start + 256, lanes]
    return total


def silu_slope(value):
    gate = jax.nn.sigmoid(value)
    return gate * (1.0 + value * (1.0 - gate))


def three_parts(value):
    high = value.astype(BF16).astype(F32)
    middle = (value - high).astype(BF16).astype(F32)
    return high, middle, value - high - middle


def edge_rows(decay, along):
    index = lax.broadcasted_iota(jnp.int32, (EDGE, TILE), 0)
    rows = jnp.zeros((EDGE, TILE), F32)
    for row, part in enumerate(three_parts(decay) + three_parts(along)):
        rows = jnp.where(index == row, part, rows)
    return rows.astype(BF16)


def read_payload(ref, seq, lanes):
    state = ref[seq, :STATE, lanes].astype(F32)
    rows = ref[seq, STATE:, lanes].astype(F32)
    decay = rows[0:1] + rows[1:2] + rows[2:3]
    along = rows[3:4] + rows[4:5] + rows[5:6]
    return state, decay, along


def write_payload(ref, seq, lanes, state, decay, along):
    ref[seq, :STATE, lanes] = state.astype(BF16)
    ref[seq, STATE:, lanes] = edge_rows(decay, along)


def after(first, second):
    return (
        second[0] + second[1] * first[0],
        second[1] * first[1],
        second[2] + second[1] * first[2],
    )


def empty():
    return (
        jnp.zeros((STATE, TILE), F32),
        jnp.ones((1, TILE), F32),
        jnp.zeros((1, TILE), F32),
    )


def parts_of_quarter():
    for seq in range(2):
        for tile in range(Q_TILES):
            yield seq, slice(TILE * tile, TILE * tile + TILE)


def joined(refs, seq, lanes):
    result = read_payload(refs[0], seq, lanes)
    for ref in refs[1:]:
        result = after(read_payload(ref, seq, lanes), result)
    return result


def plane_kernel(reverse, member, *refs):
    members, total = refs[:QUARTERS], refs[QUARTERS]
    order = range(QUARTERS)[::-1] if reverse else range(QUARTERS)
    for place in range(QUARTERS):

        @pl.when(member[0] == place)
        def _(place=place):
            for seq, lanes in parts_of_quarter():
                whole = None
                for which in order:
                    here = read_payload(members[place ^ which], seq, lanes)
                    whole = here if whole is None else after(whole, here)
                write_payload(total, seq, lanes, *whole)


def link_kernel(*refs):
    total, received, result = refs[0], refs[1:-1], refs[-1]
    for seq, lanes in parts_of_quarter():
        whole = after(joined(received, seq, lanes), read_payload(total, seq, lanes))
        write_payload(result, seq, lanes, *whole)


def spread_kernel(reverse, member, *refs):
    members, received, results = refs[:QUARTERS], refs[QUARTERS:-QUARTERS], refs[-QUARTERS:]
    order = list(range(QUARTERS)[::-1] if reverse else range(QUARTERS))
    for place in range(QUARTERS):

        @pl.when(member[0] == place)
        def _(place=place):
            for seq, lanes in parts_of_quarter():
                whole = joined(received, seq, lanes)
                for which in order:
                    write_payload(results[place ^ which], seq, lanes, *whole)
                    if which != order[-1]:
                        whole = after(whole, read_payload(members[place ^ which], seq, lanes))


def arrange_kernel(member, *refs):
    pieces, state_ref, along_ref = refs[:QUARTERS], refs[QUARTERS], refs[QUARTERS + 1]
    for by in range(QUARTERS):

        @pl.when(pl.program_id(0) == by)
        def _(by=by):
            for seq, lanes in parts_of_quarter():
                state_ref[seq, :, lanes] = pieces[by][seq, :STATE, lanes]
                rows = pieces[by][seq, STATE:, lanes].astype(F32)
                along = rows[3:4] + rows[4:5] + rows[5:6]
                along_ref[seq, :, lanes] = jnp.broadcast_to(along, (8, TILE))


def step_kernel(
    conv_input,
    weight,
    bias,
    small,
    direction,
    bc_ref,
    bt_ref,
    scores_ref,
    scores_t_ref,
    step_ref,
    sum_ref,
    step_q_ref,
    sum_q_ref,
    sum_t_ref,
):
    row = lax.broadcasted_iota(jnp.int32, (256, 256), 0)
    col = lax.broadcasted_iota(jnp.int32, (256, 256), 1)
    lower = (row >= col).astype(F32)
    lane = lax.broadcasted_iota(jnp.int32, (1, TILE), 1)
    for seq in range(2):
        mixture = mixture_of(conv_input, seq, slice(0, 256), weight[...], bias[...])
        active = mixture * jax.nn.sigmoid(mixture)
        bc_ref[seq] = active
        writes, readout = active[:, :STATE], active[:, STATE:]
        bt_ref[seq] = writes.T.astype(BF16)
        scores = dot_last(readout, writes, HIGHEST)
        scores_ref[seq] = scores
        scores_t_ref[seq] = scores.T
        along = jnp.sum(readout * direction[...], axis=1, keepdims=True)
        raw = conv_input[seq, EDGE : EDGE + 256, 256:384] + small[0:1]
        raw = jnp.where(lane < HEADS, raw, 0.0)
        step = jnp.maximum(raw, 0.0) + jnp.log1p(jnp.exp(-jnp.abs(raw)))
        log_decay = -jnp.exp(small[1:2]) * step
        running = jnp.dot(lower, log_decay, preferred_element_type=F32, precision=HIGHEST)
        step_ref[seq] = step
        sum_ref[seq] = jnp.where(lane == HEADS, along, running)
        for quarter in range(QUARTERS):
            shift = (TILE - Q_HEADS * quarter) % TILE
            step_q = pltpu.roll(step, shift, 1) if shift else step
            sum_q = pltpu.roll(running, shift, 1) if shift else running
            step_q_ref[quarter, seq] = step_q[:, :SIDE]
            sum_q_ref[quarter, seq] = jnp.where(lane == Q_HEADS, along, sum_q)[:, :SIDE]
            sum_t_ref[quarter, seq] = sum_q.T[:EDGE]


def state_kernel(
    member, conv_input, weight, bias, step_q, sum_q, bt_ref, column, x_ref, payload_ref
):
    for seq in range(2):
        running = sum_q[0, seq]
        last = running[255:256]
        scale = step_q[0, seq] * jnp.exp(last - running)
        whole = jnp.exp(last)
        for tile in range(Q_TILES):
            lanes = slice(TILE * tile, TILE * tile + TILE)
            mixture = mixture_of(conv_input, seq, lanes, weight[:, lanes], bias[:, lanes])
            x = mixture * jax.nn.sigmoid(mixture)
            x_ref[seq, :, lanes] = x
            added = dot(bt_ref[seq], (x * pick(scale, tile)).astype(BF16))
            along = jnp.sum(added * column[...], axis=0, keepdims=True)
            payload_ref[0, seq, :STATE, lanes] = (added - column[...] * along).astype(BF16)
            payload_ref[0, seq, STATE:, lanes] = edge_rows(pick(whole, tile), along)


def intra_kernel(x_ref, step_q, sum_q, sum_t, scores, skip, *refs):
    y_ref = refs[-1]
    row = lax.broadcasted_iota(jnp.int32, (SUB, SUB), 0)
    col = lax.broadcasted_iota(jnp.int32, (SUB, SUB), 1)
    causal = row >= col
    low = low_lanes()
    for seq in range(2):
        step, running = step_q[0, seq], sum_q[0, seq]
        middle = running[SUB - 1 : SUB]
        ahead = jnp.exp(middle - running[:SUB])
        later = jnp.exp(running[SUB:] - middle)
        across = scores[seq, SUB:, :SUB].astype(BF16)
        for tile in range(Q_TILES):
            lanes = slice(TILE * tile, TILE * tile + TILE)
            x = x_ref[seq, :, lanes]
            scaled = x * pick(step, tile)
            low_part = jnp.where(low, scaled, 0.0).astype(BF16)
            high_part = jnp.where(low, 0.0, scaled).astype(BF16)
            for part in range(2):
                rows = slice(SUB * part, SUB * part + SUB)
                weights = []
                for h in (2 * tile, 2 * tile + 1):
                    spread = running[rows, h : h + 1] - sum_t[0, seq, h : h + 1, rows]
                    decayed = jnp.exp(jnp.where(causal, spread, FAR))
                    weights.append((decayed * scores[seq, rows, rows]).astype(BF16))
                inside = dot(
                    jnp.concatenate(weights, 1),
                    jnp.concatenate([low_part[rows], high_part[rows]], 0),
                )
                if part:
                    earlier = (scaled[:SUB] * pick(ahead, tile)).astype(BF16)
                    inside = inside + pick(later, tile) * dot(across, earlier)
                y_ref[seq, rows, lanes] = inside + skip[:, lanes] * x[rows]


def gate_kernel(
    member,
    y_ref,
    z_ref,
    grad_ref,
    bc_ref,
    sum_ref,
    entering,
    along,
    gain,
    out_ref,
    grad_z_ref,
    grad_scan_ref,
    payload_ref,
    gain_grad_ref,
    scanned_ref,
    gated_ref,
    gate_ref,
    spread,
    state_ref,
):
    step = pl.program_id(0)
    per_seq = pl.num_programs(0) // 2
    running = sum_ref[0]
    start = jnp.exp(running)
    read_along = running[:, HEADS : HEADS + 1]
    readout = bc_ref[0, :, STATE:].astype(BF16)
    scanned_ref[...] = dot(readout, entering[0])
    squares = jnp.zeros((ROWS, TILE), F32)
    overlap = jnp.zeros((ROWS, TILE), F32)
    for tile in range(INNER // TILE):
        lanes = slice(TILE * tile, TILE * tile + TILE)
        carried = scanned_ref[:, lanes] + read_along * along[0, 0:1, lanes]
        scanned = y_ref[0, :, lanes] + pick(start, tile) * carried
        scanned_ref[:, lanes] = scanned
        z = z_ref[0, :, lanes]
        gate = jax.nn.sigmoid(z)
        gate_ref[:, lanes] = gate
        gated = scanned * (z * gate)
        gated_ref[:, lanes] = gated
        squares = squares + gated * gated
        overlap = overlap + gated * (grad_ref[0, :, lanes] * gain[:, lanes])
    mean = jnp.sum(squares, axis=1, keepdims=True) / INNER
    inverse = lax.rsqrt(mean + EPSILON)
    back = jnp.sum(overlap, axis=1, keepdims=True) / INNER * inverse * inverse * inverse

    @pl.when(step == 0)
    def _():
        gain_grad_ref[...] = jnp.zeros_like(gain_grad_ref)

    for tile in range(INNER // TILE):
        lanes = slice(TILE * tile, TILE * tile + TILE)
        gated = gated_ref[:, lanes]
        grad = grad_ref[0, :, lanes]
        scaled = gated * inverse
        out_ref[0, :, lanes] = (scaled * gain[:, lanes]).astype(BF16)
        gain_grad_ref[:, lanes] += jnp.sum(grad * scaled, axis=0, keepdims=True)
        grad_gated = inverse * (grad * gain[:, lanes]) - gated * back
        z = z_ref[0, :, lanes]
        gate = gate_ref[:, lanes]
        grad_scan = grad_gated * (z * gate)
        grad_z_ref[0, :, lanes] = (
            grad_gated * scanned_ref[:, lanes] * (gate * (1.0 + z * (1.0 - gate)))
        ).astype(BF16)
        grad_scan_ref[0, :, lanes] = grad_scan
        rounded = grad_scan.astype(BF16).astype(F32)
        spread[:, lanes] = (rounded * pick(start, tile)).astype(BF16)
    added = dot_first(readout, spread[...])

    @pl.when(step % per_seq == 0)
    def _():
        state_ref[...] = added

    @pl.when(step % per_seq != 0)
    def _():
        state_ref[...] += added

    @pl.when(step % per_seq == per_seq - 1)
    def _():
        seq = step // per_seq
        whole = start[ROWS - 1 : ROWS]
        zero = jnp.zeros((1, TILE), F32)
        for tile in range(INNER // TILE):
            lanes = slice(TILE * tile, TILE * tile + TILE)
            place = slice(TILE * (tile % Q_TILES), TILE * (tile % Q_TILES) + TILE)
            slot = member[0] ^ (tile // Q_TILES)
            payload_ref[slot, seq, :STATE, place] = state_ref[:, lanes].astype(BF16)
            payload_ref[slot, seq, STATE:, place] = edge_rows(pick(whole, tile), zero)


def intra_back_kernel(
    x_ref,
    grad_ref,
    y_ref,
    conv_input,
    weight,
    bias,
    step_q,
    sum_q,
    sum_t,
    scores_t,
    bc_ref,
    entering,
    along,
    skip,
    direction,
    *refs,
):
    known_ref, slope_ref, grad_scores_ref, heads_ref, grad_read_ref, product, spread = refs[-7:]
    row = lax.broadcasted_iota(jnp.int32, (SUB, SUB), 0)
    col = lax.broadcasted_iota(jnp.int32, (SUB, SUB), 1)
    causal = row <= col
    low = low_lanes()

    @pl.when(pl.program_id(0) == 0)
    def _():
        grad_scores_ref[...] = jnp.zeros_like(grad_scores_ref)
        grad_read_ref[...] = jnp.zeros_like(grad_read_ref)

    for seq in range(2):
        step, running = step_q[0, seq], sum_q[0, seq]
        middle = running[SUB - 1 : SUB]
        start = jnp.exp(running)
        read_along = running[:, Q_HEADS : Q_HEADS + 1]
        ahead = jnp.exp(middle - running[:SUB])
        later = jnp.exp(running[SUB:] - middle)
        across = scores_t[seq, :SUB, SUB:].astype(BF16)
        readout = bc_ref[seq, :, STATE:].astype(BF16)
        inner = [jnp.zeros((SUB, SUB), F32) for _ in range(2)]
        outer = jnp.zeros((SUB, SUB), F32)
        meeting = jnp.zeros((256, TILE), F32)
        for tile in range(Q_TILES):
            lanes = slice(TILE * tile, TILE * tile + TILE)
            x = x_ref[seq, :, lanes]
            size = pick(step, tile)
            scaled = x * size
            grad = grad_ref[seq, :, lanes]
            begin = pick(start, tile)
            low_grad = jnp.where(low, grad, 0.0).astype(BF16)
            high_grad = jnp.where(low, 0.0, grad).astype(BF16)
            rounded = grad.astype(BF16)
            line = along[seq, 0:1, lanes]
            carried = dot(readout, entering[seq, :, lanes]) + read_along * line
            through = skip[:, lanes] * x
            product[2, :, lanes] = rounded.astype(F32) * (
                y_ref[seq, :, lanes] + begin * carried - through
            )
            widened = grad * begin
            meeting = meeting + widened * line
            spread[:, lanes] = widened.astype(BF16)
            mixture = mixture_of(conv_input, seq, lanes, weight[:, lanes], bias[:, lanes])
            slope = silu_slope(mixture)
            slope_ref[seq, :, lanes] = slope.astype(BF16)
            sides = (
                jnp.where(low, scaled, 0.0).astype(BF16),
                jnp.where(low, 0.0, scaled).astype(BF16),
            )
            for part in range(2):
                rows = slice(SUB * part, SUB * part + SUB)
                weights = []
                for side in range(2):
                    h = 2 * tile + side
                    apart = sum_t[0, seq, h : h + 1, rows] - running[rows, h : h + 1]
                    decayed = jnp.exp(jnp.where(causal, apart, FAR))
                    weights.append((decayed * scores_t[seq, rows, rows]).astype(BF16))
                    inner[part] = inner[part] + decayed * dot_last(
                        sides[side][rows], rounded[rows]
                    )
                inside = dot(
                    jnp.concatenate(weights, 1),
                    jnp.concatenate([low_grad[rows], high_grad[rows]], 0),
                )
                if not part:
                    beyond = (rounded[SUB:].astype(F32) * pick(later, tile)).astype(BF16)
                    factor = pick(ahead, tile)
                    inside = inside + factor * dot(across, beyond)
                    outer = outer + dot_last((scaled[:SUB] * factor).astype(BF16), beyond)
                product[0, rows, lanes] = scaled[rows].astype(BF16).astype(F32) * inside
                product[1, rows, lanes] = x[rows] * inside
                known_ref[seq, rows, lanes] = (
                    size[rows] * inside + skip[:, lanes] * grad[rows]
                ) * slope[rows]
        grad_scores_ref[seq, :SUB, :SUB] += inner[0]
        grad_scores_ref[seq, SUB:, SUB:] += inner[1]
        grad_scores_ref[seq, :SUB, SUB:] += outer
        total = jnp.zeros((256, TILE), F32)
        for kind in range(3):
            total = total + head_sums(product[kind], head_columns(Q_LANES, TILE, Q_HEADS * kind))
        heads_ref[0, seq] = total
        grad_read_ref[seq] += (
            dot_last(spread[...], entering[seq])
            + jnp.sum(meeting, axis=1, keepdims=True) * direction[...]
        )


def channel_kernel(
    known_ref,
    slope_ref,
    x_ref,
    weight,
    step_q,
    sum_q,
    bc_ref,
    leaving,
    entering,
    along,
    column,
    grad_conv_ref,
    tail_ref,
    halo_ref,
    grad_mix_ref,
    heads_ref,
    grad_writes_ref,
    meeting_ref,
    padded,
    product,
    spread,
):
    zeros = jnp.zeros((EDGE, TILE), F32)
    padded[:EDGE] = zeros
    padded[EDGE + 256 :] = zeros
    meeting_ref[...] = jnp.zeros_like(meeting_ref)

    @pl.when(pl.program_id(0) == 0)
    def _():
        grad_writes_ref[...] = jnp.zeros_like(grad_writes_ref)

    for seq in range(2):
        running = sum_q[0, seq]
        remain = jnp.exp(running[255:256] - running)
        scale = step_q[0, seq] * remain
        writes = bc_ref[seq, :, :STATE].astype(BF16)
        for tile in range(Q_TILES):
            lanes = slice(TILE * tile, TILE * tile + TILE)
            taps = weight[:, lanes]
            x = x_ref[seq, :, lanes]
            back = leaving[seq, :, lanes]
            shared = dot(writes, back)
            left = pick(remain, tile)
            product[:, lanes] = x * (left * shared)
            factor = pick(scale, tile)
            spread[:, lanes] = (x * factor).astype(BF16)
            slope = slope_ref[seq, :, lanes].astype(F32)
            grad_mix = known_ref[seq, :, lanes] + factor * slope * shared
            grad_mix_ref[seq, :, lanes] = grad_mix.astype(BF16)
            padded[EDGE : EDGE + 256] = grad_mix
            grad_conv = taps[0:1] * padded[3 : 3 + EDGE + 256]
            for tap in range(1, CONV):
                grad_conv = (
                    grad_conv + taps[tap : tap + 1] * padded[3 - tap : 3 - tap + EDGE + 256]
                )
            halo_ref[seq, :, lanes] = grad_conv[:EDGE].astype(BF16)
            grad_conv_ref[seq, :, lanes] = grad_conv[EDGE:].astype(BF16)
            tail_ref[seq, :, lanes] = grad_conv[256:]
            state = entering[seq, :, lanes].astype(F32) + column[...] * along[seq, 0:1, lanes]
            meeting_ref[seq : seq + 1, lanes] = jnp.sum(
                state * back.astype(F32), axis=0, keepdims=True
            )
        heads_ref[0, seq] = head_sums(product[...], head_columns(Q_LANES, TILE, 0))
        grad_writes_ref[seq] += dot_last(spread[...], leaving[seq])


def sums_kernel(conv_input, grad_mix_ref, grad_ref, x_ref, sums_ref):
    sums_ref[...] = jnp.zeros_like(sums_ref)
    for seq in range(2):
        for tile in range(Q_TILES):
            lanes = slice(TILE * tile, TILE * tile + TILE)
            grad_mix = grad_mix_ref[seq, :, lanes].astype(F32)
            for tap in range(CONV):
                begin = EDGE - CONV + 1 + tap
                sums_ref[tap : tap + 1, lanes] += jnp.sum(
                    grad_mix * conv_input[seq, begin : begin + 256, lanes], axis=0, keepdims=True
                )
            sums_ref[4:5, lanes] += jnp.sum(grad_mix, axis=0, keepdims=True)
            sums_ref[5:6, lanes] += jnp.sum(
                grad_ref[seq, :, lanes] * x_ref[seq, :, lanes], axis=0, keepdims=True
            )


def last_kernel(
    conv_input,
    weight,
    bias,
    small,
    bc_ref,
    grad_scores_0,
    grad_scores_1,
    grad_writes,
    grad_read_0,
    grad_read_1,
    known_heads,
    heads,
    meeting,
    step_ref,
    sum_ref,
    grad_conv_ref,
    tail_ref,
    halo_ref,
    sums_ref,
    small_ref,
    padded,
):
    row = lax.broadcasted_iota(jnp.int32, (256, 256), 0)
    col = lax.broadcasted_iota(jnp.int32, (256, 256), 1)
    upper = (row <= col).astype(F32)
    lane = lax.broadcasted_iota(jnp.int32, (1, TILE), 1)
    line = lax.broadcasted_iota(jnp.int32, (256, 1), 0)
    padded[:EDGE] = jnp.zeros((EDGE, 256), F32)
    padded[EDGE + 256 :] = jnp.zeros((EDGE, 256), F32)
    sums_ref[...] = jnp.zeros_like(sums_ref)
    small_ref[...] = jnp.zeros_like(small_ref)
    rate = jnp.exp(small[1:2])
    met_states = head_sums(meeting[...], head_columns(INNER, TILE, 0))
    taps = weight[...]

    def gather(source, seq, kind):
        total = jnp.zeros((256, TILE), F32)
        for quarter in range(QUARTERS):
            value = source[quarter, seq]
            shift = (Q_HEADS * (quarter - kind)) % TILE
            if shift:
                value = pltpu.roll(value, shift, 1)
            first = Q_HEADS * quarter
            total = total + jnp.where((lane >= first) & (lane < first + Q_HEADS), value, 0.0)
        return total

    for seq in range(2):
        step = step_ref[seq]
        by_state = gather(heads, seq, 0)
        at_state = step * by_state
        running = sum_ref[seq]
        last = jnp.where(lane < HEADS, running[255:256], 0.0)
        end = jnp.exp(last) * met_states[seq : seq + 1] + jnp.sum(
            at_state, axis=0, keepdims=True
        )
        grad_sum = (
            gather(known_heads, seq, 2)
            - gather(known_heads, seq, 0)
            - at_state
            + jnp.where(line == 255, end, 0.0)
        )
        grad_log = jnp.dot(upper, grad_sum, preferred_element_type=F32, precision=HIGHEST)
        small_ref[1:2] += jnp.sum(-rate * step * grad_log, axis=0, keepdims=True)
        raw = conv_input[seq, EDGE : EDGE + 256, 256:384] + small[0:1]
        raw = jnp.where(lane < HEADS, raw, 0.0)
        grad_step = gather(known_heads, seq, 1) + by_state - rate * grad_log
        grad_raw = grad_step * jax.nn.sigmoid(raw)
        small_ref[0:1] += jnp.sum(grad_raw, axis=0, keepdims=True)
        grad_conv_ref[seq, :, 256:] = grad_raw[:, :HEADS].astype(BF16)
        writes, readout = bc_ref[seq, :, :STATE], bc_ref[seq, :, STATE:]
        grad_scores = grad_scores_0[seq] + grad_scores_1[seq]
        into_writes = (
            jnp.dot(grad_scores, readout, preferred_element_type=F32, precision=HIGHEST)
            + grad_writes[seq]
        )
        into_read = dot_first(grad_scores, writes, HIGHEST) + grad_read_0[seq] + grad_read_1[seq]
        mixture = mixture_of(conv_input, seq, slice(0, 256), taps, bias[...])
        grad_mix = jnp.concatenate([into_writes, into_read], 1) * silu_slope(mixture)
        padded[EDGE : EDGE + 256] = grad_mix
        grad_conv = taps[0:1] * padded[3 : 3 + EDGE + 256]
        for tap in range(1, CONV):
            grad_conv = grad_conv + taps[tap : tap + 1] * padded[3 - tap : 3 - tap + EDGE + 256]
        halo_ref[seq] = grad_conv[:EDGE].astype(BF16)
        grad_conv_ref[seq, :, :256] = grad_conv[EDGE:].astype(BF16)
        tail_ref[seq] = grad_conv[256:]
        for tap in range(CONV):
            begin = EDGE - CONV + 1 + tap
            sums_ref[tap : tap + 1] += jnp.sum(
                grad_mix * conv_input[seq, begin : begin + 256, :256], axis=0, keepdims=True
            )
        sums_ref[4:5] += jnp.sum(grad_mix, axis=0, keepdims=True)


def shape(dims, dtype=F32):
    return jax.ShapeDtypeStruct(dims, dtype)


def whole_block(dims):
    return pl.BlockSpec(dims, lambda *g: (0,) * len(dims))


def lane_block(dims, width=Q_LANES):
    return pl.BlockSpec(dims + (width,), lambda g: (0,) * len(dims) + (g,))


def quarter_block(dims):
    return pl.BlockSpec((1,) + dims, lambda g, *_: (g,) + (0,) * len(dims))


def own_lanes(dims):
    return pl.BlockSpec(
        dims + (Q_LANES,), lambda g, member: (0,) * len(dims) + (g ^ member[0],)
    )


def own_quarter(dims):
    return pl.BlockSpec((1,) + dims, lambda g, member: (g ^ member[0],) + (0,) * len(dims))


def fixed_block(dims, index):
    return pl.BlockSpec(dims, lambda g: index)


def row_block(width, length=256):
    steps = length // ROWS
    return pl.BlockSpec((1, ROWS, width), lambda g: (g // steps, g % steps, 0))


SCALAR = pl.BlockSpec(memory_space=pltpu.SMEM)
MESSAGE = (2, PAYLOAD, Q_LANES)


def tie(value, *others):
    return lax.optimization_barrier((value,) + others)[0]


def exchange(payload, member, axis, reverse, stages):
    count = lax.axis_size(axis)
    stages = iter(stages)

    def swap(value, by):
        return lax.ppermute(value, axis, [(i, i ^ by) for i in range(count)])

    def meanwhile(sent, arrived):
        work = next(stages, None)
        return tie(arrived, *work(sent)) if work else arrived

    message = shape(MESSAGE, BF16)
    block = whole_block(MESSAGE)
    members = [payload[0]] + [swap(payload[by], by) for by in range(1, QUARTERS)]
    members[-1] = meanwhile(payload, members[-1])
    total = pl.pallas_call(
        functools.partial(plane_kernel, reverse),
        grid=(1,),
        in_specs=[SCALAR] + [block] * QUARTERS,
        out_specs=block,
        out_shape=message,
        compiler_params=params(),
        cost_estimate=cost(2),
        name="plane",
    )(member, *members)
    received = []
    inclusive = total
    span = 1
    while span < count // QUARTERS:
        shift = -QUARTERS * span if reverse else QUARTERS * span
        pairs = [(i, i + shift) for i in range(count) if 0 <= i + shift < count]
        arrived = lax.ppermute(inclusive, axis, pairs)
        received.append(meanwhile(inclusive, arrived) if span < 4 else arrived)
        span *= 2
        if span < count // QUARTERS:
            inclusive = pl.pallas_call(
                link_kernel,
                grid=(1,),
                in_specs=[block] * (1 + len(received)),
                out_specs=block,
                out_shape=message,
                compiler_params=params(),
                cost_estimate=cost(1.5),
                name="link",
            )(total, *received)
    results = pl.pallas_call(
        functools.partial(spread_kernel, reverse),
        grid=(1,),
        in_specs=[SCALAR] + [block] * (QUARTERS + len(received)),
        out_specs=[block] * QUARTERS,
        out_shape=[message] * QUARTERS,
        compiler_params=params(),
        cost_estimate=cost(3),
        name="spread",
    )(member, *members, *received)
    back = [results[0]] + [swap(results[by], by) for by in range(1, QUARTERS)]
    back[-1] = meanwhile(results[-1], back[-1])
    return pl.pallas_call(
        arrange_kernel,
        grid_spec=pltpu.PrefetchScalarGridSpec(
            num_scalar_prefetch=1,
            grid=(QUARTERS,),
            in_specs=[block] * QUARTERS,
            out_specs=[own_lanes((2, STATE)), own_lanes((2, 8))],
        ),
        out_shape=[shape((2, STATE, INNER), BF16), shape((2, 8, INNER))],
        compiler_params=params(),
        cost_estimate=cost(1.5),
        name="arrange",
    )(member, *back)


class Scatter:
    def __init__(self, arrays, axis):
        self.axis = axis
        self.count = lax.axis_size(axis)
        self.place = lax.axis_index(axis)
        self.bits = list(range(self.count.bit_length() - 1))[::-1]
        self.values = [
            a.reshape((2,) * len(self.bits) + (a.shape[0] // self.count, a.shape[1]))
            for a in arrays
        ]

    def wait_for(self, *others):
        self.values = list(lax.optimization_barrier(tuple(self.values) + others))[
            : len(self.values)
        ]

    def send(self, bit):
        position = self.bits.index(bit)
        mine = (self.place >> bit) & 1
        away = [lax.dynamic_index_in_dim(v, 1 - mine, position, False) for v in self.values]
        away = jnp.concatenate([v.astype(BF16) for v in away], axis=-2)
        self.values = [lax.dynamic_index_in_dim(v, mine, position, False) for v in self.values]
        self.bits.remove(bit)
        self.away = away
        self.sent = lax.ppermute(
            away, self.axis, [(i, i ^ (1 << bit)) for i in range(self.count)]
        )

    def add(self):
        begin = 0
        for i, value in enumerate(self.values):
            end = begin + value.shape[-2]
            self.values[i] = value + self.sent[..., begin:end, :].astype(F32)
            begin = end


def add_up(value, axes):
    for axis in axes:
        count = lax.axis_size(axis)
        for bit in range(count.bit_length() - 1):
            value = value + lax.ppermute(value, axis, [(i, i ^ (1 << bit)) for i in range(count)])
    return value


def finish_kernel(gate_rows, last_rows, out_rows, in_grad, out_grad):
    step = pl.program_id(0)
    length, columns = gate_rows.shape[0] * gate_rows.shape[1], gate_rows.shape[2]

    @pl.when(step < 2 * INNER // length)
    def _():
        in_grad[...] = gate_rows[...].reshape(length, columns).astype(F32)

    @pl.when(step == 2 * INNER // length)
    def _():
        rows = last_rows.shape[0] * last_rows.shape[1]
        keep = min(rows, in_grad.shape[0])
        in_grad[:keep] = last_rows[...].reshape(rows, columns)[:keep].astype(F32)

    @pl.when(step < INNER // length)
    def _():
        group, per = out_rows.shape[0], out_rows.shape[1] // 2
        for side in range(2):
            out_grad[:, columns * side : columns * side + columns] = (
                out_rows[:, per * side : per * side + per].reshape(group * per, columns).astype(F32)
            )


def local(
    hidden_in,
    norm_gain,
    in_weight,
    conv_weight,
    conv_bias,
    step_bias,
    decay_log,
    skip_gain,
    gate_gain,
    out_weight,
    cotangent,
):
    hidden = hidden_in[0]
    upstream = cotangent[0]
    tokens, width = hidden.shape
    half = tokens // 2
    share = in_weight.shape[0]
    count = lax.axis_size("seq")
    core = lax.axis_index("fsdp")
    other = [(0, 1), (1, 0)]

    rows_of = in_weight.T
    conv_rows = lax.optimization_barrier(rows_of[INNER:])
    conv_rows_other = lax.ppermute(conv_rows, "fsdp", other)

    paired = hidden.reshape(2, half, width)
    halo = lax.ppermute(
        tie(paired[:, half - EDGE :], conv_rows), "seq", [(i, i + 1) for i in range(count - 1)]
    )
    extended = jnp.concatenate([halo, paired], axis=1).reshape(2 * (half + EDGE), width)
    rows = extended.astype(F32)
    rescale = lax.rsqrt(jnp.mean(rows * rows, axis=-1, keepdims=True) + EPSILON)
    normed_ext = (rows * rescale * norm_gain).astype(BF16)

    rows_of_writes = rows_of[2 * INNER : 2 * INNER + STATE].astype(F32)
    power = 2.0 * jnp.sum(rows_of_writes * rows_of_writes, axis=1)
    deviation = jnp.sqrt(
        power * jnp.sum(jnp.square(conv_weight[:, INNER : INNER + STATE]), axis=0)
    )
    guess = jnp.zeros((STATE,), F32)
    for point, share_of in ((-1.7320508, 1 / 6), (0.0, 2 / 3), (1.7320508, 1 / 6)):
        guess = guess + share_of * jax.nn.silu(
            conv_bias[INNER : INNER + STATE] + point * deviation
        )
    direction = guess * lax.rsqrt(jnp.sum(guess * guess) + 1e-20)
    row_direction, column_direction = direction[None], direction[:, None]
    member = (lax.axis_index("seq") % QUARTERS).astype(jnp.int32).reshape(1)

    def mine(array, axis):
        first = lax.slice_in_dim(array, 0, share, axis=axis)
        second = lax.slice_in_dim(array, share, 2 * share, axis=axis)
        return (
            jnp.where(core == 0, first, second),
            jnp.where(core == 0, second, first),
        )

    def ordered(own, foreign, axis):
        return jnp.where(
            core == 0,
            jnp.concatenate([own, foreign], axis),
            jnp.concatenate([foreign, own], axis),
        )

    own_ext, other_ext = mine(normed_ext, 1)
    normed = normed_ext.reshape(2, half + EDGE, width)[:, EDGE:].reshape(tokens, width)
    own_normed, other_normed = mine(normed, 1)

    small = jnp.pad(jnp.stack([step_bias, decay_log, skip_gain]), ((0, 5), (0, TILE - HEADS)))
    bias_row = conv_bias[None]
    gain_row = gate_gain[None]
    skip_row = jnp.repeat(skip_gain, HEAD_DIM)[None]

    own_ext = tie(own_ext, conv_rows_other, row_direction, column_direction, small, bias_row)
    conv_input = (dot_last(own_ext, conv_rows) + dot_last(other_ext, conv_rows_other)).reshape(
        2, half + EDGE, CONV_CH + HEADS
    )

    last_columns = fixed_block((2, half + EDGE, 384), (0, 0, INNER // 384))
    last_taps = fixed_block((CONV, 256), (0, INNER // 256))
    last_bias = fixed_block((1, 256), (0, INNER // 256))
    per_quarter = (QUARTERS, 2, half, SIDE)
    bc, bt, scores, scores_t, step, running, step_q, sum_q, sum_t = pl.pallas_call(
        step_kernel,
        grid=(1,),
        in_specs=[
            last_columns,
            last_taps,
            last_bias,
            whole_block((8, TILE)),
            whole_block((1, STATE)),
        ],
        out_specs=[
            whole_block((2, half, 256)),
            whole_block((2, STATE, half)),
            whole_block((2, half, half)),
            whole_block((2, half, half)),
            whole_block((2, half, TILE)),
            whole_block((2, half, TILE)),
            whole_block(per_quarter),
            whole_block(per_quarter),
            whole_block((QUARTERS, 2, EDGE, half)),
        ],
        out_shape=[
            shape((2, half, 256)),
            shape((2, STATE, half), BF16),
            shape((2, half, half)),
            shape((2, half, half)),
            shape((2, half, TILE)),
            shape((2, half, TILE)),
            shape(per_quarter),
            shape(per_quarter),
            shape((QUARTERS, 2, EDGE, half)),
        ],
        compiler_params=params(),
        cost_estimate=cost(4),
        name="steps",
    )(conv_input, conv_weight, bias_row, small, row_direction)

    columns = lane_block((2, half + EDGE))
    taps_block = lane_block((CONV,))
    row_of = lane_block((1,))
    heads_block = quarter_block((2, half, SIDE))
    line_block = quarter_block((2, EDGE, half))
    tokens_block = lane_block((2, half))
    x, payload = pl.pallas_call(
        state_kernel,
        grid_spec=pltpu.PrefetchScalarGridSpec(
            num_scalar_prefetch=1,
            grid=(QUARTERS,),
            in_specs=[
                own_lanes((2, half + EDGE)),
                own_lanes((CONV,)),
                own_lanes((1,)),
                own_quarter((2, half, SIDE)),
                own_quarter((2, half, SIDE)),
                whole_block((2, STATE, half)),
                whole_block((STATE, 1)),
            ],
            out_specs=[own_lanes((2, half)), quarter_block(MESSAGE)],
        ),
        out_shape=[shape((2, half, INNER)), shape((QUARTERS,) + MESSAGE, BF16)],
        compiler_params=params(),
        cost_estimate=cost(8),
        name="states",
    )(member, conv_input, conv_weight, bias_row, step_q, sum_q, bt, column_direction)

    gate_rows = rows_of[:INNER]
    out_rows = lax.all_gather(tie(out_weight, payload), "fsdp", axis=0, tiled=True)
    half_grid = QUARTERS // 2

    def later_half(spec, first):
        old = spec.index_map
        return pl.BlockSpec(spec.block_shape, lambda g: old(g + first))

    def shifted(specs, first):
        return [later_half(spec, first) for spec in specs]

    kept = {}

    def while_states_cross(sent):
        kept["gate"] = dot_last(tie(own_normed, sent), gate_rows)
        return inside(0)(sent) + (kept["gate"],)

    def while_first_states(sent):
        kept["rows"] = lax.ppermute(tie(rows_of, sent)[:INNER], "fsdp", other)
        kept["grad"] = dot_last(tie(upstream, sent), out_rows).reshape(2, half, INNER)
        return (kept["grad"],)

    def inside(first):
        def work(sent):
            specs = [
                tokens_block,
                heads_block,
                heads_block,
                line_block,
                whole_block((2, half, half)),
                row_of,
            ]
            inputs = [tie(x, sent), step_q, sum_q, sum_t, scores, skip_row]
            kept["inside"] = pl.pallas_call(
                intra_kernel,
                grid=(half_grid,),
                in_specs=shifted(specs, first)
                + [pl.BlockSpec(memory_space=pl.ANY)] * (first > 0),
                out_specs=later_half(tokens_block, first),
                out_shape=shape((2, half, INNER)),
                input_output_aliases={len(specs): 0} if first else {},
                compiler_params=params(),
                cost_estimate=cost(8),
                name="inside",
            )(*inputs, *([kept["inside"]] if first else []))
            return (kept["inside"],)

        return work

    def while_states_return(sent):
        kept["z"] = (
            kept["gate"] + dot_last(tie(other_normed, sent), kept["rows"])
        ).reshape(2, half, INNER)
        return (kept["z"],)

    entering, along = exchange(
        payload,
        member,
        "seq",
        False,
        [while_states_cross, while_first_states, inside(half_grid), while_states_return],
    )
    gate_rows_other = kept["rows"]
    y_inside, z, grad_normed_out = kept["inside"], kept["z"], kept["grad"]

    token_rows = row_block(INNER)
    steps = half // ROWS
    normed_out, grad_z, grad_scan, back_payload, gate_gain_grad = pl.pallas_call(
        gate_kernel,
        grid=(2 * steps,),
        in_specs=[
            SCALAR,
            token_rows,
            token_rows,
            token_rows,
            row_block(256),
            row_block(TILE),
            pl.BlockSpec((1, STATE, INNER), lambda g: (g // steps, 0, 0)),
            pl.BlockSpec((1, 8, INNER), lambda g: (g // steps, 0, 0)),
            whole_block((1, INNER)),
        ],
        out_specs=[
            token_rows,
            token_rows,
            token_rows,
            whole_block((QUARTERS,) + MESSAGE),
            whole_block((1, INNER)),
        ],
        out_shape=[
            shape((2, half, INNER), BF16),
            shape((2, half, INNER), BF16),
            shape((2, half, INNER)),
            shape((QUARTERS,) + MESSAGE, BF16),
            shape((1, INNER)),
        ],
        scratch_shapes=[
            pltpu.VMEM((ROWS, INNER), F32),
            pltpu.VMEM((ROWS, INNER), F32),
            pltpu.VMEM((ROWS, INNER), F32),
            pltpu.VMEM((ROWS, INNER), BF16),
            pltpu.VMEM((STATE, INNER), F32),
        ],
        compiler_params=params(),
        cost_estimate=cost(14),
        name="gates",
    )(
        member,
        y_inside,
        z,
        grad_normed_out,
        bc,
        running,
        entering,
        along,
        gain_row,
    )

    normed_out = normed_out.reshape(tokens, INNER)
    grad_z = grad_z.reshape(tokens, INNER)
    first_out, second_out = normed_out[:, : INNER // 2], normed_out[:, INNER // 2 :]
    own_out = jnp.where(core == 0, first_out, second_out)
    other_out = jnp.where(core == 0, second_out, first_out)

    def weight_part(own, foreign):
        sent = lax.ppermute(dot_first(*foreign).astype(BF16), "fsdp", other)
        return dot_first(*own) + sent.astype(F32)

    def while_gradients_cross(sent):
        out_part = weight_part((own_out, upstream), (other_out, upstream))
        gate_part = weight_part((grad_z, own_normed), (grad_z, other_normed))
        kept["out"] = Scatter([out_part], "seq")
        kept["gates"] = Scatter([gate_part], "seq")
        return out_part, gate_part

    state_columns = lane_block((2, STATE))
    line_columns = lane_block((2, 8))
    edge_columns = lane_block((2, EDGE))
    back_parts = []

    def inside_back(first):
        def work(sent):
            if not first:
                for part, bit in ((kept["out"], 0), (kept["gates"], 1)):
                    part.wait_for(sent)
                    part.send(bit)
            specs = [
                tokens_block,
                tokens_block,
                tokens_block,
                columns,
                taps_block,
                row_of,
                heads_block,
                heads_block,
                line_block,
                whole_block((2, half, half)),
                whole_block((2, half, 256)),
                state_columns,
                line_columns,
                row_of,
                whole_block((1, STATE)),
            ]
            inputs = [
                x,
                tie(grad_scan, sent),
                y_inside,
                conv_input,
                conv_weight,
                bias_row,
                step_q,
                sum_q,
                sum_t,
                scores_t,
                bc,
                entering,
                along,
                skip_row,
                row_direction,
            ]
            earlier = [back_parts[0][i] for i in (0, 1, 3)] if first else []
            back_parts.append(
                pl.pallas_call(
                    intra_back_kernel,
                    grid=(half_grid,),
                    in_specs=shifted(specs, first)
                    + [pl.BlockSpec(memory_space=pl.ANY)] * len(earlier),
                    out_specs=shifted(
                        [
                            tokens_block,
                            tokens_block,
                            whole_block((2, half, half)),
                            quarter_block((2, half, TILE)),
                            whole_block((2, half, STATE)),
                        ],
                        first,
                    ),
                    out_shape=[
                        shape((2, half, INNER)),
                        shape((2, half, INNER), BF16),
                        shape((2, half, half)),
                        shape((QUARTERS, 2, half, TILE)),
                        shape((2, half, STATE)),
                    ],
                    scratch_shapes=[
                        pltpu.VMEM((3, half, Q_LANES), F32),
                        pltpu.VMEM((half, Q_LANES), BF16),
                    ],
                    input_output_aliases={
                        len(specs) + i: (0, 1, 3)[i] for i in range(len(earlier))
                    },
                    compiler_params=params(),
                    cost_estimate=cost(17),
                    name="inside_back",
                )(*inputs, *earlier)
            )
            return tuple(back_parts[-1])

        return work

    def while_gradients_return(sent):
        for part in (kept["out"], kept["gates"]):
            part.sent = tie(part.sent, sent)
            part.add()
        return kept["out"].values[0], kept["gates"].values[0]

    leaving, _ = exchange(
        back_payload,
        member,
        "seq",
        True,
        [while_gradients_cross, inside_back(0), inside_back(half_grid), while_gradients_return],
    )
    out_part, gate_part = kept["out"], kept["gates"]
    for part, bit in ((out_part, 1), (gate_part, 0)):
        part.wait_for(leaving)
        part.send(bit)
    leaving = tie(leaving, out_part.away, gate_part.away)
    known, slope, _, known_heads, _ = back_parts[1]
    grad_conv, tail, halo_grad, grad_mix, heads, grad_writes, meeting = pl.pallas_call(
        channel_kernel,
        grid=(QUARTERS,),
        in_specs=[
            tokens_block,
            tokens_block,
            tokens_block,
            taps_block,
            heads_block,
            heads_block,
            whole_block((2, half, 256)),
            state_columns,
            state_columns,
            line_columns,
            whole_block((STATE, 1)),
        ],
        out_specs=[
            tokens_block,
            edge_columns,
            edge_columns,
            tokens_block,
            quarter_block((2, half, TILE)),
            whole_block((2, half, STATE)),
            lane_block((8,)),
        ],
        out_shape=[
            shape((2, half, INNER), BF16),
            shape((2, EDGE, INNER)),
            shape((2, EDGE, INNER), BF16),
            shape((2, half, INNER), BF16),
            shape((QUARTERS, 2, half, TILE)),
            shape((2, half, STATE)),
            shape((8, INNER)),
        ],
        scratch_shapes=[
            pltpu.VMEM((half + 2 * EDGE, TILE), F32),
            pltpu.VMEM((half, Q_LANES), F32),
            pltpu.VMEM((half, Q_LANES), BF16),
        ],
        compiler_params=params(),
        cost_estimate=cost(12),
        name="channels",
    )(
        known,
        slope,
        x,
        conv_weight,
        step_q,
        sum_q,
        bc,
        leaving,
        entering,
        along,
        column_direction,
    )

    grad_conv_last, tail_last, halo_last, sums_last, small_grads = pl.pallas_call(
        last_kernel,
        grid=(1,),
        in_specs=[
            last_columns,
            last_taps,
            last_bias,
            whole_block((8, TILE)),
            whole_block((2, half, 256)),
            whole_block((2, half, half)),
            whole_block((2, half, half)),
            whole_block((2, half, STATE)),
            whole_block((2, half, STATE)),
            whole_block((2, half, STATE)),
            whole_block((QUARTERS, 2, half, TILE)),
            whole_block((QUARTERS, 2, half, TILE)),
            whole_block((8, INNER)),
            whole_block((2, half, TILE)),
            whole_block((2, half, TILE)),
        ],
        out_specs=[
            whole_block((2, half, 256 + HEADS)),
            whole_block((2, EDGE, 256)),
            whole_block((2, EDGE, 256)),
            whole_block((8, 256)),
            whole_block((8, TILE)),
        ],
        out_shape=[
            shape((2, half, 256 + HEADS), BF16),
            shape((2, EDGE, 256)),
            shape((2, EDGE, 256), BF16),
            shape((8, 256)),
            shape((8, TILE)),
        ],
        scratch_shapes=[pltpu.VMEM((half + 2 * EDGE, 256), F32)],
        compiler_params=params(),
        cost_estimate=cost(6),
        name="last",
    )(
        conv_input,
        conv_weight,
        bias_row,
        small,
        bc,
        back_parts[0][2],
        back_parts[1][2],
        grad_writes,
        back_parts[0][4],
        back_parts[1][4],
        known_heads,
        heads,
        meeting,
        step,
        running,
    )

    returned = lax.ppermute(
        tie(jnp.concatenate([halo_grad, halo_last], axis=-1), out_part.sent, gate_part.sent),
        "seq",
        [(i, i - 1) for i in range(1, count)],
    )
    fixed_tail = (jnp.concatenate([tail, tail_last], axis=-1) + returned.astype(F32)).astype(BF16)
    body = half - EDGE
    grad_wide = jnp.concatenate([grad_conv[:, :body], fixed_tail[:, :, :INNER]], axis=1)
    grad_wide = grad_wide.reshape(tokens, INNER)
    per = INNER // count
    per_last = -(-(CONV_CH + HEADS - INNER) // (16 * count)) * 16
    spare = per_last * count - (CONV_CH + HEADS - INNER)
    grad_narrow = jnp.concatenate(
        [
            grad_conv_last[:, :body],
            jnp.concatenate([fixed_tail[:, :, INNER:], grad_conv_last[:, body:, 256:]], axis=-1),
        ],
        axis=1,
    ).reshape(tokens, CONV_CH + HEADS - INNER)
    grad_padded = jnp.pad(grad_narrow, ((0, 0), (0, spare)))

    for part in (out_part, gate_part):
        part.add()
    early = gate_part
    out_value = out_part.values[0]
    early.values.append(
        jnp.concatenate([out_value[..., :share], out_value[..., share:]], axis=-2)
    )
    bits = early.bits[::-1]
    early.send(bits[0])

    grad_wide, grad_padded = lax.optimization_barrier((grad_wide, grad_padded, early.away))[:2]
    wide_part = weight_part((grad_wide, own_normed), (grad_wide, other_normed))
    last_part = weight_part((grad_padded, own_normed), (grad_padded, other_normed))
    cut = share // 2
    first_part = Scatter([wide_part[:, :cut], last_part[:, :cut]], "seq")
    second_part = Scatter([wide_part[:, cut:], last_part[:, cut:]], "seq")
    first_part.send(0)
    second_part.send(1)
    early.add()
    for bit in bits[1:]:
        early.send(bit)
        early.add()
    for part, bit in ((first_part, 1), (second_part, 0)):
        part.add()
        part.send(bit)
    for part in (first_part, second_part):
        part.add()
    late = second_part
    late.values = [
        jnp.concatenate(pair, axis=-1) for pair in zip(first_part.values, second_part.values)
    ]
    late.wait_for(*early.values)
    for bit in bits:
        late.send(bit)
        late.add()

    gate_value, out_value = early.values
    shard = jnp.concatenate([gate_value, out_value] + late.values, axis=-2).astype(BF16)
    gathered = lax.all_gather(shard, "seq", axis=0)

    grad_z, grad_wide, grad_narrow, normed_out, grad_mix = lax.optimization_barrier(
        (grad_z, grad_wide, grad_narrow, normed_out, grad_mix, shard)
    )[:5]

    def through_rows(first, second):
        return (
            dot(grad_z, first) + dot(grad_wide, second[:INNER]) + dot(grad_narrow, second[INNER:])
        )

    grad_normed = ordered(
        through_rows(gate_rows, conv_rows), through_rows(gate_rows_other, conv_rows_other), 1
    )
    u = hidden.astype(F32)
    r = lax.rsqrt(jnp.mean(u * u, axis=-1, keepdims=True) + EPSILON)
    norm_gain_grad = jnp.sum(grad_normed * u * r, axis=0)
    through = grad_normed * norm_gain
    input_grad = (
        upstream.astype(F32)
        + r * through
        - u * (r * r * r) * jnp.mean(through * u, axis=-1, keepdims=True)
    ).astype(BF16)
    block_out = (hidden.astype(F32) + dot(normed_out, out_rows)).astype(BF16)

    sums = pl.pallas_call(
        sums_kernel,
        grid=(QUARTERS,),
        in_specs=[columns, tokens_block, tokens_block, tokens_block],
        out_specs=lane_block((8,)),
        out_shape=shape((8, INNER)),
        compiler_params=params(),
        cost_estimate=cost(10),
        name="sums",
    )(conv_input, grad_mix, grad_scan, x)

    skip_grad = jnp.sum(sums[5].reshape(HEADS, HEAD_DIM), axis=1)
    vector = jnp.concatenate(
        [
            norm_gain_grad,
            sums[:5].reshape(-1),
            sums_last[:5].reshape(-1),
            small_grads[:2].reshape(-1),
            gate_gain_grad[0],
            jnp.pad(skip_grad, (0, TILE - HEADS)),
        ]
    )
    length = vector.shape[0]
    vector = add_up(vector.reshape(length // TILE, TILE), ("fsdp", "seq")).reshape(length)
    parts = []
    begin = 0
    for size in (width, 5 * INNER, 5 * 256, 2 * TILE, INNER, HEADS):
        parts.append(vector[begin : begin + size])
        begin += size
    conv_sums = jnp.concatenate(
        [parts[1].reshape(5, INNER), parts[2].reshape(5, 256)], axis=1
    )
    smalls = parts[3].reshape(2, TILE)[:, :HEADS]

    group = share // per
    parts_of = INNER // share
    gathered_block = (group, per, share)
    in_grad, out_grad = pl.pallas_call(
        finish_kernel,
        grid=(2 * parts_of + 1,),
        in_specs=[
            pl.BlockSpec(
                gathered_block,
                lambda g: (jnp.minimum(g, 2 * parts_of - 1) % parts_of, g // parts_of * 2 % 4, 0),
            ),
            pl.BlockSpec((count, per_last, share), lambda g: (0, 3 * per // per_last, 0)),
            pl.BlockSpec(gathered_block, lambda g: (jnp.minimum(g, parts_of - 1), 1, 0)),
        ],
        out_specs=[
            pl.BlockSpec((share, share), lambda g: (g, 0)),
            pl.BlockSpec((share // 2, width), lambda g: (jnp.minimum(g, parts_of - 1), 0)),
        ],
        out_shape=[shape((CONV_CH + HEADS + INNER, share)), shape((2 * share, width))],
        compiler_params=params(),
        cost_estimate=cost(14),
        name="finish",
    )(gathered, gathered, gathered)
    return (
        block_out[None],
        input_grad[None],
        parts[0],
        in_grad.T,
        conv_sums[:4],
        conv_sums[4],
        smalls[0],
        smalls[1],
        parts[5],
        parts[4],
        out_grad,
    )


def solution(mesh):
    return jax.shard_map(
        local,
        mesh=mesh,
        in_specs=(
            P("fsdp", "seq", None),
            P(),
            P("fsdp", None),
            P(),
            P(),
            P(),
            P(),
            P(),
            P(),
            P("fsdp", None),
            P("fsdp", "seq", None),
        ),
        out_specs=(
            P("fsdp", "seq", None),
            P("fsdp", "seq", None),
            P(),
            P("fsdp", None),
            P(),
            P(),
            P(),
            P(),
            P(),
            P(),
            P("fsdp", None),
        ),
        check_vma=False,
    )
```

```python
import functools

import jax
import jax.numpy as jnp
from jax import lax
from jax.experimental import pallas as pl
from jax.experimental.pallas import tpu as pltpu
from jax.sharding import PartitionSpec as P

HEADS = 48
HEAD_DIM = 64
STATE = 128
CONV = 4
INNER = 3072
CONV_CH = 3328
EPSILON = 1e-05

QUARTERS = 4
Q_HEADS = HEADS // QUARTERS
Q_LANES = INNER // QUARTERS
TILE = 128
Q_TILES = Q_LANES // TILE
EDGE = 16
PAYLOAD = STATE + EDGE
ROWS = 128
SIDE = 16
SUB = 128
FAR = -1e30
MIB = 1024 * 1024
HIGHEST = lax.Precision.HIGHEST
F32 = jnp.float32
BF16 = jnp.bfloat16


def params(mebibytes):
    return pltpu.CompilerParams(vmem_limit_bytes=mebibytes * MIB)


def cost(microseconds):
    return pl.CostEstimate(
        flops=0, transcendentals=0, bytes_accessed=int(microseconds * 3_400_000)
    )


def low_lanes():
    return lax.broadcasted_iota(jnp.int32, (1, TILE), 1) < HEAD_DIM


def pick(per_head, tile):
    return jnp.where(
        low_lanes(),
        per_head[:, 2 * tile : 2 * tile + 1],
        per_head[:, 2 * tile + 1 : 2 * tile + 2],
    )


def head_columns(channels, columns, offset):
    row = lax.broadcasted_iota(jnp.int32, (channels, columns), 0)
    col = lax.broadcasted_iota(jnp.int32, (channels, columns), 1) - offset
    return ((row >= HEAD_DIM * col) & (row < HEAD_DIM * col + HEAD_DIM)).astype(BF16)


def head_sums(wide, selector):
    high = wide.astype(BF16)
    rest = (wide - high.astype(F32)).astype(BF16)
    return jnp.dot(high, selector, preferred_element_type=F32) + jnp.dot(
        rest, selector, preferred_element_type=F32
    )


def dot(left, right):
    return jnp.dot(left, right, preferred_element_type=F32)


def dot_last(left, right, precision=None):
    return lax.dot_general(
        left,
        right,
        (((1,), (1,)), ((), ())),
        preferred_element_type=F32,
        precision=precision,
    )


def dot_first(left, right, precision=None):
    return lax.dot_general(
        left,
        right,
        (((0,), (0,)), ((), ())),
        preferred_element_type=F32,
        precision=precision,
    )


def mixture_of(conv_input, seq, lanes, weight, bias):
    total = bias
    for tap in range(CONV):
        start = EDGE - CONV + 1 + tap
        total = total + weight[tap : tap + 1] * conv_input[seq, start : start + 256, lanes]
    return total


def silu_slope(value):
    gate = jax.nn.sigmoid(value)
    return gate * (1.0 + value * (1.0 - gate))


def three_parts(value):
    high = value.astype(BF16).astype(F32)
    middle = (value - high).astype(BF16).astype(F32)
    return high, middle, value - high - middle


def edge_rows(decay, along):
    index = lax.broadcasted_iota(jnp.int32, (EDGE, TILE), 0)
    rows = jnp.zeros((EDGE, TILE), F32)
    for row, part in enumerate(three_parts(decay) + three_parts(along)):
        rows = jnp.where(index == row, part, rows)
    return rows.astype(BF16)


def read_payload(ref, seq, lanes):
    state = ref[seq, :STATE, lanes].astype(F32)
    rows = ref[seq, STATE:, lanes].astype(F32)
    decay = rows[0:1] + rows[1:2] + rows[2:3]
    along = rows[3:4] + rows[4:5] + rows[5:6]
    return state, decay, along


def write_payload(ref, seq, lanes, state, decay, along):
    ref[seq, :STATE, lanes] = state.astype(BF16)
    ref[seq, STATE:, lanes] = edge_rows(decay, along)


def after(first, second):
    return (
        second[0] + second[1] * first[0],
        second[1] * first[1],
        second[2] + second[1] * first[2],
    )


def empty():
    return (
        jnp.zeros((STATE, TILE), F32),
        jnp.ones((1, TILE), F32),
        jnp.zeros((1, TILE), F32),
    )


def parts_of_quarter():
    for seq in range(2):
        for tile in range(Q_TILES):
            yield seq, slice(TILE * tile, TILE * tile + TILE)


def joined(refs, seq, lanes):
    result = read_payload(refs[0], seq, lanes)
    for ref in refs[1:]:
        result = after(read_payload(ref, seq, lanes), result)
    return result


def plane_kernel(reverse, member, *refs):
    members, total = refs[:QUARTERS], refs[QUARTERS]
    order = range(QUARTERS)[::-1] if reverse else range(QUARTERS)
    for place in range(QUARTERS):

        @pl.when(member[0] == place)
        def _(place=place):
            for seq, lanes in parts_of_quarter():
                whole = None
                for which in order:
                    here = read_payload(members[place ^ which], seq, lanes)
                    whole = here if whole is None else after(whole, here)
                write_payload(total, seq, lanes, *whole)


def link_kernel(*refs):
    total, received, result = refs[0], refs[1:-1], refs[-1]
    for seq, lanes in parts_of_quarter():
        whole = after(joined(received, seq, lanes), read_payload(total, seq, lanes))
        write_payload(result, seq, lanes, *whole)


def spread_kernel(reverse, member, *refs):
    members, received, results = refs[:QUARTERS], refs[QUARTERS:-QUARTERS], refs[-QUARTERS:]
    order = list(range(QUARTERS)[::-1] if reverse else range(QUARTERS))
    for place in range(QUARTERS):

        @pl.when(member[0] == place)
        def _(place=place):
            for seq, lanes in parts_of_quarter():
                whole = joined(received, seq, lanes)
                for which in order:
                    write_payload(results[place ^ which], seq, lanes, *whole)
                    if which != order[-1]:
                        whole = after(whole, read_payload(members[place ^ which], seq, lanes))


def arrange_kernel(member, *refs):
    pieces, state_ref, along_ref = refs[:QUARTERS], refs[QUARTERS], refs[QUARTERS + 1]
    for by in range(QUARTERS):

        @pl.when(pl.program_id(0) == by)
        def _(by=by):
            for seq, lanes in parts_of_quarter():
                state_ref[seq, :, lanes] = pieces[by][seq, :STATE, lanes]
                rows = pieces[by][seq, STATE:, lanes].astype(F32)
                along = rows[3:4] + rows[4:5] + rows[5:6]
                along_ref[seq, :, lanes] = jnp.broadcast_to(along, (8, TILE))


def step_kernel(
    conv_input,
    weight,
    bias,
    small,
    direction,
    bc_ref,
    bt_ref,
    scores_ref,
    scores_t_ref,
    step_ref,
    sum_ref,
    step_q_ref,
    sum_q_ref,
    sum_t_ref,
):
    row = lax.broadcasted_iota(jnp.int32, (256, 256), 0)
    col = lax.broadcasted_iota(jnp.int32, (256, 256), 1)
    lower = (row >= col).astype(F32)
    lane = lax.broadcasted_iota(jnp.int32, (1, TILE), 1)
    for seq in range(2):
        mixture = mixture_of(conv_input, seq, slice(0, 256), weight[...], bias[...])
        active = mixture * jax.nn.sigmoid(mixture)
        bc_ref[seq] = active
        writes, readout = active[:, :STATE], active[:, STATE:]
        bt_ref[seq] = writes.T.astype(BF16)
        scores = dot_last(readout, writes, HIGHEST)
        scores_ref[seq] = scores
        scores_t_ref[seq] = scores.T
        along = jnp.sum(readout * direction[...], axis=1, keepdims=True)
        raw = conv_input[seq, EDGE : EDGE + 256, 256:384] + small[0:1]
        raw = jnp.where(lane < HEADS, raw, 0.0)
        step = jnp.maximum(raw, 0.0) + jnp.log1p(jnp.exp(-jnp.abs(raw)))
        log_decay = -jnp.exp(small[1:2]) * step
        running = jnp.dot(lower, log_decay, preferred_element_type=F32, precision=HIGHEST)
        step_ref[seq] = step
        sum_ref[seq] = jnp.where(lane == HEADS, along, running)
        for quarter in range(QUARTERS):
            shift = (TILE - Q_HEADS * quarter) % TILE
            step_q = pltpu.roll(step, shift, 1) if shift else step
            sum_q = pltpu.roll(running, shift, 1) if shift else running
            step_q_ref[quarter, seq] = step_q[:, :SIDE]
            sum_q_ref[quarter, seq] = jnp.where(lane == Q_HEADS, along, sum_q)[:, :SIDE]
            sum_t_ref[quarter, seq] = sum_q.T[:EDGE]


def state_kernel(
    member, conv_input, weight, bias, step_q, sum_q, bt_ref, column, x_ref, payload_ref
):
    for seq in range(2):
        running = sum_q[0, seq]
        last = running[255:256]
        scale = step_q[0, seq] * jnp.exp(last - running)
        whole = jnp.exp(last)
        for tile in range(Q_TILES):
            lanes = slice(TILE * tile, TILE * tile + TILE)
            mixture = mixture_of(conv_input, seq, lanes, weight[:, lanes], bias[:, lanes])
            x = mixture * jax.nn.sigmoid(mixture)
            x_ref[seq, :, lanes] = x
            added = dot(bt_ref[seq], (x * pick(scale, tile)).astype(BF16))
            along = jnp.sum(added * column[...], axis=0, keepdims=True)
            payload_ref[0, seq, :STATE, lanes] = (added - column[...] * along).astype(BF16)
            payload_ref[0, seq, STATE:, lanes] = edge_rows(pick(whole, tile), along)


def intra_kernel(x_ref, step_q, sum_q, sum_t, scores, skip, *refs):
    y_ref = refs[-1]
    row = lax.broadcasted_iota(jnp.int32, (SUB, SUB), 0)
    col = lax.broadcasted_iota(jnp.int32, (SUB, SUB), 1)
    causal = row >= col
    low = low_lanes()
    for seq in range(2):
        step, running = step_q[0, seq], sum_q[0, seq]
        middle = running[SUB - 1 : SUB]
        ahead = jnp.exp(middle - running[:SUB])
        later = jnp.exp(running[SUB:] - middle)
        across = scores[seq, SUB:, :SUB].astype(BF16)
        for tile in range(Q_TILES):
            lanes = slice(TILE * tile, TILE * tile + TILE)
            x = x_ref[seq, :, lanes]
            scaled = x * pick(step, tile)
            low_part = jnp.where(low, scaled, 0.0).astype(BF16)
            high_part = jnp.where(low, 0.0, scaled).astype(BF16)
            for part in range(2):
                rows = slice(SUB * part, SUB * part + SUB)
                weights = []
                for h in (2 * tile, 2 * tile + 1):
                    spread = running[rows, h : h + 1] - sum_t[0, seq, h : h + 1, rows]
                    decayed = jnp.exp(jnp.where(causal, spread, FAR))
                    weights.append((decayed * scores[seq, rows, rows]).astype(BF16))
                inside = dot(
                    jnp.concatenate(weights, 1),
                    jnp.concatenate([low_part[rows], high_part[rows]], 0),
                )
                if part:
                    earlier = (scaled[:SUB] * pick(ahead, tile)).astype(BF16)
                    inside = inside + pick(later, tile) * dot(across, earlier)
                y_ref[seq, rows, lanes] = inside + skip[:, lanes] * x[rows]


def gate_kernel(
    member,
    y_ref,
    z_ref,
    grad_ref,
    bc_ref,
    sum_ref,
    entering,
    along,
    gain,
    out_ref,
    grad_z_ref,
    grad_scan_ref,
    payload_ref,
    gain_grad_ref,
    scanned_ref,
    gated_ref,
    gate_ref,
    start_ref,
    spread,
    state_ref,
):
    step = pl.program_id(0)
    per_seq = pl.num_programs(0) // 2
    running = sum_ref[0]
    start = jnp.exp(running)
    read_along = running[:, HEADS : HEADS + 1]
    readout = bc_ref[0, :, STATE:].astype(BF16)
    readout_t = bc_ref[0, :, STATE:].T.astype(BF16)
    squares = jnp.zeros((ROWS, TILE), F32)
    overlap = jnp.zeros((ROWS, TILE), F32)
    for tile in range(INNER // TILE):
        lanes = slice(TILE * tile, TILE * tile + TILE)
        if tile % 2 == 0:
            wide = dot(readout, entering[0, :, TILE * tile : TILE * tile + 2 * TILE])
        carried = wide[:, TILE * (tile % 2) : TILE * (tile % 2) + TILE]
        carried = carried + read_along * along[0, 0:1, lanes]
        begin = pick(start, tile)
        start_ref[:, lanes] = begin
        scanned = y_ref[0, :, lanes] + begin * carried
        scanned_ref[:, lanes] = scanned
        z = z_ref[0, :, lanes]
        gate = jax.nn.sigmoid(z)
        gate_ref[:, lanes] = gate
        gated = scanned * (z * gate)
        gated_ref[:, lanes] = gated
        squares = squares + gated * gated
        overlap = overlap + gated * (grad_ref[0, :, lanes] * gain[:, lanes])
    mean = jnp.sum(squares, axis=1, keepdims=True) / INNER
    inverse = lax.rsqrt(mean + EPSILON)
    back = jnp.sum(overlap, axis=1, keepdims=True) / INNER * inverse * inverse * inverse

    @pl.when(step == 0)
    def _():
        gain_grad_ref[...] = jnp.zeros_like(gain_grad_ref)

    @pl.when(step % per_seq == 0)
    def _():
        state_ref[...] = jnp.zeros_like(state_ref)

    for tile in range(INNER // TILE):
        lanes = slice(TILE * tile, TILE * tile + TILE)
        gated = gated_ref[:, lanes]
        grad = grad_ref[0, :, lanes]
        scaled = gated * inverse
        out_ref[0, :, lanes] = (scaled * gain[:, lanes]).astype(BF16)
        gain_grad_ref[:, lanes] += jnp.sum(grad * scaled, axis=0, keepdims=True)
        grad_gated = inverse * (grad * gain[:, lanes]) - gated * back
        z = z_ref[0, :, lanes]
        gate = gate_ref[:, lanes]
        grad_scan = grad_gated * (z * gate)
        grad_z_ref[0, :, lanes] = (
            grad_gated * scanned_ref[:, lanes] * (gate * (1.0 + z * (1.0 - gate)))
        ).astype(BF16)
        grad_scan_ref[0, :, lanes] = grad_scan
        spread[:, lanes] = (grad_scan * start_ref[:, lanes]).astype(BF16)
        if tile % 2:
            both = slice(TILE * tile - TILE, TILE * tile + TILE)
            state_ref[:, both] += dot(readout_t, spread[:, both])

    @pl.when(step % per_seq == per_seq - 1)
    def _():
        seq = step // per_seq
        whole = start[ROWS - 1 : ROWS]
        zero = jnp.zeros((1, TILE), F32)
        for tile in range(INNER // TILE):
            lanes = slice(TILE * tile, TILE * tile + TILE)
            place = slice(TILE * (tile % Q_TILES), TILE * (tile % Q_TILES) + TILE)
            slot = member[0] ^ (tile // Q_TILES)
            payload_ref[slot, seq, :STATE, place] = state_ref[:, lanes].astype(BF16)
            payload_ref[slot, seq, STATE:, place] = edge_rows(pick(whole, tile), zero)


def intra_back_kernel(
    x_ref,
    grad_ref,
    y_ref,
    conv_input,
    weight,
    bias,
    step_q,
    sum_q,
    sum_t,
    scores_t,
    bc_ref,
    entering,
    along,
    skip,
    direction,
    *refs,
):
    known_ref, slope_ref, grad_scores_ref, heads_ref, grad_read_ref, product, spread = refs[-7:]
    row = lax.broadcasted_iota(jnp.int32, (SUB, SUB), 0)
    col = lax.broadcasted_iota(jnp.int32, (SUB, SUB), 1)
    causal = row <= col
    low = low_lanes()

    @pl.when(pl.program_id(0) == 0)
    def _():
        grad_scores_ref[...] = jnp.zeros_like(grad_scores_ref)
        grad_read_ref[...] = jnp.zeros_like(grad_read_ref)

    for seq in range(2):
        step, running = step_q[0, seq], sum_q[0, seq]
        middle = running[SUB - 1 : SUB]
        start = jnp.exp(running)
        read_along = running[:, Q_HEADS : Q_HEADS + 1]
        ahead = jnp.exp(middle - running[:SUB])
        later = jnp.exp(running[SUB:] - middle)
        across = scores_t[seq, :SUB, SUB:].astype(BF16)
        readout = bc_ref[seq, :, STATE:].astype(BF16)
        inner = [jnp.zeros((SUB, SUB), F32) for _ in range(2)]
        outer = jnp.zeros((SUB, SUB), F32)
        meeting = jnp.zeros((256, TILE), F32)
        product[2] = dot(readout, entering[seq])
        for tile in range(Q_TILES):
            lanes = slice(TILE * tile, TILE * tile + TILE)
            x = x_ref[seq, :, lanes]
            size = pick(step, tile)
            scaled = x * size
            grad = grad_ref[seq, :, lanes]
            begin = pick(start, tile)
            low_grad = jnp.where(low, grad, 0.0).astype(BF16)
            high_grad = jnp.where(low, 0.0, grad).astype(BF16)
            rounded = grad.astype(BF16)
            line = along[seq, 0:1, lanes]
            carried = product[2, :, lanes] + read_along * line
            through = skip[:, lanes] * x
            product[2, :, lanes] = rounded.astype(F32) * (
                y_ref[seq, :, lanes] + begin * carried - through
            )
            widened = grad * begin
            meeting = meeting + widened * line
            spread[:, lanes] = widened.astype(BF16)
            mixture = mixture_of(conv_input, seq, lanes, weight[:, lanes], bias[:, lanes])
            slope = silu_slope(mixture)
            slope_ref[seq, :, lanes] = slope.astype(BF16)
            sides = (
                jnp.where(low, scaled, 0.0).astype(BF16),
                jnp.where(low, 0.0, scaled).astype(BF16),
            )
            for part in range(2):
                rows = slice(SUB * part, SUB * part + SUB)
                weights = []
                pairs = dot_last(
                    jnp.concatenate([sides[0][rows], sides[1][rows]], 0), rounded[rows]
                )
                for side in range(2):
                    h = 2 * tile + side
                    apart = sum_t[0, seq, h : h + 1, rows] - running[rows, h : h + 1]
                    decayed = jnp.exp(jnp.where(causal, apart, FAR))
                    weights.append((decayed * scores_t[seq, rows, rows]).astype(BF16))
                    inner[part] = inner[part] + decayed * pairs[SUB * side : SUB * side + SUB]
                inside = dot(
                    jnp.concatenate(weights, 1),
                    jnp.concatenate([low_grad[rows], high_grad[rows]], 0),
                )
                if not part:
                    beyond = (rounded[SUB:].astype(F32) * pick(later, tile)).astype(BF16)
                    factor = pick(ahead, tile)
                    inside = inside + factor * dot(across, beyond)
                    outer = outer + dot_last((scaled[:SUB] * factor).astype(BF16), beyond)
                product[0, rows, lanes] = scaled[rows].astype(BF16).astype(F32) * inside
                product[1, rows, lanes] = x[rows] * inside
                known_ref[seq, rows, lanes] = (
                    size[rows] * inside + skip[:, lanes] * grad[rows]
                ) * slope[rows]
        grad_scores_ref[seq, :SUB, :SUB] += inner[0]
        grad_scores_ref[seq, SUB:, SUB:] += inner[1]
        grad_scores_ref[seq, :SUB, SUB:] += outer
        total = jnp.zeros((256, TILE), F32)
        for kind in range(3):
            total = total + head_sums(product[kind], head_columns(Q_LANES, TILE, Q_HEADS * kind))
        heads_ref[0, seq] = total
        grad_read_ref[seq] += (
            dot_last(spread[...], entering[seq])
            + jnp.sum(meeting, axis=1, keepdims=True) * direction[...]
        )


def channel_kernel(
    known_ref,
    slope_ref,
    x_ref,
    weight,
    step_q,
    sum_q,
    bc_ref,
    leaving,
    entering,
    along,
    column,
    grad_conv_ref,
    tail_ref,
    halo_ref,
    grad_mix_ref,
    heads_ref,
    grad_writes_ref,
    meeting_ref,
    padded,
    product,
    spread,
):
    zeros = jnp.zeros((EDGE, TILE), F32)
    padded[:EDGE] = zeros
    padded[EDGE + 256 :] = zeros
    meeting_ref[...] = jnp.zeros_like(meeting_ref)

    @pl.when(pl.program_id(0) == 0)
    def _():
        grad_writes_ref[...] = jnp.zeros_like(grad_writes_ref)

    for seq in range(2):
        running = sum_q[0, seq]
        remain = jnp.exp(running[255:256] - running)
        scale = step_q[0, seq] * remain
        writes = bc_ref[seq, :, :STATE].astype(BF16)
        product[...] = dot(writes, leaving[seq])
        for tile in range(Q_TILES):
            lanes = slice(TILE * tile, TILE * tile + TILE)
            taps = weight[:, lanes]
            x = x_ref[seq, :, lanes]
            back = leaving[seq, :, lanes]
            shared = product[:, lanes]
            product[:, lanes] = x * shared
            factor = pick(scale, tile)
            spread[:, lanes] = (x * factor).astype(BF16)
            slope = slope_ref[seq, :, lanes].astype(F32)
            grad_mix = known_ref[seq, :, lanes] + factor * slope * shared
            grad_mix_ref[seq, :, lanes] = grad_mix.astype(BF16)
            padded[EDGE : EDGE + 256] = grad_mix
            grad_conv = taps[0:1] * padded[3 : 3 + EDGE + 256]
            for tap in range(1, CONV):
                grad_conv = (
                    grad_conv + taps[tap : tap + 1] * padded[3 - tap : 3 - tap + EDGE + 256]
                )
            halo_ref[seq, :, lanes] = grad_conv[:EDGE].astype(BF16)
            grad_conv_ref[seq, :, lanes] = grad_conv[EDGE:].astype(BF16)
            tail_ref[seq, :, lanes] = grad_conv[256:]
            state = entering[seq, :, lanes].astype(F32) + column[...] * along[seq, 0:1, lanes]
            meeting_ref[seq : seq + 1, lanes] = jnp.sum(
                state * back.astype(F32), axis=0, keepdims=True
            )
        total = dot(product[...].astype(BF16), head_columns(Q_LANES, TILE, 0))
        heads_ref[0, seq] = jnp.zeros((256, TILE), F32)
        heads_ref[0, seq, :, :SIDE] = total[:, :SIDE] * remain
        grad_writes_ref[seq] += dot_last(spread[...], leaving[seq])


def sums_kernel(conv_input, grad_mix_ref, grad_ref, x_ref, sums_ref):
    sums_ref[...] = jnp.zeros_like(sums_ref)
    for seq in range(2):
        for tile in range(Q_TILES):
            lanes = slice(TILE * tile, TILE * tile + TILE)
            grad_mix = grad_mix_ref[seq, :, lanes].astype(F32)
            for tap in range(CONV):
                begin = EDGE - CONV + 1 + tap
                sums_ref[tap : tap + 1, lanes] += jnp.sum(
                    grad_mix * conv_input[seq, begin : begin + 256, lanes], axis=0, keepdims=True
                )
            sums_ref[4:5, lanes] += jnp.sum(grad_mix, axis=0, keepdims=True)
            sums_ref[5:6, lanes] += jnp.sum(
                grad_ref[seq, :, lanes] * x_ref[seq, :, lanes], axis=0, keepdims=True
            )


def last_kernel(
    conv_input,
    weight,
    bias,
    small,
    bc_ref,
    grad_scores_0,
    grad_scores_1,
    grad_writes,
    grad_read_0,
    grad_read_1,
    known_heads,
    heads,
    meeting,
    step_ref,
    sum_ref,
    grad_conv_ref,
    tail_ref,
    halo_ref,
    sums_ref,
    small_ref,
    padded,
):
    row = lax.broadcasted_iota(jnp.int32, (256, 256), 0)
    col = lax.broadcasted_iota(jnp.int32, (256, 256), 1)
    upper = (row <= col).astype(F32)
    lane = lax.broadcasted_iota(jnp.int32, (1, TILE), 1)
    line = lax.broadcasted_iota(jnp.int32, (256, 1), 0)
    padded[:EDGE] = jnp.zeros((EDGE, 256), F32)
    padded[EDGE + 256 :] = jnp.zeros((EDGE, 256), F32)
    sums_ref[...] = jnp.zeros_like(sums_ref)
    small_ref[...] = jnp.zeros_like(small_ref)
    rate = jnp.exp(small[1:2])
    met_states = head_sums(meeting[...], head_columns(INNER, TILE, 0))
    taps = weight[...]

    def gather(source, seq, kind):
        total = jnp.zeros((256, TILE), F32)
        for quarter in range(QUARTERS):
            value = source[quarter, seq]
            shift = (Q_HEADS * (quarter - kind)) % TILE
            if shift:
                value = pltpu.roll(value, shift, 1)
            first = Q_HEADS * quarter
            total = total + jnp.where((lane >= first) & (lane < first + Q_HEADS), value, 0.0)
        return total

    for seq in range(2):
        step = step_ref[seq]
        by_state = gather(heads, seq, 0)
        at_state = step * by_state
        running = sum_ref[seq]
        last = jnp.where(lane < HEADS, running[255:256], 0.0)
        end = jnp.exp(last) * met_states[seq : seq + 1] + jnp.sum(
            at_state, axis=0, keepdims=True
        )
        grad_sum = (
            gather(known_heads, seq, 2)
            - gather(known_heads, seq, 0)
            - at_state
            + jnp.where(line == 255, end, 0.0)
        )
        grad_log = jnp.dot(upper, grad_sum, preferred_element_type=F32, precision=HIGHEST)
        small_ref[1:2] += jnp.sum(-rate * step * grad_log, axis=0, keepdims=True)
        raw = conv_input[seq, EDGE : EDGE + 256, 256:384] + small[0:1]
        raw = jnp.where(lane < HEADS, raw, 0.0)
        grad_step = gather(known_heads, seq, 1) + by_state - rate * grad_log
        grad_raw = grad_step * jax.nn.sigmoid(raw)
        small_ref[0:1] += jnp.sum(grad_raw, axis=0, keepdims=True)
        grad_conv_ref[seq, :, 256:] = grad_raw[:, :HEADS].astype(BF16)
        writes, readout = bc_ref[seq, :, :STATE], bc_ref[seq, :, STATE:]
        grad_scores = grad_scores_0[seq] + grad_scores_1[seq]
        into_writes = (
            jnp.dot(grad_scores, readout, preferred_element_type=F32, precision=HIGHEST)
            + grad_writes[seq]
        )
        into_read = dot_first(grad_scores, writes, HIGHEST) + grad_read_0[seq] + grad_read_1[seq]
        mixture = mixture_of(conv_input, seq, slice(0, 256), taps, bias[...])
        grad_mix = jnp.concatenate([into_writes, into_read], 1) * silu_slope(mixture)
        padded[EDGE : EDGE + 256] = grad_mix
        grad_conv = taps[0:1] * padded[3 : 3 + EDGE + 256]
        for tap in range(1, CONV):
            grad_conv = grad_conv + taps[tap : tap + 1] * padded[3 - tap : 3 - tap + EDGE + 256]
        halo_ref[seq] = grad_conv[:EDGE].astype(BF16)
        grad_conv_ref[seq, :, :256] = grad_conv[EDGE:].astype(BF16)
        tail_ref[seq] = grad_conv[256:]
        for tap in range(CONV):
            begin = EDGE - CONV + 1 + tap
            sums_ref[tap : tap + 1] += jnp.sum(
                grad_mix * conv_input[seq, begin : begin + 256, :256], axis=0, keepdims=True
            )
        sums_ref[4:5] += jnp.sum(grad_mix, axis=0, keepdims=True)


def shape(dims, dtype=F32):
    return jax.ShapeDtypeStruct(dims, dtype)


def whole_block(dims):
    return pl.BlockSpec(dims, lambda *g: (0,) * len(dims))


def lane_block(dims, width=Q_LANES):
    return pl.BlockSpec(dims + (width,), lambda g: (0,) * len(dims) + (g,))


def quarter_block(dims):
    return pl.BlockSpec((1,) + dims, lambda g, *_: (g,) + (0,) * len(dims))


def own_lanes(dims):
    return pl.BlockSpec(
        dims + (Q_LANES,), lambda g, member: (0,) * len(dims) + (g ^ member[0],)
    )


def own_quarter(dims):
    return pl.BlockSpec((1,) + dims, lambda g, member: (g ^ member[0],) + (0,) * len(dims))


def fixed_block(dims, index):
    return pl.BlockSpec(dims, lambda g: index)


def row_block(width, length=256):
    steps = length // ROWS
    return pl.BlockSpec((1, ROWS, width), lambda g: (g // steps, g % steps, 0))


SCALAR = pl.BlockSpec(memory_space=pltpu.SMEM)
MESSAGE = (2, PAYLOAD, Q_LANES)


def tie(value, *others):
    return lax.optimization_barrier((value,) + others)[0]


def exchange(payload, member, axis, reverse, stages):
    count = lax.axis_size(axis)
    stages = iter(stages)

    def swap(value, by):
        return lax.ppermute(value, axis, [(i, i ^ by) for i in range(count)])

    def meanwhile(sent, arrived):
        work = next(stages, None)
        return tie(arrived, *work(sent)) if work else arrived

    message = shape(MESSAGE, BF16)
    block = whole_block(MESSAGE)
    members = [payload[0]] + [swap(payload[by], by) for by in range(1, QUARTERS)]
    members[-1] = meanwhile(payload, members[-1])
    total = pl.pallas_call(
        functools.partial(plane_kernel, reverse),
        grid=(1,),
        in_specs=[SCALAR] + [block] * QUARTERS,
        out_specs=block,
        out_shape=message,
        compiler_params=params(14),
        cost_estimate=cost(2),
        name="plane",
    )(member, *members)
    received = []
    inclusive = total
    span = 1
    while span < count // QUARTERS:
        shift = -QUARTERS * span if reverse else QUARTERS * span
        pairs = [(i, i + shift) for i in range(count) if 0 <= i + shift < count]
        arrived = lax.ppermute(inclusive, axis, pairs)
        received.append(meanwhile(inclusive, arrived) if span < 4 else arrived)
        span *= 2
        if span < count // QUARTERS:
            inclusive = pl.pallas_call(
                link_kernel,
                grid=(1,),
                in_specs=[block] * (1 + len(received)),
                out_specs=block,
                out_shape=message,
                compiler_params=params(14),
                cost_estimate=cost(1.5),
                name="link",
            )(total, *received)
    results = pl.pallas_call(
        functools.partial(spread_kernel, reverse),
        grid=(1,),
        in_specs=[SCALAR] + [block] * (QUARTERS + len(received)),
        out_specs=[block] * QUARTERS,
        out_shape=[message] * QUARTERS,
        compiler_params=params(16),
        cost_estimate=cost(3),
        name="spread",
    )(member, *members, *received)
    back = [results[0]] + [swap(results[by], by) for by in range(1, QUARTERS)]
    back[-1] = meanwhile(results[-1], back[-1])
    return pl.pallas_call(
        arrange_kernel,
        grid_spec=pltpu.PrefetchScalarGridSpec(
            num_scalar_prefetch=1,
            grid=(QUARTERS,),
            in_specs=[block] * QUARTERS,
            out_specs=[own_lanes((2, STATE)), own_lanes((2, 8))],
        ),
        out_shape=[shape((2, STATE, INNER), BF16), shape((2, 8, INNER))],
        compiler_params=params(14),
        cost_estimate=cost(1.5),
        name="arrange",
    )(member, *back)


class Scatter:
    def __init__(self, arrays, axis):
        self.axis = axis
        self.count = lax.axis_size(axis)
        self.place = lax.axis_index(axis)
        self.bits = list(range(self.count.bit_length() - 1))[::-1]
        self.values = [
            a.reshape((2,) * len(self.bits) + (a.shape[0] // self.count, a.shape[1]))
            for a in arrays
        ]

    def wait_for(self, *others):
        self.values = list(lax.optimization_barrier(tuple(self.values) + others))[
            : len(self.values)
        ]

    def send(self, bit, *others):
        position = self.bits.index(bit)
        mine = (self.place >> bit) & 1
        away = [lax.dynamic_index_in_dim(v, 1 - mine, position, False) for v in self.values]
        away = jnp.concatenate([v.astype(BF16) for v in away], axis=-2)
        self.values = [lax.dynamic_index_in_dim(v, mine, position, False) for v in self.values]
        self.bits.remove(bit)
        self.away = away
        if others:
            away = tie(away, *others)
        self.sent = lax.ppermute(
            away, self.axis, [(i, i ^ (1 << bit)) for i in range(self.count)]
        )

    def add(self):
        begin = 0
        for i, value in enumerate(self.values):
            end = begin + value.shape[-2]
            self.values[i] = value + self.sent[..., begin:end, :].astype(F32)
            begin = end


def add_up(value, axes):
    for axis in axes:
        count = lax.axis_size(axis)
        for bit in range(count.bit_length() - 1):
            value = value + lax.ppermute(value, axis, [(i, i ^ (1 << bit)) for i in range(count)])
    return value


def finish_kernel(gate_rows, last_rows, out_rows, in_grad, out_grad):
    step = pl.program_id(0)
    length, columns = gate_rows.shape[0] * gate_rows.shape[1], gate_rows.shape[2]

    @pl.when(step < 2 * INNER // length)
    def _():
        in_grad[...] = gate_rows[...].reshape(length, columns).astype(F32)

    @pl.when(step == 2 * INNER // length)
    def _():
        rows = last_rows.shape[0] * last_rows.shape[1]
        keep = min(rows, in_grad.shape[0])
        in_grad[:keep] = last_rows[...].reshape(rows, columns)[:keep].astype(F32)

    @pl.when(step < INNER // length)
    def _():
        group, per = out_rows.shape[0], out_rows.shape[1] // 2
        for side in range(2):
            out_grad[:, columns * side : columns * side + columns] = (
                out_rows[:, per * side : per * side + per].reshape(group * per, columns).astype(F32)
            )


def local(
    hidden_in,
    norm_gain,
    in_weight,
    conv_weight,
    conv_bias,
    step_bias,
    decay_log,
    skip_gain,
    gate_gain,
    out_weight,
    cotangent,
):
    hidden = hidden_in[0]
    upstream = cotangent[0]
    tokens, width = hidden.shape
    half = tokens // 2
    share = in_weight.shape[0]
    count = lax.axis_size("seq")
    core = lax.axis_index("fsdp")
    other = [(0, 1), (1, 0)]

    rows_of = in_weight.T
    conv_rows = lax.optimization_barrier(rows_of[INNER:])
    conv_rows_other = lax.ppermute(conv_rows, "fsdp", other)

    paired = hidden.reshape(2, half, width)
    halo = lax.ppermute(
        tie(paired[:, half - EDGE :], conv_rows), "seq", [(i, i + 1) for i in range(count - 1)]
    )
    extended = jnp.concatenate([halo, paired], axis=1).reshape(2 * (half + EDGE), width)
    rows = extended.astype(F32)
    rescale = lax.rsqrt(jnp.mean(rows * rows, axis=-1, keepdims=True) + EPSILON)
    normed_ext = (rows * rescale * norm_gain).astype(BF16)

    rows_of_writes = rows_of[2 * INNER : 2 * INNER + STATE].astype(F32)
    power = 2.0 * jnp.sum(rows_of_writes * rows_of_writes, axis=1)
    deviation = jnp.sqrt(
        power * jnp.sum(jnp.square(conv_weight[:, INNER : INNER + STATE]), axis=0)
    )
    guess = jnp.zeros((STATE,), F32)
    for point, share_of in ((-1.7320508, 1 / 6), (0.0, 2 / 3), (1.7320508, 1 / 6)):
        guess = guess + share_of * jax.nn.silu(
            conv_bias[INNER : INNER + STATE] + point * deviation
        )
    direction = guess * lax.rsqrt(jnp.sum(guess * guess) + 1e-20)
    row_direction, column_direction = direction[None], direction[:, None]
    member = (lax.axis_index("seq") % QUARTERS).astype(jnp.int32).reshape(1)

    def mine(array, axis):
        first = lax.slice_in_dim(array, 0, share, axis=axis)
        second = lax.slice_in_dim(array, share, 2 * share, axis=axis)
        return (
            jnp.where(core == 0, first, second),
            jnp.where(core == 0, second, first),
        )

    def ordered(own, foreign, axis):
        return jnp.where(
            core == 0,
            jnp.concatenate([own, foreign], axis),
            jnp.concatenate([foreign, own], axis),
        )

    own_ext, other_ext = mine(normed_ext, 1)
    normed = normed_ext.reshape(2, half + EDGE, width)[:, EDGE:].reshape(tokens, width)
    own_normed, other_normed = mine(normed, 1)

    small = jnp.pad(jnp.stack([step_bias, decay_log, skip_gain]), ((0, 5), (0, TILE - HEADS)))
    bias_row = conv_bias[None]
    gain_row = gate_gain[None]
    skip_row = jnp.repeat(skip_gain, HEAD_DIM)[None]

    own_ext = tie(own_ext, row_direction, column_direction, small, bias_row, skip_row)
    conv_input = (dot_last(own_ext, conv_rows) + dot_last(other_ext, conv_rows_other)).reshape(
        2, half + EDGE, CONV_CH + HEADS
    )

    last_columns = fixed_block((2, half + EDGE, 384), (0, 0, INNER // 384))
    last_taps = fixed_block((CONV, 256), (0, INNER // 256))
    last_bias = fixed_block((1, 256), (0, INNER // 256))
    per_quarter = (QUARTERS, 2, half, SIDE)
    bc, bt, scores, scores_t, step, running, step_q, sum_q, sum_t = pl.pallas_call(
        step_kernel,
        grid=(1,),
        in_specs=[
            last_columns,
            last_taps,
            last_bias,
            whole_block((8, TILE)),
            whole_block((1, STATE)),
        ],
        out_specs=[
            whole_block((2, half, 256)),
            whole_block((2, STATE, half)),
            whole_block((2, half, half)),
            whole_block((2, half, half)),
            whole_block((2, half, TILE)),
            whole_block((2, half, TILE)),
            whole_block(per_quarter),
            whole_block(per_quarter),
            whole_block((QUARTERS, 2, EDGE, half)),
        ],
        out_shape=[
            shape((2, half, 256)),
            shape((2, STATE, half), BF16),
            shape((2, half, half)),
            shape((2, half, half)),
            shape((2, half, TILE)),
            shape((2, half, TILE)),
            shape(per_quarter),
            shape(per_quarter),
            shape((QUARTERS, 2, EDGE, half)),
        ],
        compiler_params=params(20),
        cost_estimate=cost(4),
        name="steps",
    )(conv_input, conv_weight, bias_row, small, row_direction)

    columns = lane_block((2, half + EDGE))
    taps_block = lane_block((CONV,))
    row_of = lane_block((1,))
    heads_block = quarter_block((2, half, SIDE))
    line_block = quarter_block((2, EDGE, half))
    tokens_block = lane_block((2, half))
    x, payload = pl.pallas_call(
        state_kernel,
        grid_spec=pltpu.PrefetchScalarGridSpec(
            num_scalar_prefetch=1,
            grid=(QUARTERS,),
            in_specs=[
                own_lanes((2, half + EDGE)),
                own_lanes((CONV,)),
                own_lanes((1,)),
                own_quarter((2, half, SIDE)),
                own_quarter((2, half, SIDE)),
                whole_block((2, STATE, half)),
                whole_block((STATE, 1)),
            ],
            out_specs=[own_lanes((2, half)), quarter_block(MESSAGE)],
        ),
        out_shape=[shape((2, half, INNER)), shape((QUARTERS,) + MESSAGE, BF16)],
        compiler_params=params(16),
        cost_estimate=cost(8),
        name="states",
    )(member, conv_input, conv_weight, bias_row, step_q, sum_q, bt, column_direction)

    gate_rows = rows_of[:INNER]
    out_rows = lax.all_gather(tie(out_weight, payload), "fsdp", axis=0, tiled=True)
    half_grid = QUARTERS // 2

    def later_half(spec, first):
        old = spec.index_map
        return pl.BlockSpec(spec.block_shape, lambda g: old(g + first))

    def shifted(specs, first):
        return [later_half(spec, first) for spec in specs]

    kept = {}

    def while_states_cross(sent):
        kept["rows"] = lax.ppermute(tie(rows_of, sent), "fsdp", other)[:INNER]
        kept["gate"] = dot_last(tie(own_normed, sent), gate_rows)
        return inside(0)(sent) + (kept["gate"],)

    def while_first_states(sent):
        kept["grad"] = dot_last(tie(upstream, sent), out_rows).reshape(2, half, INNER)
        return (kept["grad"],)

    def inside(first):
        def work(sent):
            specs = [
                tokens_block,
                heads_block,
                heads_block,
                line_block,
                whole_block((2, half, half)),
                row_of,
            ]
            inputs = [tie(x, sent), step_q, sum_q, sum_t, scores, skip_row]
            kept["inside"] = pl.pallas_call(
                intra_kernel,
                grid=(half_grid,),
                in_specs=shifted(specs, first)
                + [pl.BlockSpec(memory_space=pl.ANY)] * (first > 0),
                out_specs=later_half(tokens_block, first),
                out_shape=shape((2, half, INNER)),
                input_output_aliases={len(specs): 0} if first else {},
                compiler_params=params(60),
                cost_estimate=cost(8),
                name="inside",
            )(*inputs, *([kept["inside"]] if first else []))
            return (kept["inside"],)

        return work

    def while_states_return(sent):
        kept["z"] = (
            kept["gate"] + dot_last(tie(other_normed, sent), kept["rows"])
        ).reshape(2, half, INNER)
        return (kept["z"],)

    entering, along = exchange(
        payload,
        member,
        "seq",
        False,
        [while_states_cross, while_first_states, inside(half_grid), while_states_return],
    )
    gate_rows_other = kept["rows"]
    y_inside, z, grad_normed_out = kept["inside"], kept["z"], kept["grad"]

    token_rows = row_block(INNER)
    steps = half // ROWS
    normed_out, grad_z, grad_scan, back_payload, gate_gain_grad = pl.pallas_call(
        gate_kernel,
        grid=(2 * steps,),
        in_specs=[
            SCALAR,
            token_rows,
            token_rows,
            token_rows,
            row_block(256),
            row_block(TILE),
            pl.BlockSpec((1, STATE, INNER), lambda g: (g // steps, 0, 0)),
            pl.BlockSpec((1, 8, INNER), lambda g: (g // steps, 0, 0)),
            whole_block((1, INNER)),
        ],
        out_specs=[
            token_rows,
            token_rows,
            token_rows,
            whole_block((QUARTERS,) + MESSAGE),
            whole_block((1, INNER)),
        ],
        out_shape=[
            shape((2, half, INNER), BF16),
            shape((2, half, INNER), BF16),
            shape((2, half, INNER)),
            shape((QUARTERS,) + MESSAGE, BF16),
            shape((1, INNER)),
        ],
        scratch_shapes=[
            pltpu.VMEM((ROWS, INNER), F32),
            pltpu.VMEM((ROWS, INNER), F32),
            pltpu.VMEM((ROWS, INNER), F32),
            pltpu.VMEM((ROWS, INNER), F32),
            pltpu.VMEM((ROWS, INNER), BF16),
            pltpu.VMEM((STATE, INNER), F32),
        ],
        compiler_params=params(38),
        cost_estimate=cost(14),
        name="gates",
    )(
        member,
        y_inside,
        z,
        grad_normed_out,
        bc,
        running,
        entering,
        along,
        gain_row,
    )

    normed_out = normed_out.reshape(tokens, INNER)
    grad_z = grad_z.reshape(tokens, INNER)
    first_out, second_out = normed_out[:, : INNER // 2], normed_out[:, INNER // 2 :]
    own_out = jnp.where(core == 0, first_out, second_out)
    other_out = jnp.where(core == 0, second_out, first_out)

    def weight_part(own, foreign):
        sent = lax.ppermute(dot_first(*foreign).astype(BF16), "fsdp", other)
        return dot_first(*own) + sent.astype(F32)

    def while_gradients_cross(sent):
        out_part = weight_part((own_out, upstream), (other_out, upstream))
        gate_part = weight_part((grad_z, own_normed), (grad_z, other_normed))
        kept["out"] = Scatter([out_part], "seq")
        kept["gates"] = Scatter([gate_part], "seq")
        return out_part, gate_part

    state_columns = lane_block((2, STATE))
    line_columns = lane_block((2, 8))
    edge_columns = lane_block((2, EDGE))
    back_parts = []

    def inside_back(first):
        def work(sent):
            if not first:
                for part, bit in ((kept["out"], 0), (kept["gates"], 1)):
                    part.send(bit, sent)
            specs = [
                tokens_block,
                tokens_block,
                tokens_block,
                columns,
                taps_block,
                row_of,
                heads_block,
                heads_block,
                line_block,
                whole_block((2, half, half)),
                whole_block((2, half, 256)),
                state_columns,
                line_columns,
                row_of,
                whole_block((1, STATE)),
            ]
            inputs = [
                x,
                tie(grad_scan, sent),
                y_inside,
                conv_input,
                conv_weight,
                bias_row,
                step_q,
                sum_q,
                sum_t,
                scores_t,
                bc,
                entering,
                along,
                skip_row,
                row_direction,
            ]
            earlier = [back_parts[0][i] for i in (0, 1, 3)] if first else []
            back_parts.append(
                pl.pallas_call(
                    intra_back_kernel,
                    grid=(half_grid,),
                    in_specs=shifted(specs, first)
                    + [pl.BlockSpec(memory_space=pl.ANY)] * len(earlier),
                    out_specs=shifted(
                        [
                            tokens_block,
                            tokens_block,
                            whole_block((2, half, half)),
                            quarter_block((2, half, TILE)),
                            whole_block((2, half, STATE)),
                        ],
                        first,
                    ),
                    out_shape=[
                        shape((2, half, INNER)),
                        shape((2, half, INNER), BF16),
                        shape((2, half, half)),
                        shape((QUARTERS, 2, half, TILE)),
                        shape((2, half, STATE)),
                    ],
                    scratch_shapes=[
                        pltpu.VMEM((3, half, Q_LANES), F32),
                        pltpu.VMEM((half, Q_LANES), BF16),
                    ],
                    input_output_aliases={
                        len(specs) + i: (0, 1, 3)[i] for i in range(len(earlier))
                    },
                    compiler_params=params(60),
                    cost_estimate=cost(17),
                    name="inside_back",
                )(*inputs, *earlier)
            )
            return tuple(back_parts[-1])

        return work

    def while_gradients_return(sent):
        for part in (kept["out"], kept["gates"]):
            part.sent = tie(part.sent, sent)
            part.add()
        return kept["out"].values[0], kept["gates"].values[0]

    leaving, _ = exchange(
        back_payload,
        member,
        "seq",
        True,
        [while_gradients_cross, inside_back(0), inside_back(half_grid), while_gradients_return],
    )
    out_part, gate_part = kept["out"], kept["gates"]
    for part, bit in ((out_part, 1), (gate_part, 0)):
        part.wait_for(leaving)
        part.send(bit)
    leaving = tie(leaving, out_part.away, gate_part.away)
    known, slope, _, known_heads, _ = back_parts[1]
    grad_conv, tail, halo_grad, grad_mix, heads, grad_writes, meeting = pl.pallas_call(
        channel_kernel,
        grid=(QUARTERS,),
        in_specs=[
            tokens_block,
            tokens_block,
            tokens_block,
            taps_block,
            heads_block,
            heads_block,
            whole_block((2, half, 256)),
            state_columns,
            state_columns,
            line_columns,
            whole_block((STATE, 1)),
        ],
        out_specs=[
            tokens_block,
            edge_columns,
            edge_columns,
            tokens_block,
            quarter_block((2, half, TILE)),
            whole_block((2, half, STATE)),
            lane_block((8,)),
        ],
        out_shape=[
            shape((2, half, INNER), BF16),
            shape((2, EDGE, INNER)),
            shape((2, EDGE, INNER), BF16),
            shape((2, half, INNER), BF16),
            shape((QUARTERS, 2, half, TILE)),
            shape((2, half, STATE)),
            shape((8, INNER)),
        ],
        scratch_shapes=[
            pltpu.VMEM((half + 2 * EDGE, TILE), F32),
            pltpu.VMEM((half, Q_LANES), F32),
            pltpu.VMEM((half, Q_LANES), BF16),
        ],
        compiler_params=params(60),
        cost_estimate=cost(12),
        name="channels",
    )(
        known,
        slope,
        x,
        conv_weight,
        step_q,
        sum_q,
        bc,
        leaving,
        entering,
        along,
        column_direction,
    )

    grad_conv_last, tail_last, halo_last, sums_last, small_grads = pl.pallas_call(
        last_kernel,
        grid=(1,),
        in_specs=[
            last_columns,
            last_taps,
            last_bias,
            whole_block((8, TILE)),
            whole_block((2, half, 256)),
            whole_block((2, half, half)),
            whole_block((2, half, half)),
            whole_block((2, half, STATE)),
            whole_block((2, half, STATE)),
            whole_block((2, half, STATE)),
            whole_block((QUARTERS, 2, half, TILE)),
            whole_block((QUARTERS, 2, half, TILE)),
            whole_block((8, INNER)),
            whole_block((2, half, TILE)),
            whole_block((2, half, TILE)),
        ],
        out_specs=[
            whole_block((2, half, 256 + HEADS)),
            whole_block((2, EDGE, 256)),
            whole_block((2, EDGE, 256)),
            whole_block((8, 256)),
            whole_block((8, TILE)),
        ],
        out_shape=[
            shape((2, half, 256 + HEADS), BF16),
            shape((2, EDGE, 256)),
            shape((2, EDGE, 256), BF16),
            shape((8, 256)),
            shape((8, TILE)),
        ],
        scratch_shapes=[pltpu.VMEM((half + 2 * EDGE, 256), F32)],
        compiler_params=params(60),
        cost_estimate=cost(6),
        name="last",
    )(
        conv_input,
        conv_weight,
        bias_row,
        small,
        bc,
        back_parts[0][2],
        back_parts[1][2],
        grad_writes,
        back_parts[0][4],
        back_parts[1][4],
        known_heads,
        heads,
        meeting,
        step,
        running,
    )

    returned = lax.ppermute(
        tie(jnp.concatenate([halo_grad, halo_last], axis=-1), out_part.sent, gate_part.sent),
        "seq",
        [(i, i - 1) for i in range(1, count)],
    )
    fixed_tail = (jnp.concatenate([tail, tail_last], axis=-1) + returned.astype(F32)).astype(BF16)
    body = half - EDGE
    grad_wide = jnp.concatenate([grad_conv[:, :body], fixed_tail[:, :, :INNER]], axis=1)
    grad_wide = grad_wide.reshape(tokens, INNER)
    per = INNER // count
    per_last = -(-(CONV_CH + HEADS - INNER) // (16 * count)) * 16
    spare = per_last * count - (CONV_CH + HEADS - INNER)
    grad_narrow = jnp.concatenate(
        [
            grad_conv_last[:, :body],
            jnp.concatenate([fixed_tail[:, :, INNER:], grad_conv_last[:, body:, 256:]], axis=-1),
        ],
        axis=1,
    ).reshape(tokens, CONV_CH + HEADS - INNER)
    grad_padded = jnp.pad(grad_narrow, ((0, 0), (0, spare)))

    for part in (out_part, gate_part):
        part.add()
    early = gate_part
    out_value = out_part.values[0]
    early.values.append(
        jnp.concatenate([out_value[..., :share], out_value[..., share:]], axis=-2)
    )
    bits = early.bits[::-1]
    early.send(bits[0])

    grad_wide, grad_padded = lax.optimization_barrier((grad_wide, grad_padded, early.away))[:2]
    wide_part = weight_part((grad_wide, own_normed), (grad_wide, other_normed))
    last_part = weight_part((grad_padded, own_normed), (grad_padded, other_normed))
    cut = share // 2
    first_part = Scatter([wide_part[:, :cut], last_part[:, :cut]], "seq")
    second_part = Scatter([wide_part[:, cut:], last_part[:, cut:]], "seq")
    first_part.send(0)
    second_part.send(1)
    early.add()
    for bit in bits[1:]:
        early.send(bit)
        early.add()
    for part, bit in ((first_part, 1), (second_part, 0)):
        part.add()
        part.send(bit)
    for part in (first_part, second_part):
        part.add()
    late = second_part
    late.values = [
        jnp.concatenate(pair, axis=-1) for pair in zip(first_part.values, second_part.values)
    ]
    late.wait_for(*early.values)
    for bit in bits:
        late.send(bit)
        late.add()

    gate_value, out_value = early.values
    shard = jnp.concatenate([gate_value, out_value] + late.values, axis=-2).astype(BF16)
    gathered = lax.all_gather(shard, "seq", axis=0)

    grad_z, grad_wide, grad_narrow, normed_out, grad_mix = lax.optimization_barrier(
        (grad_z, grad_wide, grad_narrow, normed_out, grad_mix, shard)
    )[:5]

    def through_rows(first, second):
        return (
            dot(grad_z, first) + dot(grad_wide, second[:INNER]) + dot(grad_narrow, second[INNER:])
        )

    grad_normed = ordered(
        through_rows(gate_rows, conv_rows), through_rows(gate_rows_other, conv_rows_other), 1
    )
    u = hidden.astype(F32)
    r = lax.rsqrt(jnp.mean(u * u, axis=-1, keepdims=True) + EPSILON)
    norm_gain_grad = jnp.sum(grad_normed * u * r, axis=0)
    through = grad_normed * norm_gain
    input_grad = (
        upstream.astype(F32)
        + r * through
        - u * (r * r * r) * jnp.mean(through * u, axis=-1, keepdims=True)
    ).astype(BF16)
    block_out = (hidden.astype(F32) + dot(normed_out, out_rows)).astype(BF16)

    sums = pl.pallas_call(
        sums_kernel,
        grid=(QUARTERS,),
        in_specs=[columns, tokens_block, tokens_block, tokens_block],
        out_specs=lane_block((8,)),
        out_shape=shape((8, INNER)),
        compiler_params=params(60),
        cost_estimate=cost(10),
        name="sums",
    )(conv_input, grad_mix, grad_scan, x)

    skip_grad = jnp.sum(sums[5].reshape(HEADS, HEAD_DIM), axis=1)
    vector = jnp.concatenate(
        [
            norm_gain_grad,
            sums[:5].reshape(-1),
            sums_last[:5].reshape(-1),
            small_grads[:2].reshape(-1),
            gate_gain_grad[0],
            jnp.pad(skip_grad, (0, TILE - HEADS)),
        ]
    )
    length = vector.shape[0]
    vector = add_up(vector.reshape(length // TILE, TILE), ("fsdp", "seq")).reshape(length)
    parts = []
    begin = 0
    for size in (width, 5 * INNER, 5 * 256, 2 * TILE, INNER, HEADS):
        parts.append(vector[begin : begin + size])
        begin += size
    conv_sums = jnp.concatenate(
        [parts[1].reshape(5, INNER), parts[2].reshape(5, 256)], axis=1
    )
    smalls = parts[3].reshape(2, TILE)[:, :HEADS]

    group = share // per
    parts_of = INNER // share
    gathered_block = (group, per, share)
    in_grad, out_grad = pl.pallas_call(
        finish_kernel,
        grid=(2 * parts_of + 1,),
        in_specs=[
            pl.BlockSpec(
                gathered_block,
                lambda g: (jnp.minimum(g, 2 * parts_of - 1) % parts_of, g // parts_of * 2 % 4, 0),
            ),
            pl.BlockSpec((count, per_last, share), lambda g: (0, 3 * per // per_last, 0)),
            pl.BlockSpec(gathered_block, lambda g: (jnp.minimum(g, parts_of - 1), 1, 0)),
        ],
        out_specs=[
            pl.BlockSpec((share, share), lambda g: (g, 0)),
            pl.BlockSpec((share // 2, width), lambda g: (jnp.minimum(g, parts_of - 1), 0)),
        ],
        out_shape=[shape((CONV_CH + HEADS + INNER, share)), shape((2 * share, width))],
        compiler_params=params(60),
        cost_estimate=cost(14),
        name="finish",
    )(gathered, gathered, gathered)
    return (
        block_out[None],
        input_grad[None],
        parts[0],
        in_grad.T,
        conv_sums[:4],
        conv_sums[4],
        smalls[0],
        smalls[1],
        parts[5],
        parts[4],
        out_grad,
    )


def solution(mesh):
    return jax.shard_map(
        local,
        mesh=mesh,
        in_specs=(
            P("fsdp", "seq", None),
            P(),
            P("fsdp", None),
            P(),
            P(),
            P(),
            P(),
            P(),
            P(),
            P("fsdp", None),
            P("fsdp", "seq", None),
        ),
        out_specs=(
            P("fsdp", "seq", None),
            P("fsdp", "seq", None),
            P(),
            P("fsdp", None),
            P(),
            P(),
            P(),
            P(),
            P(),
            P(),
            P("fsdp", None),
        ),
        check_vma=False,
    )
```

```python
import functools

import jax
import jax.numpy as jnp
from jax import lax
from jax.experimental import pallas as pl
from jax.experimental.pallas import tpu as pltpu
from jax.sharding import PartitionSpec as P

HEADS = 48
HEAD_DIM = 64
STATE = 128
CONV = 4
INNER = 3072
CONV_CH = 3328
EPSILON = 1e-05

QUARTERS = 4
Q_HEADS = HEADS // QUARTERS
Q_LANES = INNER // QUARTERS
TILE = 128
Q_TILES = Q_LANES // TILE
EDGE = 16
PAYLOAD = STATE + EDGE
ROWS = 128
SIDE = 16
SUB = 128
FAR = -1e30
MIB = 1024 * 1024
HIGHEST = lax.Precision.HIGHEST
F32 = jnp.float32
BF16 = jnp.bfloat16


def params(mebibytes):
    return pltpu.CompilerParams(vmem_limit_bytes=mebibytes * MIB)


def cost(microseconds):
    return pl.CostEstimate(
        flops=0, transcendentals=0, bytes_accessed=int(microseconds * 3_400_000)
    )


def low_lanes():
    return lax.broadcasted_iota(jnp.int32, (1, TILE), 1) < HEAD_DIM


def pick(per_head, tile):
    return jnp.where(
        low_lanes(),
        per_head[:, 2 * tile : 2 * tile + 1],
        per_head[:, 2 * tile + 1 : 2 * tile + 2],
    )


def head_columns(channels, columns, offset):
    row = lax.broadcasted_iota(jnp.int32, (channels, columns), 0)
    col = lax.broadcasted_iota(jnp.int32, (channels, columns), 1) - offset
    return ((row >= HEAD_DIM * col) & (row < HEAD_DIM * col + HEAD_DIM)).astype(BF16)


def head_sums(wide, selector):
    high = wide.astype(BF16)
    rest = (wide - high.astype(F32)).astype(BF16)
    return jnp.dot(high, selector, preferred_element_type=F32) + jnp.dot(
        rest, selector, preferred_element_type=F32
    )


def dot(left, right):
    return jnp.dot(left, right, preferred_element_type=F32)


def dot_last(left, right, precision=None):
    return lax.dot_general(
        left,
        right,
        (((1,), (1,)), ((), ())),
        preferred_element_type=F32,
        precision=precision,
    )


def dot_first(left, right, precision=None):
    return lax.dot_general(
        left,
        right,
        (((0,), (0,)), ((), ())),
        preferred_element_type=F32,
        precision=precision,
    )


def mixture_of(conv_input, seq, lanes, weight, bias):
    total = bias
    for tap in range(CONV):
        start = EDGE - CONV + 1 + tap
        total = total + weight[tap : tap + 1] * conv_input[seq, start : start + 256, lanes]
    return total


def silu_slope(value):
    gate = jax.nn.sigmoid(value)
    return gate * (1.0 + value * (1.0 - gate))


def three_parts(value):
    high = value.astype(BF16).astype(F32)
    middle = (value - high).astype(BF16).astype(F32)
    return high, middle, value - high - middle


def edge_rows(decay, along):
    index = lax.broadcasted_iota(jnp.int32, (EDGE, TILE), 0)
    rows = jnp.zeros((EDGE, TILE), F32)
    for row, part in enumerate(three_parts(decay) + three_parts(along)):
        rows = jnp.where(index == row, part, rows)
    return rows.astype(BF16)


def read_payload(ref, seq, lanes):
    state = ref[seq, :STATE, lanes].astype(F32)
    rows = ref[seq, STATE:, lanes].astype(F32)
    decay = rows[0:1] + rows[1:2] + rows[2:3]
    along = rows[3:4] + rows[4:5] + rows[5:6]
    return state, decay, along


def write_payload(ref, seq, lanes, state, decay, along):
    ref[seq, :STATE, lanes] = state.astype(BF16)
    ref[seq, STATE:, lanes] = edge_rows(decay, along)


def after(first, second):
    return (
        second[0] + second[1] * first[0],
        second[1] * first[1],
        second[2] + second[1] * first[2],
    )


def empty():
    return (
        jnp.zeros((STATE, TILE), F32),
        jnp.ones((1, TILE), F32),
        jnp.zeros((1, TILE), F32),
    )


def parts_of_quarter():
    for seq in range(2):
        for tile in range(Q_TILES):
            yield seq, slice(TILE * tile, TILE * tile + TILE)


def joined(refs, seq, lanes):
    result = read_payload(refs[0], seq, lanes)
    for ref in refs[1:]:
        result = after(read_payload(ref, seq, lanes), result)
    return result


def plane_kernel(reverse, member, *refs):
    members, total = refs[:QUARTERS], refs[QUARTERS]
    order = range(QUARTERS)[::-1] if reverse else range(QUARTERS)
    for place in range(QUARTERS):

        @pl.when(member[0] == place)
        def _(place=place):
            for seq, lanes in parts_of_quarter():
                whole = None
                for which in order:
                    here = read_payload(members[place ^ which], seq, lanes)
                    whole = here if whole is None else after(whole, here)
                write_payload(total, seq, lanes, *whole)


def link_kernel(*refs):
    total, received, result = refs[0], refs[1:-1], refs[-1]
    for seq, lanes in parts_of_quarter():
        whole = after(joined(received, seq, lanes), read_payload(total, seq, lanes))
        write_payload(result, seq, lanes, *whole)


def spread_kernel(reverse, member, *refs):
    members, received, results = refs[:QUARTERS], refs[QUARTERS:-QUARTERS], refs[-QUARTERS:]
    order = list(range(QUARTERS)[::-1] if reverse else range(QUARTERS))
    for place in range(QUARTERS):

        @pl.when(member[0] == place)
        def _(place=place):
            for seq, lanes in parts_of_quarter():
                whole = joined(received, seq, lanes)
                for which in order:
                    write_payload(results[place ^ which], seq, lanes, *whole)
                    if which != order[-1]:
                        whole = after(whole, read_payload(members[place ^ which], seq, lanes))


def arrange_kernel(member, *refs):
    pieces, state_ref, along_ref = refs[:QUARTERS], refs[QUARTERS], refs[QUARTERS + 1]
    for by in range(QUARTERS):

        @pl.when(pl.program_id(0) == by)
        def _(by=by):
            for seq, lanes in parts_of_quarter():
                state_ref[seq, :, lanes] = pieces[by][seq, :STATE, lanes]
                rows = pieces[by][seq, STATE:, lanes].astype(F32)
                along = rows[3:4] + rows[4:5] + rows[5:6]
                along_ref[seq, :, lanes] = jnp.broadcast_to(along, (8, TILE))


def step_kernel(
    conv_input,
    weight,
    bias,
    small,
    in_rows,
    bc_ref,
    bt_ref,
    scores_ref,
    scores_t_ref,
    step_ref,
    sum_ref,
    step_q_ref,
    sum_q_ref,
    sum_t_ref,
    direction,
    column,
):
    values = in_rows[...].astype(F32)
    power = 2.0 * jnp.sum(values * values, axis=1, keepdims=True)
    power = jnp.broadcast_to(power, (STATE, STATE)).T[0:1]
    taps = weight[:, :STATE]
    deviation = jnp.sqrt(power * jnp.sum(taps * taps, axis=0, keepdims=True))
    guess = jnp.zeros((1, STATE), F32)
    for point, share in ((-1.7320508, 1 / 6), (0.0, 2 / 3), (1.7320508, 1 / 6)):
        level = bias[:, :STATE] + point * deviation
        guess = guess + share * (level * jax.nn.sigmoid(level))
    guess = guess * lax.rsqrt(jnp.sum(guess * guess, axis=1, keepdims=True) + 1e-20)
    direction[...] = guess
    column[...] = jnp.broadcast_to(guess, (STATE, STATE)).T[:, 0:1]
    row = lax.broadcasted_iota(jnp.int32, (256, 256), 0)
    col = lax.broadcasted_iota(jnp.int32, (256, 256), 1)
    lower = (row >= col).astype(F32)
    lane = lax.broadcasted_iota(jnp.int32, (1, TILE), 1)
    for seq in range(2):
        mixture = mixture_of(conv_input, seq, slice(0, 256), weight[...], bias[...])
        active = mixture * jax.nn.sigmoid(mixture)
        bc_ref[seq] = active
        writes, readout = active[:, :STATE], active[:, STATE:]
        bt_ref[seq] = writes.T.astype(BF16)
        scores = dot_last(readout, writes, HIGHEST)
        scores_ref[seq] = scores
        scores_t_ref[seq] = scores.T
        along = jnp.sum(readout * direction[...], axis=1, keepdims=True)
        raw = conv_input[seq, EDGE : EDGE + 256, 256:384] + small[0:1]
        raw = jnp.where(lane < HEADS, raw, 0.0)
        step = jnp.maximum(raw, 0.0) + jnp.log1p(jnp.exp(-jnp.abs(raw)))
        log_decay = -jnp.exp(small[1:2]) * step
        running = jnp.dot(lower, log_decay, preferred_element_type=F32, precision=HIGHEST)
        step_ref[seq] = step
        sum_ref[seq] = jnp.where(lane == HEADS, along, running)
        for quarter in range(QUARTERS):
            shift = (TILE - Q_HEADS * quarter) % TILE
            step_q = pltpu.roll(step, shift, 1) if shift else step
            sum_q = pltpu.roll(running, shift, 1) if shift else running
            step_q_ref[quarter, seq] = step_q[:, :SIDE]
            sum_q_ref[quarter, seq] = jnp.where(lane == Q_HEADS, along, sum_q)[:, :SIDE]
            sum_t_ref[quarter, seq] = sum_q.T[:EDGE]


def state_kernel(
    member, conv_input, weight, bias, step_q, sum_q, bt_ref, column, x_ref, *payloads
):
    for by, payload_ref in enumerate(payloads[:QUARTERS]):

        @pl.when(pl.program_id(0) == by)
        def _(payload_ref=payload_ref):
            state_of_quarter(
                conv_input, weight, bias, step_q, sum_q, bt_ref, column, x_ref, payload_ref
            )


def state_of_quarter(
    conv_input, weight, bias, step_q, sum_q, bt_ref, column, x_ref, payload_ref
):
    for seq in range(2):
        running = sum_q[0, seq]
        last = running[255:256]
        scale = step_q[0, seq] * jnp.exp(last - running)
        whole = jnp.exp(last)
        for tile in range(Q_TILES):
            lanes = slice(TILE * tile, TILE * tile + TILE)
            mixture = mixture_of(conv_input, seq, lanes, weight[:, lanes], bias[:, lanes])
            x = mixture * jax.nn.sigmoid(mixture)
            x_ref[seq, :, lanes] = x
            added = dot(bt_ref[seq], (x * pick(scale, tile)).astype(BF16))
            along = jnp.sum(added * column[...], axis=0, keepdims=True)
            payload_ref[seq, :STATE, lanes] = (added - column[...] * along).astype(BF16)
            payload_ref[seq, STATE:, lanes] = edge_rows(pick(whole, tile), along)


def intra_kernel(x_ref, step_q, sum_q, sum_t, scores, skip, *refs):
    y_ref = refs[-1]
    row = lax.broadcasted_iota(jnp.int32, (SUB, SUB), 0)
    col = lax.broadcasted_iota(jnp.int32, (SUB, SUB), 1)
    causal = row >= col
    low = low_lanes()
    for seq in range(2):
        step, running = step_q[0, seq], sum_q[0, seq]
        middle = running[SUB - 1 : SUB]
        ahead = jnp.exp(middle - running[:SUB])
        later = jnp.exp(running[SUB:] - middle)
        across = scores[seq, SUB:, :SUB].astype(BF16)
        for tile in range(Q_TILES):
            lanes = slice(TILE * tile, TILE * tile + TILE)
            x = x_ref[seq, :, lanes]
            scaled = x * pick(step, tile)
            low_part = jnp.where(low, scaled, 0.0).astype(BF16)
            high_part = jnp.where(low, 0.0, scaled).astype(BF16)
            for part in range(2):
                rows = slice(SUB * part, SUB * part + SUB)
                weights = []
                for h in (2 * tile, 2 * tile + 1):
                    spread = running[rows, h : h + 1] - sum_t[0, seq, h : h + 1, rows]
                    decayed = jnp.exp(jnp.where(causal, spread, FAR))
                    weights.append((decayed * scores[seq, rows, rows]).astype(BF16))
                inside = dot(
                    jnp.concatenate(weights, 1),
                    jnp.concatenate([low_part[rows], high_part[rows]], 0),
                )
                if part:
                    earlier = (scaled[:SUB] * pick(ahead, tile)).astype(BF16)
                    inside = inside + pick(later, tile) * dot(across, earlier)
                y_ref[seq, rows, lanes] = inside + skip[:, lanes] * x[rows]


def gate_kernel(
    member,
    y_ref,
    z_ref,
    grad_ref,
    bc_ref,
    sum_ref,
    entering,
    along,
    gain,
    out_ref,
    grad_z_ref,
    grad_scan_ref,
    payload_0,
    payload_1,
    payload_2,
    payload_3,
    gain_grad_ref,
    scanned_ref,
    gated_ref,
    gate_ref,
    start_ref,
    spread,
    state_ref,
):
    step = pl.program_id(0)
    per_seq = pl.num_programs(0) // 2
    running = sum_ref[0]
    start = jnp.exp(running)
    read_along = running[:, HEADS : HEADS + 1]
    readout = bc_ref[0, :, STATE:].astype(BF16)
    readout_t = bc_ref[0, :, STATE:].T.astype(BF16)
    squares = jnp.zeros((ROWS, TILE), F32)
    overlap = jnp.zeros((ROWS, TILE), F32)
    for tile in range(INNER // TILE):
        lanes = slice(TILE * tile, TILE * tile + TILE)
        if tile % 2 == 0:
            wide = dot(readout, entering[0, :, TILE * tile : TILE * tile + 2 * TILE])
        carried = wide[:, TILE * (tile % 2) : TILE * (tile % 2) + TILE]
        carried = carried + read_along * along[0, 0:1, lanes]
        begin = pick(start, tile)
        start_ref[:, lanes] = begin
        scanned = y_ref[0, :, lanes] + begin * carried
        scanned_ref[:, lanes] = scanned
        z = z_ref[0, :, lanes]
        gate = jax.nn.sigmoid(z)
        gate_ref[:, lanes] = gate
        gated = scanned * (z * gate)
        gated_ref[:, lanes] = gated
        squares = squares + gated * gated
        overlap = overlap + gated * (grad_ref[0, :, lanes] * gain[:, lanes])
    mean = jnp.sum(squares, axis=1, keepdims=True) / INNER
    inverse = lax.rsqrt(mean + EPSILON)
    back = jnp.sum(overlap, axis=1, keepdims=True) / INNER * inverse * inverse * inverse

    @pl.when(step == 0)
    def _():
        gain_grad_ref[...] = jnp.zeros_like(gain_grad_ref)

    @pl.when(step % per_seq == 0)
    def _():
        state_ref[...] = jnp.zeros_like(state_ref)

    for tile in range(INNER // TILE):
        lanes = slice(TILE * tile, TILE * tile + TILE)
        gated = gated_ref[:, lanes]
        grad = grad_ref[0, :, lanes]
        scaled = gated * inverse
        out_ref[0, :, lanes] = (scaled * gain[:, lanes]).astype(BF16)
        gain_grad_ref[:, lanes] += jnp.sum(grad * scaled, axis=0, keepdims=True)
        grad_gated = inverse * (grad * gain[:, lanes]) - gated * back
        z = z_ref[0, :, lanes]
        gate = gate_ref[:, lanes]
        grad_scan = grad_gated * (z * gate)
        grad_z_ref[0, :, lanes] = (
            grad_gated * scanned_ref[:, lanes] * (gate * (1.0 + z * (1.0 - gate)))
        ).astype(BF16)
        grad_scan_ref[0, :, lanes] = grad_scan
        spread[:, lanes] = (grad_scan * start_ref[:, lanes]).astype(BF16)
        if tile % 2:
            both = slice(TILE * tile - TILE, TILE * tile + TILE)
            state_ref[:, both] += dot(readout_t, spread[:, both])

    @pl.when(step % per_seq == per_seq - 1)
    def _():
        seq = step // per_seq
        whole = start[ROWS - 1 : ROWS]
        zero = jnp.zeros((1, TILE), F32)
        for tile in range(INNER // TILE):
            lanes = slice(TILE * tile, TILE * tile + TILE)
            place = slice(TILE * (tile % Q_TILES), TILE * (tile % Q_TILES) + TILE)
            slot = member[0] ^ (tile // Q_TILES)
            state = state_ref[:, lanes].astype(BF16)
            edge = edge_rows(pick(whole, tile), zero)
            for by, payload_ref in enumerate((payload_0, payload_1, payload_2, payload_3)):

                @pl.when(slot == by)
                def _(payload_ref=payload_ref, state=state, edge=edge, place=place):
                    payload_ref[seq, :STATE, place] = state
                    payload_ref[seq, STATE:, place] = edge


def intra_back_kernel(
    x_ref,
    grad_ref,
    y_ref,
    conv_input,
    weight,
    bias,
    step_q,
    sum_q,
    sum_t,
    scores_t,
    bc_ref,
    entering,
    along,
    skip,
    direction,
    *refs,
):
    known_ref, slope_ref, grad_scores_ref, heads_ref, grad_read_ref, product, spread = refs[-7:]
    row = lax.broadcasted_iota(jnp.int32, (SUB, SUB), 0)
    col = lax.broadcasted_iota(jnp.int32, (SUB, SUB), 1)
    causal = row <= col
    low = low_lanes()

    @pl.when(pl.program_id(0) == 0)
    def _():
        grad_scores_ref[...] = jnp.zeros_like(grad_scores_ref)
        grad_read_ref[...] = jnp.zeros_like(grad_read_ref)

    for seq in range(2):
        step, running = step_q[0, seq], sum_q[0, seq]
        middle = running[SUB - 1 : SUB]
        start = jnp.exp(running)
        read_along = running[:, Q_HEADS : Q_HEADS + 1]
        ahead = jnp.exp(middle - running[:SUB])
        later = jnp.exp(running[SUB:] - middle)
        across = scores_t[seq, :SUB, SUB:].astype(BF16)
        readout = bc_ref[seq, :, STATE:].astype(BF16)
        inner = [jnp.zeros((SUB, SUB), F32) for _ in range(2)]
        outer = jnp.zeros((SUB, SUB), F32)
        meeting = jnp.zeros((256, TILE), F32)
        product[2] = dot(readout, entering[seq])
        for tile in range(Q_TILES):
            lanes = slice(TILE * tile, TILE * tile + TILE)
            x = x_ref[seq, :, lanes]
            size = pick(step, tile)
            scaled = x * size
            grad = grad_ref[seq, :, lanes]
            begin = pick(start, tile)
            low_grad = jnp.where(low, grad, 0.0).astype(BF16)
            high_grad = jnp.where(low, 0.0, grad).astype(BF16)
            rounded = grad.astype(BF16)
            line = along[seq, 0:1, lanes]
            carried = product[2, :, lanes] + read_along * line
            through = skip[:, lanes] * x
            product[2, :, lanes] = rounded.astype(F32) * (
                y_ref[seq, :, lanes] + begin * carried - through
            )
            widened = grad * begin
            meeting = meeting + widened * line
            spread[:, lanes] = widened.astype(BF16)
            mixture = mixture_of(conv_input, seq, lanes, weight[:, lanes], bias[:, lanes])
            slope = silu_slope(mixture)
            slope_ref[seq, :, lanes] = slope.astype(BF16)
            sides = (
                jnp.where(low, scaled, 0.0).astype(BF16),
                jnp.where(low, 0.0, scaled).astype(BF16),
            )
            for part in range(2):
                rows = slice(SUB * part, SUB * part + SUB)
                weights = []
                pairs = dot_last(
                    jnp.concatenate([sides[0][rows], sides[1][rows]], 0), rounded[rows]
                )
                for side in range(2):
                    h = 2 * tile + side
                    apart = sum_t[0, seq, h : h + 1, rows] - running[rows, h : h + 1]
                    decayed = jnp.exp(jnp.where(causal, apart, FAR))
                    weights.append((decayed * scores_t[seq, rows, rows]).astype(BF16))
                    inner[part] = inner[part] + decayed * pairs[SUB * side : SUB * side + SUB]
                inside = dot(
                    jnp.concatenate(weights, 1),
                    jnp.concatenate([low_grad[rows], high_grad[rows]], 0),
                )
                if not part:
                    beyond = (rounded[SUB:].astype(F32) * pick(later, tile)).astype(BF16)
                    factor = pick(ahead, tile)
                    inside = inside + factor * dot(across, beyond)
                    outer = outer + dot_last((scaled[:SUB] * factor).astype(BF16), beyond)
                product[0, rows, lanes] = scaled[rows].astype(BF16).astype(F32) * inside
                product[1, rows, lanes] = x[rows] * inside
                known_ref[seq, rows, lanes] = (
                    size[rows] * inside + skip[:, lanes] * grad[rows]
                ) * slope[rows]
        grad_scores_ref[seq, :SUB, :SUB] += inner[0]
        grad_scores_ref[seq, SUB:, SUB:] += inner[1]
        grad_scores_ref[seq, :SUB, SUB:] += outer
        total = jnp.zeros((256, TILE), F32)
        for kind in range(3):
            total = total + head_sums(product[kind], head_columns(Q_LANES, TILE, Q_HEADS * kind))
        heads_ref[0, seq] = total
        grad_read_ref[seq] += (
            dot_last(spread[...], entering[seq])
            + jnp.sum(meeting, axis=1, keepdims=True) * direction[...]
        )


def channel_kernel(
    known_ref,
    slope_ref,
    x_ref,
    weight,
    step_q,
    sum_q,
    bc_ref,
    leaving,
    entering,
    along,
    column,
    grad_conv_ref,
    tail_ref,
    halo_ref,
    grad_mix_ref,
    heads_ref,
    grad_writes_ref,
    meeting_ref,
    padded,
    product,
    spread,
):
    zeros = jnp.zeros((EDGE, TILE), F32)
    padded[:EDGE] = zeros
    padded[EDGE + 256 :] = zeros
    meeting_ref[...] = jnp.zeros_like(meeting_ref)

    @pl.when(pl.program_id(0) == 0)
    def _():
        grad_writes_ref[...] = jnp.zeros_like(grad_writes_ref)

    for seq in range(2):
        running = sum_q[0, seq]
        remain = jnp.exp(running[255:256] - running)
        scale = step_q[0, seq] * remain
        writes = bc_ref[seq, :, :STATE].astype(BF16)
        product[...] = dot(writes, leaving[seq])
        for tile in range(Q_TILES):
            lanes = slice(TILE * tile, TILE * tile + TILE)
            taps = weight[:, lanes]
            x = x_ref[seq, :, lanes]
            back = leaving[seq, :, lanes]
            shared = product[:, lanes]
            product[:, lanes] = x * shared
            factor = pick(scale, tile)
            spread[:, lanes] = (x * factor).astype(BF16)
            slope = slope_ref[seq, :, lanes].astype(F32)
            grad_mix = known_ref[seq, :, lanes] + factor * slope * shared
            grad_mix_ref[seq, :, lanes] = grad_mix.astype(BF16)
            padded[EDGE : EDGE + 256] = grad_mix
            grad_conv = taps[0:1] * padded[3 : 3 + EDGE + 256]
            for tap in range(1, CONV):
                grad_conv = (
                    grad_conv + taps[tap : tap + 1] * padded[3 - tap : 3 - tap + EDGE + 256]
                )
            halo_ref[seq, :, lanes] = grad_conv[:EDGE].astype(BF16)
            grad_conv_ref[seq, :, lanes] = grad_conv[EDGE:].astype(BF16)
            tail_ref[seq, :, lanes] = grad_conv[256:]
            state = entering[seq, :, lanes].astype(F32) + column[...] * along[seq, 0:1, lanes]
            meeting_ref[seq : seq + 1, lanes] = jnp.sum(
                state * back.astype(F32), axis=0, keepdims=True
            )
        total = dot(product[...].astype(BF16), head_columns(Q_LANES, TILE, 0))
        heads_ref[0, seq] = jnp.zeros((256, TILE), F32)
        heads_ref[0, seq, :, :SIDE] = total[:, :SIDE] * remain
        grad_writes_ref[seq] += dot_last(spread[...], leaving[seq])


def sums_kernel(conv_input, grad_mix_ref, grad_ref, x_ref, sums_ref):
    sums_ref[...] = jnp.zeros_like(sums_ref)
    for seq in range(2):
        for tile in range(Q_TILES):
            lanes = slice(TILE * tile, TILE * tile + TILE)
            grad_mix = grad_mix_ref[seq, :, lanes].astype(F32)
            for tap in range(CONV):
                begin = EDGE - CONV + 1 + tap
                sums_ref[tap : tap + 1, lanes] += jnp.sum(
                    grad_mix * conv_input[seq, begin : begin + 256, lanes], axis=0, keepdims=True
                )
            sums_ref[4:5, lanes] += jnp.sum(grad_mix, axis=0, keepdims=True)
            sums_ref[5:6, lanes] += jnp.sum(
                grad_ref[seq, :, lanes] * x_ref[seq, :, lanes], axis=0, keepdims=True
            )


def last_kernel(
    conv_input,
    weight,
    bias,
    small,
    bc_ref,
    grad_scores_0,
    grad_scores_1,
    grad_writes,
    grad_read_0,
    grad_read_1,
    known_heads,
    heads,
    meeting,
    step_ref,
    sum_ref,
    grad_conv_ref,
    tail_ref,
    halo_ref,
    sums_ref,
    small_ref,
    padded,
):
    row = lax.broadcasted_iota(jnp.int32, (256, 256), 0)
    col = lax.broadcasted_iota(jnp.int32, (256, 256), 1)
    upper = (row <= col).astype(F32)
    lane = lax.broadcasted_iota(jnp.int32, (1, TILE), 1)
    line = lax.broadcasted_iota(jnp.int32, (256, 1), 0)
    padded[:EDGE] = jnp.zeros((EDGE, 256), F32)
    padded[EDGE + 256 :] = jnp.zeros((EDGE, 256), F32)
    sums_ref[...] = jnp.zeros_like(sums_ref)
    small_ref[...] = jnp.zeros_like(small_ref)
    rate = jnp.exp(small[1:2])
    met_states = head_sums(meeting[...], head_columns(INNER, TILE, 0))
    taps = weight[...]

    def gather(source, seq, kind):
        total = jnp.zeros((256, TILE), F32)
        for quarter in range(QUARTERS):
            value = source[quarter, seq]
            shift = (Q_HEADS * (quarter - kind)) % TILE
            if shift:
                value = pltpu.roll(value, shift, 1)
            first = Q_HEADS * quarter
            total = total + jnp.where((lane >= first) & (lane < first + Q_HEADS), value, 0.0)
        return total

    for seq in range(2):
        step = step_ref[seq]
        by_state = gather(heads, seq, 0)
        at_state = step * by_state
        running = sum_ref[seq]
        last = jnp.where(lane < HEADS, running[255:256], 0.0)
        end = jnp.exp(last) * met_states[seq : seq + 1] + jnp.sum(
            at_state, axis=0, keepdims=True
        )
        grad_sum = (
            gather(known_heads, seq, 2)
            - gather(known_heads, seq, 0)
            - at_state
            + jnp.where(line == 255, end, 0.0)
        )
        grad_log = jnp.dot(upper, grad_sum, preferred_element_type=F32, precision=HIGHEST)
        small_ref[1:2] += jnp.sum(-rate * step * grad_log, axis=0, keepdims=True)
        raw = conv_input[seq, EDGE : EDGE + 256, 256:384] + small[0:1]
        raw = jnp.where(lane < HEADS, raw, 0.0)
        grad_step = gather(known_heads, seq, 1) + by_state - rate * grad_log
        grad_raw = grad_step * jax.nn.sigmoid(raw)
        small_ref[0:1] += jnp.sum(grad_raw, axis=0, keepdims=True)
        grad_conv_ref[seq, :, 256:] = grad_raw[:, :HEADS].astype(BF16)
        writes, readout = bc_ref[seq, :, :STATE], bc_ref[seq, :, STATE:]
        grad_scores = grad_scores_0[seq] + grad_scores_1[seq]
        into_writes = (
            jnp.dot(grad_scores, readout, preferred_element_type=F32, precision=HIGHEST)
            + grad_writes[seq]
        )
        into_read = dot_first(grad_scores, writes, HIGHEST) + grad_read_0[seq] + grad_read_1[seq]
        mixture = mixture_of(conv_input, seq, slice(0, 256), taps, bias[...])
        grad_mix = jnp.concatenate([into_writes, into_read], 1) * silu_slope(mixture)
        padded[EDGE : EDGE + 256] = grad_mix
        grad_conv = taps[0:1] * padded[3 : 3 + EDGE + 256]
        for tap in range(1, CONV):
            grad_conv = grad_conv + taps[tap : tap + 1] * padded[3 - tap : 3 - tap + EDGE + 256]
        halo_ref[seq] = grad_conv[:EDGE].astype(BF16)
        grad_conv_ref[seq, :, :256] = grad_conv[EDGE:].astype(BF16)
        tail_ref[seq] = grad_conv[256:]
        for tap in range(CONV):
            begin = EDGE - CONV + 1 + tap
            sums_ref[tap : tap + 1] += jnp.sum(
                grad_mix * conv_input[seq, begin : begin + 256, :256], axis=0, keepdims=True
            )
        sums_ref[4:5] += jnp.sum(grad_mix, axis=0, keepdims=True)


def shape(dims, dtype=F32):
    return jax.ShapeDtypeStruct(dims, dtype)


def whole_block(dims):
    return pl.BlockSpec(dims, lambda *g: (0,) * len(dims))


def lane_block(dims, width=Q_LANES):
    return pl.BlockSpec(dims + (width,), lambda g: (0,) * len(dims) + (g,))


def quarter_block(dims):
    return pl.BlockSpec((1,) + dims, lambda g, *_: (g,) + (0,) * len(dims))


def own_lanes(dims):
    return pl.BlockSpec(
        dims + (Q_LANES,), lambda g, member: (0,) * len(dims) + (g ^ member[0],)
    )


def own_quarter(dims):
    return pl.BlockSpec((1,) + dims, lambda g, member: (g ^ member[0],) + (0,) * len(dims))


def fixed_block(dims, index):
    return pl.BlockSpec(dims, lambda g: index)


def row_block(width, length=256):
    steps = length // ROWS
    return pl.BlockSpec((1, ROWS, width), lambda g: (g // steps, g % steps, 0))


SCALAR = pl.BlockSpec(memory_space=pltpu.SMEM)
MESSAGE = (2, PAYLOAD, Q_LANES)


def tie(value, *others):
    return lax.optimization_barrier((value,) + others)[0]


def exchange(payload, member, axis, reverse, stages):
    count = lax.axis_size(axis)
    stages = iter(stages)

    def swap(value, by):
        return lax.ppermute(value, axis, [(i, i ^ by) for i in range(count)])

    def meanwhile(sent, arrived):
        work = next(stages, None)
        return tie(arrived, *work(sent)) if work else arrived

    message = shape(MESSAGE, BF16)
    block = whole_block(MESSAGE)
    members = [payload[0]] + [swap(payload[by], by) for by in range(1, QUARTERS)]
    members[-1] = meanwhile(payload[-1], members[-1])
    total = pl.pallas_call(
        functools.partial(plane_kernel, reverse),
        grid=(1,),
        in_specs=[SCALAR] + [block] * QUARTERS,
        out_specs=block,
        out_shape=message,
        compiler_params=params(14),
        cost_estimate=cost(2),
        name="plane",
    )(member, *members)
    received = []
    inclusive = total
    span = 1
    while span < count // QUARTERS:
        shift = -QUARTERS * span if reverse else QUARTERS * span
        pairs = [(i, i + shift) for i in range(count) if 0 <= i + shift < count]
        arrived = lax.ppermute(inclusive, axis, pairs)
        received.append(meanwhile(inclusive, arrived) if span < 4 else arrived)
        span *= 2
        if span < count // QUARTERS:
            inclusive = pl.pallas_call(
                link_kernel,
                grid=(1,),
                in_specs=[block] * (1 + len(received)),
                out_specs=block,
                out_shape=message,
                compiler_params=params(14),
                cost_estimate=cost(1.5),
                name="link",
            )(total, *received)
    results = pl.pallas_call(
        functools.partial(spread_kernel, reverse),
        grid=(1,),
        in_specs=[SCALAR] + [block] * (QUARTERS + len(received)),
        out_specs=[block] * QUARTERS,
        out_shape=[message] * QUARTERS,
        compiler_params=params(16),
        cost_estimate=cost(3),
        name="spread",
    )(member, *members, *received)
    back = [results[0]] + [swap(results[by], by) for by in range(1, QUARTERS)]
    back[-1] = meanwhile(results[-1], back[-1])
    return pl.pallas_call(
        arrange_kernel,
        grid_spec=pltpu.PrefetchScalarGridSpec(
            num_scalar_prefetch=1,
            grid=(QUARTERS,),
            in_specs=[block] * QUARTERS,
            out_specs=[own_lanes((2, STATE)), own_lanes((2, 8))],
        ),
        out_shape=[shape((2, STATE, INNER), BF16), shape((2, 8, INNER))],
        compiler_params=params(14),
        cost_estimate=cost(1.5),
        name="arrange",
    )(member, *back)


class Scatter:
    def __init__(self, arrays, axis):
        self.axis = axis
        self.count = lax.axis_size(axis)
        self.place = lax.axis_index(axis)
        self.bits = list(range(self.count.bit_length() - 1))[::-1]
        self.values = [
            a.reshape((2,) * len(self.bits) + (a.shape[0] // self.count, a.shape[1]))
            for a in arrays
        ]

    def wait_for(self, *others):
        self.values = list(lax.optimization_barrier(tuple(self.values) + others))[
            : len(self.values)
        ]

    def send(self, bit, *others):
        position = self.bits.index(bit)
        mine = (self.place >> bit) & 1
        away = [lax.dynamic_index_in_dim(v, 1 - mine, position, False) for v in self.values]
        away = jnp.concatenate([v.astype(BF16) for v in away], axis=-2)
        self.values = [lax.dynamic_index_in_dim(v, mine, position, False) for v in self.values]
        self.bits.remove(bit)
        self.away = away
        if others:
            away = tie(away, *others)
        self.sent = lax.ppermute(
            away, self.axis, [(i, i ^ (1 << bit)) for i in range(self.count)]
        )

    def add(self):
        begin = 0
        for i, value in enumerate(self.values):
            end = begin + value.shape[-2]
            self.values[i] = value + self.sent[..., begin:end, :].astype(F32)
            begin = end


def add_up(value, axes):
    for axis in axes:
        count = lax.axis_size(axis)
        for bit in range(count.bit_length() - 1):
            value = value + lax.ppermute(value, axis, [(i, i ^ (1 << bit)) for i in range(count)])
    return value


def finish_kernel(gate_rows, last_rows, out_rows, in_grad, out_grad):
    step = pl.program_id(0)
    length, columns = gate_rows.shape[0] * gate_rows.shape[1], gate_rows.shape[2]

    @pl.when(step < 2 * INNER // length)
    def _():
        in_grad[...] = gate_rows[...].reshape(length, columns).astype(F32)

    @pl.when(step == 2 * INNER // length)
    def _():
        rows = last_rows.shape[0] * last_rows.shape[1]
        keep = min(rows, in_grad.shape[0])
        in_grad[:keep] = last_rows[...].reshape(rows, columns)[:keep].astype(F32)

    @pl.when(step < INNER // length)
    def _():
        group, per = out_rows.shape[0], out_rows.shape[1] // 2
        for side in range(2):
            out_grad[:, columns * side : columns * side + columns] = (
                out_rows[:, per * side : per * side + per].reshape(group * per, columns).astype(F32)
            )


def local(
    hidden_in,
    norm_gain,
    in_weight,
    conv_weight,
    conv_bias,
    step_bias,
    decay_log,
    skip_gain,
    gate_gain,
    out_weight,
    cotangent,
):
    hidden = hidden_in[0]
    upstream = cotangent[0]
    tokens, width = hidden.shape
    half = tokens // 2
    share = in_weight.shape[0]
    count = lax.axis_size("seq")
    core = lax.axis_index("fsdp")
    other = [(0, 1), (1, 0)]

    rows_of = in_weight.T
    conv_rows = lax.optimization_barrier(rows_of[INNER:])
    conv_rows_other = lax.ppermute(conv_rows, "fsdp", other)

    paired = hidden.reshape(2, half, width)
    halo = lax.ppermute(
        tie(paired[:, half - EDGE :], conv_rows), "seq", [(i, i + 1) for i in range(count - 1)]
    )
    extended = jnp.concatenate([halo, paired], axis=1).reshape(2 * (half + EDGE), width)
    rows = extended.astype(F32)
    rescale = lax.rsqrt(jnp.mean(rows * rows, axis=-1, keepdims=True) + EPSILON)
    normed_ext = (rows * rescale * norm_gain).astype(BF16)

    member = (lax.axis_index("seq") % QUARTERS).astype(jnp.int32).reshape(1)

    def mine(array, axis):
        first = lax.slice_in_dim(array, 0, share, axis=axis)
        second = lax.slice_in_dim(array, share, 2 * share, axis=axis)
        return (
            jnp.where(core == 0, first, second),
            jnp.where(core == 0, second, first),
        )

    def ordered(own, foreign, axis):
        return jnp.where(
            core == 0,
            jnp.concatenate([own, foreign], axis),
            jnp.concatenate([foreign, own], axis),
        )

    own_ext, other_ext = mine(normed_ext, 1)
    normed = normed_ext.reshape(2, half + EDGE, width)[:, EDGE:].reshape(tokens, width)
    own_normed, other_normed = mine(normed, 1)

    small = jnp.pad(jnp.stack([step_bias, decay_log, skip_gain]), ((0, 5), (0, TILE - HEADS)))
    bias_row = conv_bias[None]
    gain_row = gate_gain[None]
    skip_row = jnp.repeat(skip_gain, HEAD_DIM)[None]

    own_ext = tie(own_ext, small, bias_row, skip_row)
    conv_input = (dot_last(own_ext, conv_rows) + dot_last(other_ext, conv_rows_other)).reshape(
        2, half + EDGE, CONV_CH + HEADS
    )

    last_columns = fixed_block((2, half + EDGE, 384), (0, 0, INNER // 384))
    last_taps = fixed_block((CONV, 256), (0, INNER // 256))
    last_bias = fixed_block((1, 256), (0, INNER // 256))
    per_quarter = (QUARTERS, 2, half, SIDE)
    (
        bc,
        bt,
        scores,
        scores_t,
        step,
        running,
        step_q,
        sum_q,
        sum_t,
        row_direction,
        column_direction,
    ) = pl.pallas_call(
        step_kernel,
        grid=(1,),
        in_specs=[
            last_columns,
            last_taps,
            last_bias,
            whole_block((8, TILE)),
            fixed_block((STATE, share), (2 * INNER // STATE, 0)),
        ],
        out_specs=[
            whole_block((2, half, 256)),
            whole_block((2, STATE, half)),
            whole_block((2, half, half)),
            whole_block((2, half, half)),
            whole_block((2, half, TILE)),
            whole_block((2, half, TILE)),
            whole_block(per_quarter),
            whole_block(per_quarter),
            whole_block((QUARTERS, 2, EDGE, half)),
            whole_block((1, STATE)),
            whole_block((STATE, 1)),
        ],
        out_shape=[
            shape((2, half, 256)),
            shape((2, STATE, half), BF16),
            shape((2, half, half)),
            shape((2, half, half)),
            shape((2, half, TILE)),
            shape((2, half, TILE)),
            shape(per_quarter),
            shape(per_quarter),
            shape((QUARTERS, 2, EDGE, half)),
            shape((1, STATE)),
            shape((STATE, 1)),
        ],
        compiler_params=params(20),
        cost_estimate=cost(4),
        name="steps",
    )(conv_input, conv_weight, bias_row, small, rows_of)

    columns = lane_block((2, half + EDGE))
    taps_block = lane_block((CONV,))
    row_of = lane_block((1,))
    heads_block = quarter_block((2, half, SIDE))
    line_block = quarter_block((2, EDGE, half))
    tokens_block = lane_block((2, half))
    x, *payload = pl.pallas_call(
        state_kernel,
        grid_spec=pltpu.PrefetchScalarGridSpec(
            num_scalar_prefetch=1,
            grid=(QUARTERS,),
            in_specs=[
                own_lanes((2, half + EDGE)),
                own_lanes((CONV,)),
                own_lanes((1,)),
                own_quarter((2, half, SIDE)),
                own_quarter((2, half, SIDE)),
                whole_block((2, STATE, half)),
                whole_block((STATE, 1)),
            ],
            out_specs=[own_lanes((2, half))] + [whole_block(MESSAGE)] * QUARTERS,
        ),
        out_shape=[shape((2, half, INNER))] + [shape(MESSAGE, BF16)] * QUARTERS,
        compiler_params=params(16),
        cost_estimate=cost(8),
        name="states",
    )(member, conv_input, conv_weight, bias_row, step_q, sum_q, bt, column_direction)

    gate_rows = rows_of[:INNER]
    out_rows = lax.all_gather(tie(out_weight, *payload), "fsdp", axis=0, tiled=True)
    half_grid = QUARTERS // 2

    def later_half(spec, first):
        old = spec.index_map
        return pl.BlockSpec(spec.block_shape, lambda g: old(g + first))

    def shifted(specs, first):
        return [later_half(spec, first) for spec in specs]

    kept = {}

    def while_states_cross(sent):
        kept["rows"] = lax.ppermute(tie(rows_of, sent), "fsdp", other)[:INNER]
        kept["gate"] = dot_last(tie(own_normed, sent), gate_rows)
        return inside(0)(sent) + (kept["gate"],)

    def while_first_states(sent):
        kept["grad"] = dot_last(tie(upstream, sent), out_rows).reshape(2, half, INNER)
        return (kept["grad"],)

    def inside(first):
        def work(sent):
            specs = [
                tokens_block,
                heads_block,
                heads_block,
                line_block,
                whole_block((2, half, half)),
                row_of,
            ]
            inputs = [tie(x, sent), step_q, sum_q, sum_t, scores, skip_row]
            kept["inside"] = pl.pallas_call(
                intra_kernel,
                grid=(half_grid,),
                in_specs=shifted(specs, first)
                + [pl.BlockSpec(memory_space=pl.ANY)] * (first > 0),
                out_specs=later_half(tokens_block, first),
                out_shape=shape((2, half, INNER)),
                input_output_aliases={len(specs): 0} if first else {},
                compiler_params=params(60),
                cost_estimate=cost(8),
                name="inside",
            )(*inputs, *([kept["inside"]] if first else []))
            return (kept["inside"],)

        return work

    def while_states_return(sent):
        kept["z"] = (
            kept["gate"] + dot_last(tie(other_normed, sent), kept["rows"])
        ).reshape(2, half, INNER)
        return (kept["z"],)

    entering, along = exchange(
        payload,
        member,
        "seq",
        False,
        [while_states_cross, while_first_states, inside(half_grid), while_states_return],
    )
    gate_rows_other = kept["rows"]
    y_inside, z, grad_normed_out = kept["inside"], kept["z"], kept["grad"]

    token_rows = row_block(INNER)
    steps = half // ROWS
    normed_out, grad_z, grad_scan, *back_payload, gate_gain_grad = pl.pallas_call(
        gate_kernel,
        grid=(2 * steps,),
        in_specs=[
            SCALAR,
            token_rows,
            token_rows,
            token_rows,
            row_block(256),
            row_block(TILE),
            pl.BlockSpec((1, STATE, INNER), lambda g: (g // steps, 0, 0)),
            pl.BlockSpec((1, 8, INNER), lambda g: (g // steps, 0, 0)),
            whole_block((1, INNER)),
        ],
        out_specs=[
            token_rows,
            token_rows,
            token_rows,
            *[whole_block(MESSAGE)] * QUARTERS,
            whole_block((1, INNER)),
        ],
        out_shape=[
            shape((2, half, INNER), BF16),
            shape((2, half, INNER), BF16),
            shape((2, half, INNER)),
            *[shape(MESSAGE, BF16)] * QUARTERS,
            shape((1, INNER)),
        ],
        scratch_shapes=[
            pltpu.VMEM((ROWS, INNER), F32),
            pltpu.VMEM((ROWS, INNER), F32),
            pltpu.VMEM((ROWS, INNER), F32),
            pltpu.VMEM((ROWS, INNER), F32),
            pltpu.VMEM((ROWS, INNER), BF16),
            pltpu.VMEM((STATE, INNER), F32),
        ],
        compiler_params=params(38),
        cost_estimate=cost(14),
        name="gates",
    )(
        member,
        y_inside,
        z,
        grad_normed_out,
        bc,
        running,
        entering,
        along,
        gain_row,
    )

    normed_out = normed_out.reshape(tokens, INNER)
    grad_z = grad_z.reshape(tokens, INNER)
    first_out, second_out = normed_out[:, : INNER // 2], normed_out[:, INNER // 2 :]
    own_out = jnp.where(core == 0, first_out, second_out)
    other_out = jnp.where(core == 0, second_out, first_out)

    def weight_part(own, foreign):
        sent = lax.ppermute(dot_first(*foreign).astype(BF16), "fsdp", other)
        return dot_first(*own) + sent.astype(F32)

    def while_gradients_cross(sent):
        out_part = weight_part((own_out, upstream), (other_out, upstream))
        gate_part = weight_part((grad_z, own_normed), (grad_z, other_normed))
        kept["out"] = Scatter([out_part], "seq")
        kept["gates"] = Scatter([gate_part], "seq")
        return out_part, gate_part

    state_columns = lane_block((2, STATE))
    line_columns = lane_block((2, 8))
    edge_columns = lane_block((2, EDGE))
    back_parts = []

    def inside_back(first):
        def work(sent):
            if not first:
                for part, bit in ((kept["out"], 0), (kept["gates"], 1)):
                    part.send(bit, sent)
            specs = [
                tokens_block,
                tokens_block,
                tokens_block,
                columns,
                taps_block,
                row_of,
                heads_block,
                heads_block,
                line_block,
                whole_block((2, half, half)),
                whole_block((2, half, 256)),
                state_columns,
                line_columns,
                row_of,
                whole_block((1, STATE)),
            ]
            inputs = [
                x,
                tie(grad_scan, sent),
                y_inside,
                conv_input,
                conv_weight,
                bias_row,
                step_q,
                sum_q,
                sum_t,
                scores_t,
                bc,
                entering,
                along,
                skip_row,
                row_direction,
            ]
            earlier = [back_parts[0][i] for i in (0, 1, 3)] if first else []
            back_parts.append(
                pl.pallas_call(
                    intra_back_kernel,
                    grid=(half_grid,),
                    in_specs=shifted(specs, first)
                    + [pl.BlockSpec(memory_space=pl.ANY)] * len(earlier),
                    out_specs=shifted(
                        [
                            tokens_block,
                            tokens_block,
                            whole_block((2, half, half)),
                            quarter_block((2, half, TILE)),
                            whole_block((2, half, STATE)),
                        ],
                        first,
                    ),
                    out_shape=[
                        shape((2, half, INNER)),
                        shape((2, half, INNER), BF16),
                        shape((2, half, half)),
                        shape((QUARTERS, 2, half, TILE)),
                        shape((2, half, STATE)),
                    ],
                    scratch_shapes=[
                        pltpu.VMEM((3, half, Q_LANES), F32),
                        pltpu.VMEM((half, Q_LANES), BF16),
                    ],
                    input_output_aliases={
                        len(specs) + i: (0, 1, 3)[i] for i in range(len(earlier))
                    },
                    compiler_params=params(60),
                    cost_estimate=cost(17),
                    name="inside_back",
                )(*inputs, *earlier)
            )
            return tuple(back_parts[-1])

        return work

    def while_gradients_return(sent):
        for part in (kept["out"], kept["gates"]):
            part.sent = tie(part.sent, sent)
            part.add()
        return kept["out"].values[0], kept["gates"].values[0]

    leaving, _ = exchange(
        back_payload,
        member,
        "seq",
        True,
        [while_gradients_cross, inside_back(0), inside_back(half_grid), while_gradients_return],
    )
    out_part, gate_part = kept["out"], kept["gates"]
    for part, bit in ((out_part, 1), (gate_part, 0)):
        part.wait_for(leaving)
        part.send(bit)
    leaving = tie(leaving, out_part.away, gate_part.away)
    known, slope, _, known_heads, _ = back_parts[1]
    grad_conv, tail, halo_grad, grad_mix, heads, grad_writes, meeting = pl.pallas_call(
        channel_kernel,
        grid=(QUARTERS,),
        in_specs=[
            tokens_block,
            tokens_block,
            tokens_block,
            taps_block,
            heads_block,
            heads_block,
            whole_block((2, half, 256)),
            state_columns,
            state_columns,
            line_columns,
            whole_block((STATE, 1)),
        ],
        out_specs=[
            tokens_block,
            edge_columns,
            edge_columns,
            tokens_block,
            quarter_block((2, half, TILE)),
            whole_block((2, half, STATE)),
            lane_block((8,)),
        ],
        out_shape=[
            shape((2, half, INNER), BF16),
            shape((2, EDGE, INNER)),
            shape((2, EDGE, INNER), BF16),
            shape((2, half, INNER), BF16),
            shape((QUARTERS, 2, half, TILE)),
            shape((2, half, STATE)),
            shape((8, INNER)),
        ],
        scratch_shapes=[
            pltpu.VMEM((half + 2 * EDGE, TILE), F32),
            pltpu.VMEM((half, Q_LANES), F32),
            pltpu.VMEM((half, Q_LANES), BF16),
        ],
        compiler_params=params(60),
        cost_estimate=cost(12),
        name="channels",
    )(
        known,
        slope,
        x,
        conv_weight,
        step_q,
        sum_q,
        bc,
        leaving,
        entering,
        along,
        column_direction,
    )

    grad_conv_last, tail_last, halo_last, sums_last, small_grads = pl.pallas_call(
        last_kernel,
        grid=(1,),
        in_specs=[
            last_columns,
            last_taps,
            last_bias,
            whole_block((8, TILE)),
            whole_block((2, half, 256)),
            whole_block((2, half, half)),
            whole_block((2, half, half)),
            whole_block((2, half, STATE)),
            whole_block((2, half, STATE)),
            whole_block((2, half, STATE)),
            whole_block((QUARTERS, 2, half, TILE)),
            whole_block((QUARTERS, 2, half, TILE)),
            whole_block((8, INNER)),
            whole_block((2, half, TILE)),
            whole_block((2, half, TILE)),
        ],
        out_specs=[
            whole_block((2, half, 256 + HEADS)),
            whole_block((2, EDGE, 256)),
            whole_block((2, EDGE, 256)),
            whole_block((8, 256)),
            whole_block((8, TILE)),
        ],
        out_shape=[
            shape((2, half, 256 + HEADS), BF16),
            shape((2, EDGE, 256)),
            shape((2, EDGE, 256), BF16),
            shape((8, 256)),
            shape((8, TILE)),
        ],
        scratch_shapes=[pltpu.VMEM((half + 2 * EDGE, 256), F32)],
        compiler_params=params(60),
        cost_estimate=cost(6),
        name="last",
    )(
        conv_input,
        conv_weight,
        bias_row,
        small,
        bc,
        back_parts[0][2],
        back_parts[1][2],
        grad_writes,
        back_parts[0][4],
        back_parts[1][4],
        known_heads,
        heads,
        meeting,
        step,
        running,
    )

    returned = lax.ppermute(
        tie(jnp.concatenate([halo_grad, halo_last], axis=-1), out_part.sent, gate_part.sent),
        "seq",
        [(i, i - 1) for i in range(1, count)],
    )
    fixed_tail = (jnp.concatenate([tail, tail_last], axis=-1) + returned.astype(F32)).astype(BF16)
    body = half - EDGE
    grad_wide = jnp.concatenate([grad_conv[:, :body], fixed_tail[:, :, :INNER]], axis=1)
    grad_wide = grad_wide.reshape(tokens, INNER)
    per = INNER // count
    per_last = -(-(CONV_CH + HEADS - INNER) // (16 * count)) * 16
    spare = per_last * count - (CONV_CH + HEADS - INNER)
    grad_narrow = jnp.concatenate(
        [
            grad_conv_last[:, :body],
            jnp.concatenate([fixed_tail[:, :, INNER:], grad_conv_last[:, body:, 256:]], axis=-1),
        ],
        axis=1,
    ).reshape(tokens, CONV_CH + HEADS - INNER)
    grad_padded = jnp.pad(grad_narrow, ((0, 0), (0, spare)))

    for part in (out_part, gate_part):
        part.add()
    early = gate_part
    out_value = out_part.values[0]
    early.values.append(
        jnp.concatenate([out_value[..., :share], out_value[..., share:]], axis=-2)
    )
    bits = early.bits[::-1]
    early.send(bits[0])

    grad_wide, grad_padded = lax.optimization_barrier((grad_wide, grad_padded, early.away))[:2]
    wide_part = weight_part((grad_wide, own_normed), (grad_wide, other_normed))
    last_part = weight_part((grad_padded, own_normed), (grad_padded, other_normed))
    cut = share // 2
    first_part = Scatter([wide_part[:, :cut], last_part[:, :cut]], "seq")
    second_part = Scatter([wide_part[:, cut:], last_part[:, cut:]], "seq")
    first_part.send(0)
    second_part.send(1)
    early.add()
    for bit in bits[1:]:
        early.send(bit)
        early.add()
    for part, bit in ((first_part, 1), (second_part, 0)):
        part.add()
        part.send(bit)
    for part in (first_part, second_part):
        part.add()
    late = second_part
    late.values = [
        jnp.concatenate(pair, axis=-1) for pair in zip(first_part.values, second_part.values)
    ]
    late.wait_for(*early.values)
    for bit in bits:
        late.send(bit)
        late.add()

    gate_value, out_value = early.values
    shard = jnp.concatenate([gate_value, out_value] + late.values, axis=-2).astype(BF16)
    gathered = lax.all_gather(shard, "seq", axis=0)

    grad_z, grad_wide, grad_narrow, normed_out, grad_mix = lax.optimization_barrier(
        (grad_z, grad_wide, grad_narrow, normed_out, grad_mix, shard)
    )[:5]

    def through_rows(first, second):
        return (
            dot(grad_z, first) + dot(grad_wide, second[:INNER]) + dot(grad_narrow, second[INNER:])
        )

    grad_normed = ordered(
        through_rows(gate_rows, conv_rows), through_rows(gate_rows_other, conv_rows_other), 1
    )
    u = hidden.astype(F32)
    r = lax.rsqrt(jnp.mean(u * u, axis=-1, keepdims=True) + EPSILON)
    norm_gain_grad = jnp.sum(grad_normed * u * r, axis=0)
    through = grad_normed * norm_gain
    input_grad = (
        upstream.astype(F32)
        + r * through
        - u * (r * r * r) * jnp.mean(through * u, axis=-1, keepdims=True)
    ).astype(BF16)
    block_out = (hidden.astype(F32) + dot(normed_out, out_rows)).astype(BF16)

    sums = pl.pallas_call(
        sums_kernel,
        grid=(QUARTERS,),
        in_specs=[columns, tokens_block, tokens_block, tokens_block],
        out_specs=lane_block((8,)),
        out_shape=shape((8, INNER)),
        compiler_params=params(60),
        cost_estimate=cost(10),
        name="sums",
    )(conv_input, grad_mix, grad_scan, x)

    skip_grad = jnp.sum(sums[5].reshape(HEADS, HEAD_DIM), axis=1)
    vector = jnp.concatenate(
        [
            norm_gain_grad,
            sums[:5].reshape(-1),
            sums_last[:5].reshape(-1),
            small_grads[:2].reshape(-1),
            gate_gain_grad[0],
            jnp.pad(skip_grad, (0, TILE - HEADS)),
        ]
    )
    length = vector.shape[0]
    vector = add_up(vector.reshape(length // TILE, TILE), ("fsdp", "seq")).reshape(length)
    parts = []
    begin = 0
    for size in (width, 5 * INNER, 5 * 256, 2 * TILE, INNER, HEADS):
        parts.append(vector[begin : begin + size])
        begin += size
    conv_sums = jnp.concatenate(
        [parts[1].reshape(5, INNER), parts[2].reshape(5, 256)], axis=1
    )
    smalls = parts[3].reshape(2, TILE)[:, :HEADS]

    group = share // per
    parts_of = INNER // share
    gathered_block = (group, per, share)
    in_grad, out_grad = pl.pallas_call(
        finish_kernel,
        grid=(2 * parts_of + 1,),
        in_specs=[
            pl.BlockSpec(
                gathered_block,
                lambda g: (jnp.minimum(g, 2 * parts_of - 1) % parts_of, g // parts_of * 2 % 4, 0),
            ),
            pl.BlockSpec((count, per_last, share), lambda g: (0, 3 * per // per_last, 0)),
            pl.BlockSpec(gathered_block, lambda g: (jnp.minimum(g, parts_of - 1), 1, 0)),
        ],
        out_specs=[
            pl.BlockSpec((share, share), lambda g: (g, 0)),
            pl.BlockSpec((share // 2, width), lambda g: (jnp.minimum(g, parts_of - 1), 0)),
        ],
        out_shape=[shape((CONV_CH + HEADS + INNER, share)), shape((2 * share, width))],
        compiler_params=params(60),
        cost_estimate=cost(14),
        name="finish",
    )(gathered, gathered, gathered)
    return (
        block_out[None],
        input_grad[None],
        parts[0],
        in_grad.T,
        conv_sums[:4],
        conv_sums[4],
        smalls[0],
        smalls[1],
        parts[5],
        parts[4],
        out_grad,
    )


def solution(mesh):
    return jax.shard_map(
        local,
        mesh=mesh,
        in_specs=(
            P("fsdp", "seq", None),
            P(),
            P("fsdp", None),
            P(),
            P(),
            P(),
            P(),
            P(),
            P(),
            P("fsdp", None),
            P("fsdp", "seq", None),
        ),
        out_specs=(
            P("fsdp", "seq", None),
            P("fsdp", "seq", None),
            P(),
            P("fsdp", None),
            P(),
            P(),
            P(),
            P(),
            P(),
            P(),
            P("fsdp", None),
        ),
        check_vma=False,
    )
```

```python
import functools

import jax
import jax.numpy as jnp
from jax import lax
from jax.experimental import pallas as pl
from jax.experimental.pallas import tpu as pltpu
from jax.sharding import PartitionSpec as P

HEADS = 48
HEAD_DIM = 64
STATE = 128
CONV = 4
INNER = 3072
CONV_CH = 3328
EPSILON = 1e-05

QUARTERS = 4
Q_HEADS = HEADS // QUARTERS
Q_LANES = INNER // QUARTERS
TILE = 128
Q_TILES = Q_LANES // TILE
EDGE = 16
PAYLOAD = STATE + EDGE
ROWS = 128
SIDE = 16
SUB = 128
FAR = -1e30
MIB = 1024 * 1024
HIGHEST = lax.Precision.HIGHEST
F32 = jnp.float32
BF16 = jnp.bfloat16


def params(mebibytes):
    return pltpu.CompilerParams(vmem_limit_bytes=mebibytes * MIB)


def cost(microseconds):
    return pl.CostEstimate(
        flops=0, transcendentals=0, bytes_accessed=int(microseconds * 3_400_000)
    )


def low_lanes():
    return lax.broadcasted_iota(jnp.int32, (1, TILE), 1) < HEAD_DIM


def pick(per_head, tile):
    return jnp.where(
        low_lanes(),
        per_head[:, 2 * tile : 2 * tile + 1],
        per_head[:, 2 * tile + 1 : 2 * tile + 2],
    )


def head_columns(channels, columns, offset):
    row = lax.broadcasted_iota(jnp.int32, (channels, columns), 0)
    col = lax.broadcasted_iota(jnp.int32, (channels, columns), 1) - offset
    return ((row >= HEAD_DIM * col) & (row < HEAD_DIM * col + HEAD_DIM)).astype(BF16)


def head_sums(wide, selector):
    high = wide.astype(BF16)
    rest = (wide - high.astype(F32)).astype(BF16)
    return jnp.dot(high, selector, preferred_element_type=F32) + jnp.dot(
        rest, selector, preferred_element_type=F32
    )


def dot(left, right):
    return jnp.dot(left, right, preferred_element_type=F32)


def dot_last(left, right, precision=None):
    return lax.dot_general(
        left,
        right,
        (((1,), (1,)), ((), ())),
        preferred_element_type=F32,
        precision=precision,
    )


def dot_first(left, right, precision=None):
    return lax.dot_general(
        left,
        right,
        (((0,), (0,)), ((), ())),
        preferred_element_type=F32,
        precision=precision,
    )


def mixture_of(conv_input, seq, lanes, weight, bias):
    total = bias
    for tap in range(CONV):
        start = EDGE - CONV + 1 + tap
        total = total + weight[tap : tap + 1] * conv_input[seq, start : start + 256, lanes]
    return total


def silu_slope(value):
    gate = jax.nn.sigmoid(value)
    return gate * (1.0 + value * (1.0 - gate))


def three_parts(value):
    high = value.astype(BF16).astype(F32)
    middle = (value - high).astype(BF16).astype(F32)
    return high, middle, value - high - middle


def edge_rows(decay, along):
    index = lax.broadcasted_iota(jnp.int32, (EDGE, TILE), 0)
    rows = jnp.zeros((EDGE, TILE), F32)
    for row, part in enumerate(three_parts(decay) + three_parts(along)):
        rows = jnp.where(index == row, part, rows)
    return rows.astype(BF16)


def read_payload(ref, seq, lanes):
    state = ref[seq, :STATE, lanes].astype(F32)
    rows = ref[seq, STATE:, lanes].astype(F32)
    decay = rows[0:1] + rows[1:2] + rows[2:3]
    along = rows[3:4] + rows[4:5] + rows[5:6]
    return state, decay, along


def write_payload(ref, seq, lanes, state, decay, along):
    ref[seq, :STATE, lanes] = state.astype(BF16)
    ref[seq, STATE:, lanes] = edge_rows(decay, along)


def after(first, second):
    return (
        second[0] + second[1] * first[0],
        second[1] * first[1],
        second[2] + second[1] * first[2],
    )


def empty():
    return (
        jnp.zeros((STATE, TILE), F32),
        jnp.ones((1, TILE), F32),
        jnp.zeros((1, TILE), F32),
    )


def parts_of_quarter():
    for seq in range(2):
        for tile in range(Q_TILES):
            yield seq, slice(TILE * tile, TILE * tile + TILE)


def joined(refs, seq, lanes):
    result = read_payload(refs[0], seq, lanes)
    for ref in refs[1:]:
        result = after(read_payload(ref, seq, lanes), result)
    return result


def plane_kernel(reverse, member, *refs):
    members, total = refs[:QUARTERS], refs[QUARTERS]
    order = range(QUARTERS)[::-1] if reverse else range(QUARTERS)
    for place in range(QUARTERS):

        @pl.when(member[0] == place)
        def _(place=place):
            for seq, lanes in parts_of_quarter():
                whole = None
                for which in order:
                    here = read_payload(members[place ^ which], seq, lanes)
                    whole = here if whole is None else after(whole, here)
                write_payload(total, seq, lanes, *whole)


def link_kernel(*refs):
    total, received, result = refs[0], refs[1:-1], refs[-1]
    for seq, lanes in parts_of_quarter():
        whole = after(joined(received, seq, lanes), read_payload(total, seq, lanes))
        write_payload(result, seq, lanes, *whole)


def spread_kernel(reverse, member, *refs):
    members, received, results = refs[:QUARTERS], refs[QUARTERS:-QUARTERS], refs[-QUARTERS:]
    order = list(range(QUARTERS)[::-1] if reverse else range(QUARTERS))
    for place in range(QUARTERS):

        @pl.when(member[0] == place)
        def _(place=place):
            for seq, lanes in parts_of_quarter():
                whole = joined(received, seq, lanes)
                for which in order:
                    write_payload(results[place ^ which], seq, lanes, *whole)
                    if which != order[-1]:
                        whole = after(whole, read_payload(members[place ^ which], seq, lanes))


def arrange_kernel(member, *refs):
    pieces, state_ref, along_ref = refs[:QUARTERS], refs[QUARTERS], refs[QUARTERS + 1]
    for by in range(QUARTERS):

        @pl.when(pl.program_id(0) == by)
        def _(by=by):
            for seq, lanes in parts_of_quarter():
                state_ref[seq, :, lanes] = pieces[by][seq, :STATE, lanes]
                rows = pieces[by][seq, STATE:, lanes].astype(F32)
                along = rows[3:4] + rows[4:5] + rows[5:6]
                along_ref[seq, :, lanes] = jnp.broadcast_to(along, (8, TILE))


def step_kernel(
    conv_input,
    weight,
    bias,
    small,
    in_rows,
    bc_ref,
    bt_ref,
    scores_ref,
    scores_t_ref,
    step_ref,
    sum_ref,
    step_q_ref,
    sum_q_ref,
    sum_t_ref,
    direction,
    column,
):
    values = in_rows[...].astype(F32)
    power = 2.0 * jnp.sum(values * values, axis=1, keepdims=True)
    power = jnp.broadcast_to(power, (STATE, STATE)).T[0:1]
    taps = weight[:, :STATE]
    deviation = jnp.sqrt(power * jnp.sum(taps * taps, axis=0, keepdims=True))
    guess = jnp.zeros((1, STATE), F32)
    for point, share in ((-1.7320508, 1 / 6), (0.0, 2 / 3), (1.7320508, 1 / 6)):
        level = bias[:, :STATE] + point * deviation
        guess = guess + share * (level * jax.nn.sigmoid(level))
    guess = guess * lax.rsqrt(jnp.sum(guess * guess, axis=1, keepdims=True) + 1e-20)
    direction[...] = guess
    column[...] = jnp.broadcast_to(guess, (STATE, STATE)).T[:, 0:1]
    row = lax.broadcasted_iota(jnp.int32, (256, 256), 0)
    col = lax.broadcasted_iota(jnp.int32, (256, 256), 1)
    lower = (row >= col).astype(F32)
    lane = lax.broadcasted_iota(jnp.int32, (1, TILE), 1)
    for seq in range(2):
        mixture = mixture_of(conv_input, seq, slice(0, 256), weight[...], bias[...])
        active = mixture * jax.nn.sigmoid(mixture)
        bc_ref[seq] = active
        writes, readout = active[:, :STATE], active[:, STATE:]
        bt_ref[seq] = writes.T.astype(BF16)
        scores = dot_last(readout, writes, HIGHEST)
        scores_ref[seq] = scores
        scores_t_ref[seq] = scores.T
        along = jnp.sum(readout * direction[...], axis=1, keepdims=True)
        raw = conv_input[seq, EDGE : EDGE + 256, 256:384] + small[0:1]
        raw = jnp.where(lane < HEADS, raw, 0.0)
        step = jnp.maximum(raw, 0.0) + jnp.log1p(jnp.exp(-jnp.abs(raw)))
        log_decay = -jnp.exp(small[1:2]) * step
        running = jnp.dot(lower, log_decay, preferred_element_type=F32, precision=HIGHEST)
        step_ref[seq] = step
        sum_ref[seq] = jnp.where(lane == HEADS, along, running)
        for quarter in range(QUARTERS):
            shift = (TILE - Q_HEADS * quarter) % TILE
            step_q = pltpu.roll(step, shift, 1) if shift else step
            sum_q = pltpu.roll(running, shift, 1) if shift else running
            step_q_ref[quarter, seq] = step_q[:, :SIDE]
            sum_q_ref[quarter, seq] = jnp.where(lane == Q_HEADS, along, sum_q)[:, :SIDE]
            sum_t_ref[quarter, seq] = sum_q.T[:EDGE]


def state_kernel(
    member, conv_input, weight, bias, step_q, sum_q, bt_ref, column, x_ref, *payloads
):
    for by, payload_ref in enumerate(payloads[:QUARTERS]):

        @pl.when(pl.program_id(0) == by)
        def _(payload_ref=payload_ref):
            state_of_quarter(
                conv_input, weight, bias, step_q, sum_q, bt_ref, column, x_ref, payload_ref
            )


def state_of_quarter(
    conv_input, weight, bias, step_q, sum_q, bt_ref, column, x_ref, payload_ref
):
    for seq in range(2):
        running = sum_q[0, seq]
        last = running[255:256]
        scale = step_q[0, seq] * jnp.exp(last - running)
        whole = jnp.exp(last)
        for tile in range(Q_TILES):
            lanes = slice(TILE * tile, TILE * tile + TILE)
            mixture = mixture_of(conv_input, seq, lanes, weight[:, lanes], bias[:, lanes])
            x = mixture * jax.nn.sigmoid(mixture)
            x_ref[seq, :, lanes] = x
            added = dot(bt_ref[seq], (x * pick(scale, tile)).astype(BF16))
            along = jnp.sum(added * column[...], axis=0, keepdims=True)
            payload_ref[seq, :STATE, lanes] = (added - column[...] * along).astype(BF16)
            payload_ref[seq, STATE:, lanes] = edge_rows(pick(whole, tile), along)


def intra_kernel(x_ref, step_q, sum_q, sum_t, scores, skip, *refs):
    y_ref = refs[-1]
    row = lax.broadcasted_iota(jnp.int32, (SUB, SUB), 0)
    col = lax.broadcasted_iota(jnp.int32, (SUB, SUB), 1)
    causal = row >= col
    low = low_lanes()
    for seq in range(2):
        step, running = step_q[0, seq], sum_q[0, seq]
        middle = running[SUB - 1 : SUB]
        ahead = jnp.exp(middle - running[:SUB])
        later = jnp.exp(running[SUB:] - middle)
        across = scores[seq, SUB:, :SUB].astype(BF16)
        for tile in range(Q_TILES):
            lanes = slice(TILE * tile, TILE * tile + TILE)
            x = x_ref[seq, :, lanes]
            scaled = x * pick(step, tile)
            low_part = jnp.where(low, scaled, 0.0).astype(BF16)
            high_part = jnp.where(low, 0.0, scaled).astype(BF16)
            for part in range(2):
                rows = slice(SUB * part, SUB * part + SUB)
                weights = []
                for h in (2 * tile, 2 * tile + 1):
                    spread = running[rows, h : h + 1] - sum_t[0, seq, h : h + 1, rows]
                    decayed = jnp.exp(jnp.where(causal, spread, FAR))
                    weights.append((decayed * scores[seq, rows, rows]).astype(BF16))
                inside = dot(
                    jnp.concatenate(weights, 1),
                    jnp.concatenate([low_part[rows], high_part[rows]], 0),
                )
                if part:
                    earlier = (scaled[:SUB] * pick(ahead, tile)).astype(BF16)
                    inside = inside + pick(later, tile) * dot(across, earlier)
                y_ref[seq, rows, lanes] = inside + skip[:, lanes] * x[rows]


def gate_kernel(
    member,
    y_ref,
    z_ref,
    grad_ref,
    bc_ref,
    sum_ref,
    entering,
    along,
    gain,
    out_ref,
    grad_z_ref,
    grad_scan_ref,
    payload_0,
    payload_1,
    payload_2,
    payload_3,
    gain_grad_ref,
    scanned_ref,
    gated_ref,
    gate_ref,
    start_ref,
    spread,
    state_ref,
):
    step = pl.program_id(0)
    per_seq = pl.num_programs(0) // 2
    running = sum_ref[0]
    start = jnp.exp(running)
    read_along = running[:, HEADS : HEADS + 1]
    readout = bc_ref[0, :, STATE:].astype(BF16)
    readout_t = bc_ref[0, :, STATE:].T.astype(BF16)
    squares = jnp.zeros((ROWS, TILE), F32)
    overlap = jnp.zeros((ROWS, TILE), F32)
    for tile in range(INNER // TILE):
        lanes = slice(TILE * tile, TILE * tile + TILE)
        if tile % 2 == 0:
            wide = dot(readout, entering[0, :, TILE * tile : TILE * tile + 2 * TILE])
        carried = wide[:, TILE * (tile % 2) : TILE * (tile % 2) + TILE]
        carried = carried + read_along * along[0, 0:1, lanes]
        begin = pick(start, tile)
        start_ref[:, lanes] = begin
        scanned = y_ref[0, :, lanes] + begin * carried
        scanned_ref[:, lanes] = scanned
        z = z_ref[0, :, lanes]
        gate = jax.nn.sigmoid(z)
        gate_ref[:, lanes] = gate
        gated = scanned * (z * gate)
        gated_ref[:, lanes] = gated
        squares = squares + gated * gated
        overlap = overlap + gated * (grad_ref[0, :, lanes] * gain[:, lanes])
    mean = jnp.sum(squares, axis=1, keepdims=True) / INNER
    inverse = lax.rsqrt(mean + EPSILON)
    back = jnp.sum(overlap, axis=1, keepdims=True) / INNER * inverse * inverse * inverse

    @pl.when(step == 0)
    def _():
        gain_grad_ref[...] = jnp.zeros_like(gain_grad_ref)

    @pl.when(step % per_seq == 0)
    def _():
        state_ref[...] = jnp.zeros_like(state_ref)

    for tile in range(INNER // TILE):
        lanes = slice(TILE * tile, TILE * tile + TILE)
        gated = gated_ref[:, lanes]
        grad = grad_ref[0, :, lanes]
        scaled = gated * inverse
        out_ref[0, :, lanes] = (scaled * gain[:, lanes]).astype(BF16)
        gain_grad_ref[:, lanes] += jnp.sum(grad * scaled, axis=0, keepdims=True)
        grad_gated = inverse * (grad * gain[:, lanes]) - gated * back
        z = z_ref[0, :, lanes]
        gate = gate_ref[:, lanes]
        grad_scan = grad_gated * (z * gate)
        grad_z_ref[0, :, lanes] = (
            grad_gated * scanned_ref[:, lanes] * (gate * (1.0 + z * (1.0 - gate)))
        ).astype(BF16)
        grad_scan_ref[0, :, lanes] = grad_scan
        spread[:, lanes] = (grad_scan * start_ref[:, lanes]).astype(BF16)
        if tile % 2:
            both = slice(TILE * tile - TILE, TILE * tile + TILE)
            state_ref[:, both] += dot(readout_t, spread[:, both])

    @pl.when(step % per_seq == per_seq - 1)
    def _():
        seq = step // per_seq
        whole = start[ROWS - 1 : ROWS]
        zero = jnp.zeros((1, TILE), F32)
        for tile in range(INNER // TILE):
            lanes = slice(TILE * tile, TILE * tile + TILE)
            place = slice(TILE * (tile % Q_TILES), TILE * (tile % Q_TILES) + TILE)
            slot = member[0] ^ (tile // Q_TILES)
            state = state_ref[:, lanes].astype(BF16)
            edge = edge_rows(pick(whole, tile), zero)
            for by, payload_ref in enumerate((payload_0, payload_1, payload_2, payload_3)):

                @pl.when(slot == by)
                def _(payload_ref=payload_ref, state=state, edge=edge, place=place):
                    payload_ref[seq, :STATE, place] = state
                    payload_ref[seq, STATE:, place] = edge


def intra_back_kernel(
    x_ref,
    grad_ref,
    y_ref,
    conv_input,
    weight,
    bias,
    step_q,
    sum_q,
    sum_t,
    scores_t,
    bc_ref,
    entering,
    along,
    skip,
    direction,
    *refs,
):
    known_ref, slope_ref, grad_scores_ref, heads_ref, grad_read_ref, product, spread = refs[-7:]
    row = lax.broadcasted_iota(jnp.int32, (SUB, SUB), 0)
    col = lax.broadcasted_iota(jnp.int32, (SUB, SUB), 1)
    causal = row <= col
    low = low_lanes()

    @pl.when(pl.program_id(0) == 0)
    def _():
        grad_scores_ref[...] = jnp.zeros_like(grad_scores_ref)
        grad_read_ref[...] = jnp.zeros_like(grad_read_ref)

    for seq in range(2):
        step, running = step_q[0, seq], sum_q[0, seq]
        middle = running[SUB - 1 : SUB]
        start = jnp.exp(running)
        read_along = running[:, Q_HEADS : Q_HEADS + 1]
        ahead = jnp.exp(middle - running[:SUB])
        later = jnp.exp(running[SUB:] - middle)
        across = scores_t[seq, :SUB, SUB:].astype(BF16)
        readout = bc_ref[seq, :, STATE:].astype(BF16)
        inner = [jnp.zeros((SUB, SUB), F32) for _ in range(2)]
        outer = jnp.zeros((SUB, SUB), F32)
        meeting = jnp.zeros((256, TILE), F32)
        product[2] = dot(readout, entering[seq])
        for tile in range(Q_TILES):
            lanes = slice(TILE * tile, TILE * tile + TILE)
            x = x_ref[seq, :, lanes]
            size = pick(step, tile)
            scaled = x * size
            grad = grad_ref[seq, :, lanes]
            begin = pick(start, tile)
            low_grad = jnp.where(low, grad, 0.0).astype(BF16)
            high_grad = jnp.where(low, 0.0, grad).astype(BF16)
            rounded = grad.astype(BF16)
            line = along[seq, 0:1, lanes]
            carried = product[2, :, lanes] + read_along * line
            through = skip[:, lanes] * x
            product[2, :, lanes] = rounded.astype(F32) * (
                y_ref[seq, :, lanes] + begin * carried - through
            )
            widened = grad * begin
            meeting = meeting + widened * line
            spread[:, lanes] = widened.astype(BF16)
            mixture = mixture_of(conv_input, seq, lanes, weight[:, lanes], bias[:, lanes])
            slope = silu_slope(mixture)
            slope_ref[seq, :, lanes] = slope.astype(BF16)
            sides = (
                jnp.where(low, scaled, 0.0).astype(BF16),
                jnp.where(low, 0.0, scaled).astype(BF16),
            )
            for part in range(2):
                rows = slice(SUB * part, SUB * part + SUB)
                weights = []
                pairs = dot_last(
                    jnp.concatenate([sides[0][rows], sides[1][rows]], 0), rounded[rows]
                )
                for side in range(2):
                    h = 2 * tile + side
                    apart = sum_t[0, seq, h : h + 1, rows] - running[rows, h : h + 1]
                    decayed = jnp.exp(jnp.where(causal, apart, FAR))
                    weights.append((decayed * scores_t[seq, rows, rows]).astype(BF16))
                    inner[part] = inner[part] + decayed * pairs[SUB * side : SUB * side + SUB]
                inside = dot(
                    jnp.concatenate(weights, 1),
                    jnp.concatenate([low_grad[rows], high_grad[rows]], 0),
                )
                if not part:
                    beyond = (rounded[SUB:].astype(F32) * pick(later, tile)).astype(BF16)
                    factor = pick(ahead, tile)
                    inside = inside + factor * dot(across, beyond)
                    outer = outer + dot_last((scaled[:SUB] * factor).astype(BF16), beyond)
                product[0, rows, lanes] = scaled[rows].astype(BF16).astype(F32) * inside
                product[1, rows, lanes] = x[rows] * inside
                known_ref[seq, rows, lanes] = (
                    size[rows] * inside + skip[:, lanes] * grad[rows]
                ) * slope[rows]
        grad_scores_ref[seq, :SUB, :SUB] += inner[0]
        grad_scores_ref[seq, SUB:, SUB:] += inner[1]
        grad_scores_ref[seq, :SUB, SUB:] += outer
        total = jnp.zeros((256, TILE), F32)
        for kind in range(3):
            total = total + head_sums(product[kind], head_columns(Q_LANES, TILE, Q_HEADS * kind))
        heads_ref[0, seq] = total
        grad_read_ref[seq] += (
            dot_last(spread[...], entering[seq])
            + jnp.sum(meeting, axis=1, keepdims=True) * direction[...]
        )


def channel_kernel(
    known_ref,
    slope_ref,
    x_ref,
    weight,
    step_q,
    sum_q,
    bc_ref,
    leaving,
    entering,
    along,
    column,
    grad_conv_ref,
    tail_ref,
    halo_ref,
    grad_mix_ref,
    heads_ref,
    grad_writes_ref,
    meeting_ref,
    padded,
    product,
    spread,
):
    zeros = jnp.zeros((EDGE, TILE), F32)
    padded[:EDGE] = zeros
    padded[EDGE + 256 :] = zeros
    meeting_ref[...] = jnp.zeros_like(meeting_ref)

    @pl.when(pl.program_id(0) == 0)
    def _():
        grad_writes_ref[...] = jnp.zeros_like(grad_writes_ref)

    for seq in range(2):
        running = sum_q[0, seq]
        remain = jnp.exp(running[255:256] - running)
        scale = step_q[0, seq] * remain
        writes = bc_ref[seq, :, :STATE].astype(BF16)
        product[...] = dot(writes, leaving[seq])
        for tile in range(Q_TILES):
            lanes = slice(TILE * tile, TILE * tile + TILE)
            taps = weight[:, lanes]
            x = x_ref[seq, :, lanes]
            back = leaving[seq, :, lanes]
            shared = product[:, lanes]
            product[:, lanes] = x * shared
            factor = pick(scale, tile)
            spread[:, lanes] = (x * factor).astype(BF16)
            slope = slope_ref[seq, :, lanes].astype(F32)
            grad_mix = known_ref[seq, :, lanes] + factor * slope * shared
            grad_mix_ref[seq, :, lanes] = grad_mix.astype(BF16)
            padded[EDGE : EDGE + 256] = grad_mix
            grad_conv = taps[0:1] * padded[3 : 3 + EDGE + 256]
            for tap in range(1, CONV):
                grad_conv = (
                    grad_conv + taps[tap : tap + 1] * padded[3 - tap : 3 - tap + EDGE + 256]
                )
            halo_ref[seq, :, lanes] = grad_conv[:EDGE].astype(BF16)
            grad_conv_ref[seq, :, lanes] = grad_conv[EDGE:].astype(BF16)
            tail_ref[seq, :, lanes] = grad_conv[256:]
            state = entering[seq, :, lanes].astype(F32) + column[...] * along[seq, 0:1, lanes]
            meeting_ref[seq : seq + 1, lanes] = jnp.sum(
                state * back.astype(F32), axis=0, keepdims=True
            )
        total = dot(product[...].astype(BF16), head_columns(Q_LANES, TILE, 0))
        heads_ref[0, seq] = jnp.zeros((256, TILE), F32)
        heads_ref[0, seq, :, :SIDE] = total[:, :SIDE] * remain
        grad_writes_ref[seq] += dot_last(spread[...], leaving[seq])


def sums_kernel(conv_input, grad_mix_ref, grad_ref, x_ref, sums_ref):
    sums_ref[...] = jnp.zeros_like(sums_ref)
    for seq in range(2):
        for tile in range(Q_TILES):
            lanes = slice(TILE * tile, TILE * tile + TILE)
            grad_mix = grad_mix_ref[seq, :, lanes].astype(F32)
            for tap in range(CONV):
                begin = EDGE - CONV + 1 + tap
                sums_ref[tap : tap + 1, lanes] += jnp.sum(
                    grad_mix * conv_input[seq, begin : begin + 256, lanes], axis=0, keepdims=True
                )
            sums_ref[4:5, lanes] += jnp.sum(grad_mix, axis=0, keepdims=True)
            sums_ref[5:6, lanes] += jnp.sum(
                grad_ref[seq, :, lanes] * x_ref[seq, :, lanes], axis=0, keepdims=True
            )


def last_kernel(
    conv_input,
    weight,
    bias,
    small,
    bc_ref,
    grad_scores_0,
    grad_scores_1,
    grad_writes,
    grad_read_0,
    grad_read_1,
    known_heads,
    heads,
    meeting,
    step_ref,
    sum_ref,
    grad_conv_ref,
    tail_ref,
    halo_ref,
    sums_ref,
    small_ref,
    padded,
):
    row = lax.broadcasted_iota(jnp.int32, (256, 256), 0)
    col = lax.broadcasted_iota(jnp.int32, (256, 256), 1)
    upper = (row <= col).astype(F32)
    lane = lax.broadcasted_iota(jnp.int32, (1, TILE), 1)
    line = lax.broadcasted_iota(jnp.int32, (256, 1), 0)
    padded[:EDGE] = jnp.zeros((EDGE, 256), F32)
    padded[EDGE + 256 :] = jnp.zeros((EDGE, 256), F32)
    sums_ref[...] = jnp.zeros_like(sums_ref)
    small_ref[...] = jnp.zeros_like(small_ref)
    rate = jnp.exp(small[1:2])
    met_states = head_sums(meeting[...], head_columns(INNER, TILE, 0))
    taps = weight[...]

    def gather(source, seq, kind):
        total = jnp.zeros((256, TILE), F32)
        for quarter in range(QUARTERS):
            value = source[quarter, seq]
            shift = (Q_HEADS * (quarter - kind)) % TILE
            if shift:
                value = pltpu.roll(value, shift, 1)
            first = Q_HEADS * quarter
            total = total + jnp.where((lane >= first) & (lane < first + Q_HEADS), value, 0.0)
        return total

    for seq in range(2):
        step = step_ref[seq]
        by_state = gather(heads, seq, 0)
        at_state = step * by_state
        running = sum_ref[seq]
        last = jnp.where(lane < HEADS, running[255:256], 0.0)
        end = jnp.exp(last) * met_states[seq : seq + 1] + jnp.sum(
            at_state, axis=0, keepdims=True
        )
        grad_sum = (
            gather(known_heads, seq, 2)
            - gather(known_heads, seq, 0)
            - at_state
            + jnp.where(line == 255, end, 0.0)
        )
        grad_log = jnp.dot(upper, grad_sum, preferred_element_type=F32, precision=HIGHEST)
        small_ref[1:2] += jnp.sum(-rate * step * grad_log, axis=0, keepdims=True)
        raw = conv_input[seq, EDGE : EDGE + 256, 256:384] + small[0:1]
        raw = jnp.where(lane < HEADS, raw, 0.0)
        grad_step = gather(known_heads, seq, 1) + by_state - rate * grad_log
        grad_raw = grad_step * jax.nn.sigmoid(raw)
        small_ref[0:1] += jnp.sum(grad_raw, axis=0, keepdims=True)
        grad_conv_ref[seq, :, 256:] = grad_raw[:, :HEADS].astype(BF16)
        writes, readout = bc_ref[seq, :, :STATE], bc_ref[seq, :, STATE:]
        grad_scores = grad_scores_0[seq] + grad_scores_1[seq]
        into_writes = (
            jnp.dot(grad_scores, readout, preferred_element_type=F32, precision=HIGHEST)
            + grad_writes[seq]
        )
        into_read = dot_first(grad_scores, writes, HIGHEST) + grad_read_0[seq] + grad_read_1[seq]
        mixture = mixture_of(conv_input, seq, slice(0, 256), taps, bias[...])
        grad_mix = jnp.concatenate([into_writes, into_read], 1) * silu_slope(mixture)
        padded[EDGE : EDGE + 256] = grad_mix
        grad_conv = taps[0:1] * padded[3 : 3 + EDGE + 256]
        for tap in range(1, CONV):
            grad_conv = grad_conv + taps[tap : tap + 1] * padded[3 - tap : 3 - tap + EDGE + 256]
        halo_ref[seq] = grad_conv[:EDGE].astype(BF16)
        grad_conv_ref[seq, :, :256] = grad_conv[EDGE:].astype(BF16)
        tail_ref[seq] = grad_conv[256:]
        for tap in range(CONV):
            begin = EDGE - CONV + 1 + tap
            sums_ref[tap : tap + 1] += jnp.sum(
                grad_mix * conv_input[seq, begin : begin + 256, :256], axis=0, keepdims=True
            )
        sums_ref[4:5] += jnp.sum(grad_mix, axis=0, keepdims=True)


def shape(dims, dtype=F32):
    return jax.ShapeDtypeStruct(dims, dtype)


def whole_block(dims):
    return pl.BlockSpec(dims, lambda *g: (0,) * len(dims))


def lane_block(dims, width=Q_LANES):
    return pl.BlockSpec(dims + (width,), lambda g: (0,) * len(dims) + (g,))


def quarter_block(dims):
    return pl.BlockSpec((1,) + dims, lambda g, *_: (g,) + (0,) * len(dims))


def own_lanes(dims):
    return pl.BlockSpec(
        dims + (Q_LANES,), lambda g, member: (0,) * len(dims) + (g ^ member[0],)
    )


def own_quarter(dims):
    return pl.BlockSpec((1,) + dims, lambda g, member: (g ^ member[0],) + (0,) * len(dims))


def fixed_block(dims, index):
    return pl.BlockSpec(dims, lambda g: index)


def row_block(width, length=256):
    steps = length // ROWS
    return pl.BlockSpec((1, ROWS, width), lambda g: (g // steps, g % steps, 0))


SCALAR = pl.BlockSpec(memory_space=pltpu.SMEM)
MESSAGE = (2, PAYLOAD, Q_LANES)


def tie(value, *others):
    return lax.optimization_barrier((value,) + others)[0]


def exchange(payload, member, axis, reverse, stages):
    count = lax.axis_size(axis)
    stages = iter(stages)

    def swap(value, by):
        return lax.ppermute(value, axis, [(i, i ^ by) for i in range(count)])

    def meanwhile(sent, arrived):
        work = next(stages, None)
        return tie(arrived, *work(sent)) if work else arrived

    message = shape(MESSAGE, BF16)
    block = whole_block(MESSAGE)
    members = [payload[0]] + [swap(payload[by], by) for by in range(1, QUARTERS)]
    members[-1] = meanwhile(payload[-1], members[-1])
    total = pl.pallas_call(
        functools.partial(plane_kernel, reverse),
        grid=(1,),
        in_specs=[SCALAR] + [block] * QUARTERS,
        out_specs=block,
        out_shape=message,
        compiler_params=params(14),
        cost_estimate=cost(2),
        name="plane",
    )(member, *members)
    received = []
    inclusive = total
    span = 1
    while span < count // QUARTERS:
        shift = -QUARTERS * span if reverse else QUARTERS * span
        pairs = [(i, i + shift) for i in range(count) if 0 <= i + shift < count]
        arrived = lax.ppermute(inclusive, axis, pairs)
        received.append(meanwhile(inclusive, arrived) if span < 4 else arrived)
        span *= 2
        if span < count // QUARTERS:
            inclusive = pl.pallas_call(
                link_kernel,
                grid=(1,),
                in_specs=[block] * (1 + len(received)),
                out_specs=block,
                out_shape=message,
                compiler_params=params(14),
                cost_estimate=cost(1.5),
                name="link",
            )(total, *received)
    results = pl.pallas_call(
        functools.partial(spread_kernel, reverse),
        grid=(1,),
        in_specs=[SCALAR] + [block] * (QUARTERS + len(received)),
        out_specs=[block] * QUARTERS,
        out_shape=[message] * QUARTERS,
        compiler_params=params(16),
        cost_estimate=cost(3),
        name="spread",
    )(member, *members, *received)
    back = [results[0]] + [swap(results[by], by) for by in range(1, QUARTERS)]
    back[-1] = meanwhile(results[-1], back[-1])
    return pl.pallas_call(
        arrange_kernel,
        grid_spec=pltpu.PrefetchScalarGridSpec(
            num_scalar_prefetch=1,
            grid=(QUARTERS,),
            in_specs=[block] * QUARTERS,
            out_specs=[own_lanes((2, STATE)), own_lanes((2, 8))],
        ),
        out_shape=[shape((2, STATE, INNER), BF16), shape((2, 8, INNER))],
        compiler_params=params(14),
        cost_estimate=cost(1.5),
        name="arrange",
    )(member, *back)


class Scatter:
    def __init__(self, arrays, axis):
        self.axis = axis
        self.count = lax.axis_size(axis)
        self.place = lax.axis_index(axis)
        self.bits = list(range(self.count.bit_length() - 1))[::-1]
        self.values = [
            a.reshape((2,) * len(self.bits) + (a.shape[0] // self.count, a.shape[1]))
            for a in arrays
        ]

    def wait_for(self, *others):
        self.values = list(lax.optimization_barrier(tuple(self.values) + others))[
            : len(self.values)
        ]

    def send(self, bit, *others):
        position = self.bits.index(bit)
        mine = (self.place >> bit) & 1
        away = [lax.dynamic_index_in_dim(v, 1 - mine, position, False) for v in self.values]
        away = jnp.concatenate([v.astype(BF16) for v in away], axis=-2)
        self.values = [lax.dynamic_index_in_dim(v, mine, position, False) for v in self.values]
        self.bits.remove(bit)
        self.away = away
        if others:
            away = tie(away, *others)
        self.sent = lax.ppermute(
            away, self.axis, [(i, i ^ (1 << bit)) for i in range(self.count)]
        )

    def add(self):
        begin = 0
        for i, value in enumerate(self.values):
            end = begin + value.shape[-2]
            self.values[i] = value + self.sent[..., begin:end, :].astype(F32)
            begin = end


def add_up(value, axes):
    for axis in axes:
        count = lax.axis_size(axis)
        for bit in range(count.bit_length() - 1):
            value = value + lax.ppermute(value, axis, [(i, i ^ (1 << bit)) for i in range(count)])
    return value


def finish_kernel(gate_rows, last_rows, out_rows, in_grad, out_grad):
    step = pl.program_id(0)
    length, columns = gate_rows.shape[0] * gate_rows.shape[1], gate_rows.shape[2]

    @pl.when(step < 2 * INNER // length)
    def _():
        in_grad[...] = gate_rows[...].reshape(length, columns).astype(F32)

    @pl.when(step == 2 * INNER // length)
    def _():
        rows = last_rows.shape[0] * last_rows.shape[1]
        keep = min(rows, in_grad.shape[0])
        in_grad[:keep] = last_rows[...].reshape(rows, columns)[:keep].astype(F32)

    @pl.when(step < INNER // length)
    def _():
        group, per = out_rows.shape[0], out_rows.shape[1] // 2
        for side in range(2):
            out_grad[:, columns * side : columns * side + columns] = (
                out_rows[:, per * side : per * side + per].reshape(group * per, columns).astype(F32)
            )


def local(
    hidden_in,
    norm_gain,
    in_weight,
    conv_weight,
    conv_bias,
    step_bias,
    decay_log,
    skip_gain,
    gate_gain,
    out_weight,
    cotangent,
):
    hidden = hidden_in[0]
    upstream = cotangent[0]
    tokens, width = hidden.shape
    half = tokens // 2
    share = in_weight.shape[0]
    count = lax.axis_size("seq")
    core = lax.axis_index("fsdp")
    other = [(0, 1), (1, 0)]

    rows_of = in_weight.T
    conv_rows = lax.optimization_barrier(rows_of[INNER:])
    conv_rows_other = lax.ppermute(conv_rows, "fsdp", other)

    paired = hidden.reshape(2, half, width)
    halo = lax.ppermute(
        tie(paired[:, half - EDGE :], conv_rows), "seq", [(i, i + 1) for i in range(count - 1)]
    )
    extended = jnp.concatenate([halo, paired], axis=1).reshape(2 * (half + EDGE), width)
    rows = extended.astype(F32)
    rescale = lax.rsqrt(jnp.mean(rows * rows, axis=-1, keepdims=True) + EPSILON)
    normed_ext = (rows * rescale * norm_gain).astype(BF16)

    member = (lax.axis_index("seq") % QUARTERS).astype(jnp.int32).reshape(1)

    def mine(array, axis):
        first = lax.slice_in_dim(array, 0, share, axis=axis)
        second = lax.slice_in_dim(array, share, 2 * share, axis=axis)
        return (
            jnp.where(core == 0, first, second),
            jnp.where(core == 0, second, first),
        )

    def ordered(own, foreign, axis):
        return jnp.where(
            core == 0,
            jnp.concatenate([own, foreign], axis),
            jnp.concatenate([foreign, own], axis),
        )

    own_ext, other_ext = mine(normed_ext, 1)
    normed = normed_ext.reshape(2, half + EDGE, width)[:, EDGE:].reshape(tokens, width)

    small = jnp.pad(jnp.stack([step_bias, decay_log, skip_gain]), ((0, 5), (0, TILE - HEADS)))
    bias_row = conv_bias[None]
    gain_row = gate_gain[None]
    skip_row = jnp.repeat(skip_gain, HEAD_DIM)[None]

    own_ext = tie(own_ext, small, bias_row, skip_row)
    conv_input = (dot_last(own_ext, conv_rows) + dot_last(other_ext, conv_rows_other)).reshape(
        2, half + EDGE, CONV_CH + HEADS
    )

    last_columns = fixed_block((2, half + EDGE, 384), (0, 0, INNER // 384))
    last_taps = fixed_block((CONV, 256), (0, INNER // 256))
    last_bias = fixed_block((1, 256), (0, INNER // 256))
    per_quarter = (QUARTERS, 2, half, SIDE)
    (
        bc,
        bt,
        scores,
        scores_t,
        step,
        running,
        step_q,
        sum_q,
        sum_t,
        row_direction,
        column_direction,
    ) = pl.pallas_call(
        step_kernel,
        grid=(1,),
        in_specs=[
            last_columns,
            last_taps,
            last_bias,
            whole_block((8, TILE)),
            fixed_block((STATE, share), (2 * INNER // STATE, 0)),
        ],
        out_specs=[
            whole_block((2, half, 256)),
            whole_block((2, STATE, half)),
            whole_block((2, half, half)),
            whole_block((2, half, half)),
            whole_block((2, half, TILE)),
            whole_block((2, half, TILE)),
            whole_block(per_quarter),
            whole_block(per_quarter),
            whole_block((QUARTERS, 2, EDGE, half)),
            whole_block((1, STATE)),
            whole_block((STATE, 1)),
        ],
        out_shape=[
            shape((2, half, 256)),
            shape((2, STATE, half), BF16),
            shape((2, half, half)),
            shape((2, half, half)),
            shape((2, half, TILE)),
            shape((2, half, TILE)),
            shape(per_quarter),
            shape(per_quarter),
            shape((QUARTERS, 2, EDGE, half)),
            shape((1, STATE)),
            shape((STATE, 1)),
        ],
        compiler_params=params(20),
        cost_estimate=cost(4),
        name="steps",
    )(conv_input, conv_weight, bias_row, small, rows_of)

    columns = lane_block((2, half + EDGE))
    taps_block = lane_block((CONV,))
    row_of = lane_block((1,))
    heads_block = quarter_block((2, half, SIDE))
    line_block = quarter_block((2, EDGE, half))
    tokens_block = lane_block((2, half))
    x, *payload = pl.pallas_call(
        state_kernel,
        grid_spec=pltpu.PrefetchScalarGridSpec(
            num_scalar_prefetch=1,
            grid=(QUARTERS,),
            in_specs=[
                own_lanes((2, half + EDGE)),
                own_lanes((CONV,)),
                own_lanes((1,)),
                own_quarter((2, half, SIDE)),
                own_quarter((2, half, SIDE)),
                whole_block((2, STATE, half)),
                whole_block((STATE, 1)),
            ],
            out_specs=[own_lanes((2, half))] + [whole_block(MESSAGE)] * QUARTERS,
        ),
        out_shape=[shape((2, half, INNER))] + [shape(MESSAGE, BF16)] * QUARTERS,
        compiler_params=params(60),
        cost_estimate=cost(8),
        name="states",
    )(member, conv_input, conv_weight, bias_row, step_q, sum_q, bt, column_direction)

    gate_rows = rows_of[:INNER]
    out_rows = lax.all_gather(tie(out_weight, *payload), "fsdp", axis=0, tiled=True)
    half_grid = QUARTERS // 2

    def later_half(spec, first):
        old = spec.index_map
        return pl.BlockSpec(spec.block_shape, lambda g: old(g + first))

    def shifted(specs, first):
        return [later_half(spec, first) for spec in specs]

    kept = {}

    def while_states_cross(sent):
        kept["rows"] = lax.ppermute(tie(rows_of, sent), "fsdp", other)[:INNER]
        kept["normed"] = mine(tie(normed, sent), 1)
        kept["gate"] = dot_last(kept["normed"][0], gate_rows)
        return inside(0)(sent) + (kept["gate"],)

    def while_first_states(sent):
        kept["grad"] = dot_last(tie(upstream, sent), out_rows).reshape(2, half, INNER)
        return (kept["grad"],)

    def inside(first):
        def work(sent):
            specs = [
                tokens_block,
                heads_block,
                heads_block,
                line_block,
                whole_block((2, half, half)),
                row_of,
            ]
            inputs = [tie(x, sent), step_q, sum_q, sum_t, scores, skip_row]
            kept["inside"] = pl.pallas_call(
                intra_kernel,
                grid=(half_grid,),
                in_specs=shifted(specs, first)
                + [pl.BlockSpec(memory_space=pl.ANY)] * (first > 0),
                out_specs=later_half(tokens_block, first),
                out_shape=shape((2, half, INNER)),
                input_output_aliases={len(specs): 0} if first else {},
                compiler_params=params(60),
                cost_estimate=cost(8),
                name="inside",
            )(*inputs, *([kept["inside"]] if first else []))
            return (kept["inside"],)

        return work

    def while_states_return(sent):
        kept["z"] = (
            kept["gate"] + dot_last(tie(kept["normed"][1], sent), kept["rows"])
        ).reshape(2, half, INNER)
        return (kept["z"],)

    entering, along = exchange(
        payload,
        member,
        "seq",
        False,
        [while_states_cross, while_first_states, inside(half_grid), while_states_return],
    )
    gate_rows_other = kept["rows"]
    own_normed, other_normed = kept["normed"]
    y_inside, z, grad_normed_out = kept["inside"], kept["z"], kept["grad"]

    token_rows = row_block(INNER)
    steps = half // ROWS
    normed_out, grad_z, grad_scan, *back_payload, gate_gain_grad = pl.pallas_call(
        gate_kernel,
        grid=(2 * steps,),
        in_specs=[
            SCALAR,
            token_rows,
            token_rows,
            token_rows,
            row_block(256),
            row_block(TILE),
            pl.BlockSpec((1, STATE, INNER), lambda g: (g // steps, 0, 0)),
            pl.BlockSpec((1, 8, INNER), lambda g: (g // steps, 0, 0)),
            whole_block((1, INNER)),
        ],
        out_specs=[
            token_rows,
            token_rows,
            token_rows,
            *[whole_block(MESSAGE)] * QUARTERS,
            whole_block((1, INNER)),
        ],
        out_shape=[
            shape((2, half, INNER), BF16),
            shape((2, half, INNER), BF16),
            shape((2, half, INNER)),
            *[shape(MESSAGE, BF16)] * QUARTERS,
            shape((1, INNER)),
        ],
        scratch_shapes=[
            pltpu.VMEM((ROWS, INNER), F32),
            pltpu.VMEM((ROWS, INNER), F32),
            pltpu.VMEM((ROWS, INNER), F32),
            pltpu.VMEM((ROWS, INNER), F32),
            pltpu.VMEM((ROWS, INNER), BF16),
            pltpu.VMEM((STATE, INNER), F32),
        ],
        compiler_params=params(38),
        cost_estimate=cost(14),
        name="gates",
    )(
        member,
        y_inside,
        z,
        grad_normed_out,
        bc,
        running,
        entering,
        along,
        gain_row,
    )

    normed_out = normed_out.reshape(tokens, INNER)
    grad_z = grad_z.reshape(tokens, INNER)
    first_out, second_out = normed_out[:, : INNER // 2], normed_out[:, INNER // 2 :]
    own_out = jnp.where(core == 0, first_out, second_out)
    other_out = jnp.where(core == 0, second_out, first_out)

    def weight_part(own, foreign):
        sent = lax.ppermute(dot_first(*foreign).astype(BF16), "fsdp", other)
        return dot_first(*own) + sent.astype(F32)

    def while_gradients_cross(sent):
        out_part = weight_part((own_out, upstream), (other_out, upstream))
        gate_part = weight_part((grad_z, own_normed), (grad_z, other_normed))
        kept["out"] = Scatter([out_part], "seq")
        kept["gates"] = Scatter([gate_part], "seq")
        return out_part, gate_part

    state_columns = lane_block((2, STATE))
    line_columns = lane_block((2, 8))
    edge_columns = lane_block((2, EDGE))
    back_parts = []

    def inside_back(first):
        def work(sent):
            if not first:
                for part, bit in ((kept["out"], 0), (kept["gates"], 1)):
                    part.send(bit, sent)
            specs = [
                tokens_block,
                tokens_block,
                tokens_block,
                columns,
                taps_block,
                row_of,
                heads_block,
                heads_block,
                line_block,
                whole_block((2, half, half)),
                whole_block((2, half, 256)),
                state_columns,
                line_columns,
                row_of,
                whole_block((1, STATE)),
            ]
            inputs = [
                x,
                tie(grad_scan, sent),
                y_inside,
                conv_input,
                conv_weight,
                bias_row,
                step_q,
                sum_q,
                sum_t,
                scores_t,
                bc,
                entering,
                along,
                skip_row,
                row_direction,
            ]
            earlier = [back_parts[0][i] for i in (0, 1, 3)] if first else []
            back_parts.append(
                pl.pallas_call(
                    intra_back_kernel,
                    grid=(half_grid,),
                    in_specs=shifted(specs, first)
                    + [pl.BlockSpec(memory_space=pl.ANY)] * len(earlier),
                    out_specs=shifted(
                        [
                            tokens_block,
                            tokens_block,
                            whole_block((2, half, half)),
                            quarter_block((2, half, TILE)),
                            whole_block((2, half, STATE)),
                        ],
                        first,
                    ),
                    out_shape=[
                        shape((2, half, INNER)),
                        shape((2, half, INNER), BF16),
                        shape((2, half, half)),
                        shape((QUARTERS, 2, half, TILE)),
                        shape((2, half, STATE)),
                    ],
                    scratch_shapes=[
                        pltpu.VMEM((3, half, Q_LANES), F32),
                        pltpu.VMEM((half, Q_LANES), BF16),
                    ],
                    input_output_aliases={
                        len(specs) + i: (0, 1, 3)[i] for i in range(len(earlier))
                    },
                    compiler_params=params(60),
                    cost_estimate=cost(17),
                    name="inside_back",
                )(*inputs, *earlier)
            )
            return tuple(back_parts[-1])

        return work

    def while_gradients_return(sent):
        for part in (kept["out"], kept["gates"]):
            part.sent = tie(part.sent, sent)
            part.add()
        return kept["out"].values[0], kept["gates"].values[0]

    leaving, _ = exchange(
        back_payload,
        member,
        "seq",
        True,
        [while_gradients_cross, inside_back(0), inside_back(half_grid), while_gradients_return],
    )
    out_part, gate_part = kept["out"], kept["gates"]
    for part, bit in ((out_part, 1), (gate_part, 0)):
        part.wait_for(leaving)
        part.send(bit)
    leaving = tie(leaving, out_part.away, gate_part.away)
    known, slope, _, known_heads, _ = back_parts[1]
    grad_conv, tail, halo_grad, grad_mix, heads, grad_writes, meeting = pl.pallas_call(
        channel_kernel,
        grid=(QUARTERS,),
        in_specs=[
            tokens_block,
            tokens_block,
            tokens_block,
            taps_block,
            heads_block,
            heads_block,
            whole_block((2, half, 256)),
            state_columns,
            state_columns,
            line_columns,
            whole_block((STATE, 1)),
        ],
        out_specs=[
            tokens_block,
            edge_columns,
            edge_columns,
            tokens_block,
            quarter_block((2, half, TILE)),
            whole_block((2, half, STATE)),
            lane_block((8,)),
        ],
        out_shape=[
            shape((2, half, INNER), BF16),
            shape((2, EDGE, INNER)),
            shape((2, EDGE, INNER), BF16),
            shape((2, half, INNER), BF16),
            shape((QUARTERS, 2, half, TILE)),
            shape((2, half, STATE)),
            shape((8, INNER)),
        ],
        scratch_shapes=[
            pltpu.VMEM((half + 2 * EDGE, TILE), F32),
            pltpu.VMEM((half, Q_LANES), F32),
            pltpu.VMEM((half, Q_LANES), BF16),
        ],
        compiler_params=params(60),
        cost_estimate=cost(12),
        name="channels",
    )(
        known,
        slope,
        x,
        conv_weight,
        step_q,
        sum_q,
        bc,
        leaving,
        entering,
        along,
        column_direction,
    )

    grad_conv_last, tail_last, halo_last, sums_last, small_grads = pl.pallas_call(
        last_kernel,
        grid=(1,),
        in_specs=[
            last_columns,
            last_taps,
            last_bias,
            whole_block((8, TILE)),
            whole_block((2, half, 256)),
            whole_block((2, half, half)),
            whole_block((2, half, half)),
            whole_block((2, half, STATE)),
            whole_block((2, half, STATE)),
            whole_block((2, half, STATE)),
            whole_block((QUARTERS, 2, half, TILE)),
            whole_block((QUARTERS, 2, half, TILE)),
            whole_block((8, INNER)),
            whole_block((2, half, TILE)),
            whole_block((2, half, TILE)),
        ],
        out_specs=[
            whole_block((2, half, 256 + HEADS)),
            whole_block((2, EDGE, 256)),
            whole_block((2, EDGE, 256)),
            whole_block((8, 256)),
            whole_block((8, TILE)),
        ],
        out_shape=[
            shape((2, half, 256 + HEADS), BF16),
            shape((2, EDGE, 256)),
            shape((2, EDGE, 256), BF16),
            shape((8, 256)),
            shape((8, TILE)),
        ],
        scratch_shapes=[pltpu.VMEM((half + 2 * EDGE, 256), F32)],
        compiler_params=params(60),
        cost_estimate=cost(6),
        name="last",
    )(
        conv_input,
        conv_weight,
        bias_row,
        small,
        bc,
        back_parts[0][2],
        back_parts[1][2],
        grad_writes,
        back_parts[0][4],
        back_parts[1][4],
        known_heads,
        heads,
        meeting,
        step,
        running,
    )

    returned = lax.ppermute(
        tie(jnp.concatenate([halo_grad, halo_last], axis=-1), out_part.sent, gate_part.sent),
        "seq",
        [(i, i - 1) for i in range(1, count)],
    )
    fixed_tail = (jnp.concatenate([tail, tail_last], axis=-1) + returned.astype(F32)).astype(BF16)
    body = half - EDGE
    grad_wide = jnp.concatenate([grad_conv[:, :body], fixed_tail[:, :, :INNER]], axis=1)
    grad_wide = grad_wide.reshape(tokens, INNER)
    per = INNER // count
    per_last = -(-(CONV_CH + HEADS - INNER) // (16 * count)) * 16
    spare = per_last * count - (CONV_CH + HEADS - INNER)
    grad_narrow = jnp.concatenate(
        [
            grad_conv_last[:, :body],
            jnp.concatenate([fixed_tail[:, :, INNER:], grad_conv_last[:, body:, 256:]], axis=-1),
        ],
        axis=1,
    ).reshape(tokens, CONV_CH + HEADS - INNER)
    grad_padded = jnp.pad(grad_narrow, ((0, 0), (0, spare)))

    for part in (out_part, gate_part):
        part.add()
    early = gate_part
    out_value = out_part.values[0]
    early.values.append(
        jnp.concatenate([out_value[..., :share], out_value[..., share:]], axis=-2)
    )
    bits = early.bits[::-1]
    early.send(bits[0])

    grad_wide, grad_padded = lax.optimization_barrier((grad_wide, grad_padded, early.away))[:2]
    wide_part = weight_part((grad_wide, own_normed), (grad_wide, other_normed))
    last_part = weight_part((grad_padded, own_normed), (grad_padded, other_normed))
    cut = share // 2
    first_part = Scatter([wide_part[:, :cut], last_part[:, :cut]], "seq")
    second_part = Scatter([wide_part[:, cut:], last_part[:, cut:]], "seq")
    first_part.send(0)
    second_part.send(1)
    early.add()
    for bit in bits[1:]:
        early.send(bit)
        early.add()
    for part, bit in ((first_part, 1), (second_part, 0)):
        part.add()
        part.send(bit)
    for part in (first_part, second_part):
        part.add()
    late = second_part
    late.values = [
        jnp.concatenate(pair, axis=-1) for pair in zip(first_part.values, second_part.values)
    ]
    late.wait_for(*early.values)
    for bit in bits:
        late.send(bit)
        late.add()

    gate_value, out_value = early.values
    shard = jnp.concatenate([gate_value, out_value] + late.values, axis=-2).astype(BF16)
    gathered = lax.all_gather(shard, "seq", axis=0)

    grad_z, grad_wide, grad_narrow, normed_out, grad_mix = lax.optimization_barrier(
        (grad_z, grad_wide, grad_narrow, normed_out, grad_mix, shard)
    )[:5]

    def through_rows(first, second):
        return (
            dot(grad_z, first) + dot(grad_wide, second[:INNER]) + dot(grad_narrow, second[INNER:])
        )

    grad_normed = ordered(
        through_rows(gate_rows, conv_rows), through_rows(gate_rows_other, conv_rows_other), 1
    )
    u = hidden.astype(F32)
    r = lax.rsqrt(jnp.mean(u * u, axis=-1, keepdims=True) + EPSILON)
    norm_gain_grad = jnp.sum(grad_normed * u * r, axis=0)
    through = grad_normed * norm_gain
    input_grad = (
        upstream.astype(F32)
        + r * through
        - u * (r * r * r) * jnp.mean(through * u, axis=-1, keepdims=True)
    ).astype(BF16)
    block_out = (hidden.astype(F32) + dot(normed_out, out_rows)).astype(BF16)

    sums = pl.pallas_call(
        sums_kernel,
        grid=(QUARTERS,),
        in_specs=[columns, tokens_block, tokens_block, tokens_block],
        out_specs=lane_block((8,)),
        out_shape=shape((8, INNER)),
        compiler_params=params(60),
        cost_estimate=cost(10),
        name="sums",
    )(conv_input, grad_mix, grad_scan, x)

    skip_grad = jnp.sum(sums[5].reshape(HEADS, HEAD_DIM), axis=1)
    vector = jnp.concatenate(
        [
            norm_gain_grad,
            sums[:5].reshape(-1),
            sums_last[:5].reshape(-1),
            small_grads[:2].reshape(-1),
            gate_gain_grad[0],
            jnp.pad(skip_grad, (0, TILE - HEADS)),
        ]
    )
    length = vector.shape[0]
    vector = add_up(vector.reshape(length // TILE, TILE), ("fsdp", "seq")).reshape(length)
    parts = []
    begin = 0
    for size in (width, 5 * INNER, 5 * 256, 2 * TILE, INNER, HEADS):
        parts.append(vector[begin : begin + size])
        begin += size
    conv_sums = jnp.concatenate(
        [parts[1].reshape(5, INNER), parts[2].reshape(5, 256)], axis=1
    )
    smalls = parts[3].reshape(2, TILE)[:, :HEADS]

    group = share // per
    parts_of = INNER // share
    gathered_block = (group, per, share)
    in_grad, out_grad = pl.pallas_call(
        finish_kernel,
        grid=(2 * parts_of + 1,),
        in_specs=[
            pl.BlockSpec(
                gathered_block,
                lambda g: (jnp.minimum(g, 2 * parts_of - 1) % parts_of, g // parts_of * 2 % 4, 0),
            ),
            pl.BlockSpec((count, per_last, share), lambda g: (0, 3 * per // per_last, 0)),
            pl.BlockSpec(gathered_block, lambda g: (jnp.minimum(g, parts_of - 1), 1, 0)),
        ],
        out_specs=[
            pl.BlockSpec((share, share), lambda g: (g, 0)),
            pl.BlockSpec((share // 2, width), lambda g: (jnp.minimum(g, parts_of - 1), 0)),
        ],
        out_shape=[shape((CONV_CH + HEADS + INNER, share)), shape((2 * share, width))],
        compiler_params=params(60),
        cost_estimate=cost(14),
        name="finish",
    )(gathered, gathered, gathered)
    return (
        block_out[None],
        input_grad[None],
        parts[0],
        in_grad.T,
        conv_sums[:4],
        conv_sums[4],
        smalls[0],
        smalls[1],
        parts[5],
        parts[4],
        out_grad,
    )


def solution(mesh):
    return jax.shard_map(
        local,
        mesh=mesh,
        in_specs=(
            P("fsdp", "seq", None),
            P(),
            P("fsdp", None),
            P(),
            P(),
            P(),
            P(),
            P(),
            P(),
            P("fsdp", None),
            P("fsdp", "seq", None),
        ),
        out_specs=(
            P("fsdp", "seq", None),
            P("fsdp", "seq", None),
            P(),
            P("fsdp", None),
            P(),
            P(),
            P(),
            P(),
            P(),
            P(),
            P("fsdp", None),
        ),
        check_vma=False,
    )
```
